128 devices in a mesh: gx: 32 (over y, z, core), gy: 4 (over x).
Axes of the slice: x: 4, y: 4, z: 4, core: 2. Of those that a mesh axis runs over, the one named last changes fastest.
Arguments:
- ice_state: float32 [128, 5, 32, 1024], P(('gx', 'gy')), may hold values from -4 to 4
- thickness: float32 [128, 5, 32, 1024], P(('gx', 'gy')), may hold values from 0.3 to 3
- concentration: float32 [128, 5, 32, 1024], P(('gx', 'gy')), may hold values from 0.04 to 0.2
- cat_mask: int32 [128, 5, 32, 1024], P(('gx', 'gy')), may hold values 0 or 1
- forcing: float32 [16384, 4, 1024], P(('gx', 'gy')), may hold values from -4 to 4
- ice_target: int32 [16384], P(('gx', 'gy')), may hold values from -1 to 4095, as said below
Outputs:
- ice_out: float32 [128, 5, 32, 1024], P(('gx', 'gy'))
- ocean_stress: float32 [16384, 2, 1024], P(('gx', 'gy'))
The draws below stay inside these ranges and needn't reach their ends.
Inputs may be any that keep to these rules, and one draw needn't show every extreme that they name: `ice_target`: each ice index 0 to 4095 appears exactly once, all others are -1. The ocean blocks of one device carry at most 1 ice blocks of any one cap column, and some device carries exactly 1 of some column.
All inputs are finite; a program needn't handle non-finite values. No bound on the sum of `cat_mask` on one device may be relied on, other than what follows from the above.
Results may differ from the reference program's by a relative error of at most 0.00002.
Values sent between devices are 32-bit elements; how exact they have to be, the bound alone decides.
A program may use at most 128 MiB of HBM per device.

```python
import math
import jax
import jax.numpy as jnp
from jax import lax

BS = 32
CELLS = 1024
NCAT = 5
IY = 32
SUB = 8
OBLK_DEV = 128
IX = 128
L = 1024
OCEAN_BLOCK_COUNT = 16384
CAP = 1
N_GX = 32
N_GY = 4


def draw_ice_target(key, part):
    key = jax.random.fold_in(key, 11)
    devices = N_GX * N_GY
    seat_count = 2 * N_GX * CAP
    polar_rank = jnp.arange(2 * N_GX, dtype=jnp.int32)
    source_device = polar_rank // 2 * N_GY + polar_rank % 2 * (N_GY - 1)
    seat_ids = jnp.arange(seat_count, dtype=jnp.int32)

    def owner_pick(owner_key):
        first_key, row_key = jax.random.split(owner_key)
        shuffle = jax.random.permutation(first_key, seat_count).astype(jnp.int32)
        position = jnp.argsort(shuffle).astype(jnp.int32)
        chosen_source = shuffle[0] // CAP
        priority = jnp.where(seat_ids // CAP == chosen_source, seat_ids % CAP - CAP, position)
        picked = jnp.argsort(priority)[:IY].astype(jnp.int32)
        row_order = jax.random.permutation(row_key, IY).astype(jnp.int32)
        return (source_device[picked // CAP], row_order)
    owner_keys = jax.random.split(jax.random.fold_in(key, 1), devices)
    senders, row_order = jax.vmap(owner_pick)(owner_keys)
    global_index = (jnp.arange(devices, dtype=jnp.int32)[:, None] * IY + row_order).reshape(-1)
    senders = senders.reshape(-1)
    by_sender = jnp.argsort(senders, stable=True)
    sorted_senders = senders[by_sender]
    first_of = jnp.searchsorted(sorted_senders, sorted_senders, side='left').astype(jnp.int32)
    rank_sorted = jnp.arange(sorted_senders.shape[0], dtype=jnp.int32) - first_of
    rank_of = jnp.zeros_like(rank_sorted).at[by_sender].set(rank_sorted)

    def slot_table(slot_key):
        return jax.random.permutation(slot_key, OBLK_DEV).astype(jnp.int32)
    slot_keys = jax.random.split(jax.random.fold_in(key, 2), devices)
    slot_tables = jax.vmap(slot_table)(slot_keys)
    slot_pick = slot_tables[senders, rank_of]
    result = jnp.full((devices * OBLK_DEV,), -1, jnp.int32)
    return result.at[senders * OBLK_DEV + slot_pick].set(global_index.astype(jnp.int32))


def touch_ends(values, stream_key, smallest, high):
    longest = values.shape.index(max(values.shape))
    spots = []
    for shift in (0, 1):
        where = [jax.random.randint(jax.random.fold_in(stream_key, axis), (), 0, length) for axis, length in enumerate(values.shape)]
        where[longest] = (where[longest] + shift) % values.shape[longest]
        spots.append(tuple(where))
    return values.at[spots[0]].set(smallest).at[spots[1]].set(high)


def levels(rng, extent, pieces, least, largest):
    factor_of = 1.0
    for dim, parts in pieces:
        heights = jax.random.uniform(jax.random.fold_in(jax.random.fold_in(rng, 6), dim), (parts,), jnp.float32, least / len(pieces), largest / len(pieces))
        factor_of = factor_of * jnp.repeat(jnp.exp(heights), extent[dim] // parts).reshape((-1,) + (1,) * (len(extent) - 1 - dim))
    return factor_of


def noise(key, extent, deviation, most, cuts=(), kind=jnp.bfloat16):
    values = deviation * jax.random.normal(key, extent, jnp.float32)
    if cuts:
        values = values * levels(key, extent, cuts, -0.22, 0.18)
    return jnp.clip(values, -most, most).astype(kind)


def setup_inputs(seed: int = 0) -> dict:
    streams_of = jax.random.split(jax.random.key(seed), 7)
    ice_state = noise(streams_of[0], (IX, 5, BS, L), 0.5, 4.0, ((0, 128),), jnp.float32)
    thickness = jnp.clip(jnp.exp(math.log(3.0) - 2.3025851 * jax.random.uniform(streams_of[1], (IX, NCAT, BS, L), jnp.float32) ** levels(streams_of[1], (IX, NCAT, BS, L), ((0, 128),), -0.2, 0.2)), 0.3, 3.0)
    concentration = jnp.clip(0.04 + 0.16 * jax.random.uniform(streams_of[2], (IX, NCAT, BS, L), jnp.float32) ** levels(streams_of[2], (IX, NCAT, BS, L), ((0, 128),), -0.2, 0.2), 0.04, 0.2)
    cat_mask = touch_ends((jax.random.randint(streams_of[3], (IX, NCAT, BS, L), 0, 4) < 3).astype(jnp.int32), jax.random.fold_in(streams_of[3], 1), 0, 1)
    forcing = noise(streams_of[4], (OCEAN_BLOCK_COUNT, 4, CELLS), 0.5, 4.0, ((0, 128),), jnp.float32)
    ice_target = draw_ice_target(jax.random.fold_in(streams_of[6], 71), 0)
    return {"ice_state": ice_state, "thickness": thickness, "concentration": concentration, "cat_mask": cat_mask, "forcing": forcing, "ice_target": ice_target}


ELASTIC = 0.5
ECC_SQUARED = 4.0
CREEP = 0.05
PRESSURE_SCALE = 1.0
COMPACTNESS_DECAY = 2.0
BASE_MASS = 0.5
DRAG_COEFF = 1.0
TIME_STEP = 0.5
CORIOLIS = 0.2

def ice_static(thickness, concentration, cat_mask):
    present = cat_mask.astype(jnp.float32)
    ice_fraction = lax.optimization_barrier(jnp.sum(concentration * present, axis=0))
    ice_volume = lax.optimization_barrier(jnp.sum(thickness * concentration * present, axis=0))
    ice_mass = ice_volume + BASE_MASS
    ice_strength = PRESSURE_SCALE * ice_volume * jnp.exp(-COMPACTNESS_DECAY * (1.0 - ice_fraction))
    return (ice_fraction, ice_mass, ice_strength)

def stress_update(vel_sides, sig_sum, sig_diff, sig_shear, ice_strength):
    east_side, west_side, north_side, south_side = vel_sides
    stretch_x = 0.5 * (east_side[0] - west_side[0])
    stretch_y = 0.5 * (north_side[1] - south_side[1])
    divergence = stretch_x + stretch_y
    tension = stretch_x - stretch_y
    shearing = 0.5 * (north_side[0] - south_side[0]) + 0.5 * (east_side[1] - west_side[1])
    deform = jnp.sqrt(divergence * divergence + (tension * tension + shearing * shearing) / ECC_SQUARED) + CREEP
    damping = ice_strength + ELASTIC * ECC_SQUARED * deform
    new_sum = (ice_strength * sig_sum + ELASTIC * ice_strength * (divergence - deform)) / (ice_strength + ELASTIC * deform)
    new_diff = (ice_strength * sig_diff + ELASTIC * ice_strength * tension) / damping
    new_shear = (ice_strength * sig_shear + 0.5 * ELASTIC * ice_strength * shearing) / damping
    return (new_sum, new_diff, new_shear)

def momentum_update(vel_east, vel_north, sig_sides, ice_forcing, ice_fraction, ice_mass):
    east_side, west_side, north_side, south_side = sig_sides
    normal_east = 0.5 * (east_side[0] + east_side[1])
    normal_west = 0.5 * (west_side[0] + west_side[1])
    normal_upper = 0.5 * (north_side[0] - north_side[1])
    normal_lower = 0.5 * (south_side[0] - south_side[1])
    force_east = 0.5 * (normal_east - normal_west) + 0.5 * (north_side[2] - south_side[2])
    force_north = 0.5 * (east_side[2] - west_side[2]) + 0.5 * (normal_upper - normal_lower)
    slip_east = ice_forcing[0] - vel_east
    slip_north = ice_forcing[1] - vel_north
    drag_rate = DRAG_COEFF * ice_fraction * jnp.sqrt(slip_east * slip_east + slip_north * slip_north)
    divisor = ice_mass + TIME_STEP * drag_rate
    new_east = (ice_mass * vel_east + TIME_STEP * (force_east + ice_fraction * ice_forcing[2] + drag_rate * ice_forcing[0] + CORIOLIS * ice_mass * vel_north)) / divisor
    new_north = (ice_mass * vel_north + TIME_STEP * (force_north + ice_fraction * ice_forcing[3] + drag_rate * ice_forcing[1] - CORIOLIS * ice_mass * vel_east)) / divisor
    return (new_east, new_north)

def ocean_drag(vel_east, vel_north, ice_forcing, ice_fraction):
    slip_east = vel_east - ice_forcing[0]
    slip_north = vel_north - ice_forcing[1]
    drag_rate = DRAG_COEFF * ice_fraction * jnp.sqrt(slip_east * slip_east + slip_north * slip_north)
    return jnp.stack([drag_rate * slip_east, drag_rate * slip_north])

def to_grid(values):
    return jnp.transpose(values, (1, 0, 2, 3)).reshape(values.shape[1], values.shape[0] * values.shape[2], values.shape[3])

def sides(field, fold_sign):
    east_side = jnp.roll(field, -1, axis=1)
    west_side = jnp.roll(field, 1, axis=1)
    folded = fold_sign[:, None] * field[:, ::-1, -1]
    north_side = jnp.concatenate([field[:, :, 1:], folded[:, :, None]], axis=2)
    south_side = jnp.concatenate([jnp.zeros_like(field[:, :, :1]), field[:, :, :-1]], axis=2)
    return (east_side, west_side, north_side, south_side)

def reference(ice_state, thickness, concentration, cat_mask, forcing, ice_target):
    columns = ice_state.shape[0]
    total = columns * IY
    carried = ice_target >= 0
    where_to = jnp.where(carried, ice_target, total).astype(jnp.int32)
    source = jnp.zeros((total,), jnp.int32).at[where_to].set(jnp.arange(ice_target.shape[0], dtype=jnp.int32), mode='drop')
    ice_blocks = forcing[source]
    ice_forcing = jnp.transpose(ice_blocks.reshape(columns, IY, 4, BS, BS), (2, 0, 3, 1, 4)).reshape(4, columns * BS, IY * BS)
    state = to_grid(ice_state)
    ice_fraction, ice_mass, ice_strength = ice_static(to_grid(thickness), to_grid(concentration), to_grid(cat_mask))
    vel_east, vel_north = (state[0], state[1])
    sig_sum, sig_diff, sig_shear = (state[2], state[3], state[4])
    vel_sign = jnp.array([-1.0, -1.0], dtype=jnp.float32)
    sig_sign = jnp.array([1.0, 1.0, 1.0], dtype=jnp.float32)
    for subcycle in range(SUB):
        vel_sides = sides(jnp.stack([vel_east, vel_north]), vel_sign)
        sig_sum, sig_diff, sig_shear = stress_update(vel_sides, sig_sum, sig_diff, sig_shear, ice_strength)
        sig_sides = sides(jnp.stack([sig_sum, sig_diff, sig_shear]), sig_sign)
        vel_east, vel_north = momentum_update(vel_east, vel_north, sig_sides, ice_forcing, ice_fraction, ice_mass)
    final = jnp.stack([vel_east, vel_north, sig_sum, sig_diff, sig_shear])
    ice_out = jnp.transpose(final.reshape(5, columns, BS, IY * BS), (1, 0, 2, 3))
    drag_stress = ocean_drag(vel_east, vel_north, ice_forcing, ice_fraction)
    stress_blocks = jnp.transpose(drag_stress.reshape(2, columns, BS, IY, BS), (1, 3, 0, 2, 4)).reshape(total, 2, BS * BS)
    picked = stress_blocks[jnp.where(carried, ice_target, 0).astype(jnp.int32)]
    ocean_stress = jnp.where(carried[:, None, None], picked, jnp.zeros_like(picked))
    return (ice_out, ocean_stress)
```

```python
import jax
import jax.numpy as jnp
from jax import lax
from jax.experimental import pallas as pl
from jax.experimental.pallas import tpu as pltpu
from jax.sharding import PartitionSpec as P

MESH = pl.DeviceIdType.MESH
SUB = 8
HALF = 4
H = 2 * HALF
NLON = 32
W = NLON + 2 * H
OWN = H * 8
END = OWN + NLON * 8
NDEV = 128
RB = 33
PER = W // 8
F32 = jnp.float32


def at(d):
    return (d // 4, d % 4)


def rot(x, shift, axis):
    return pltpu.roll(x, shift % x.shape[axis], axis)


def iota(shape, axis):
    return lax.broadcasted_iota(jnp.int32, shape, axis)


def within(i, count):
    return jnp.minimum(jnp.maximum(i, 0), count - 1)


def root(x):
    return x * lax.rsqrt(jnp.maximum(x, 1e-30))


def stress(due_x, dun_y, due_y, dun_x, ss, sd, sh, strength):
    plus = due_x + dun_y
    minus = due_x - dun_y
    cross = due_y + dun_x
    deform = 0.5 * root(plus * plus + 0.25 * (minus * minus + cross * cross)) + 0.05
    ss = strength * (ss + 0.25 * plus - 0.5 * deform) / (strength + 0.5 * deform)
    scaled = strength / (strength + 2.0 * deform)
    sd = scaled * (sd + 0.25 * minus)
    sh = scaled * (sh + 0.125 * cross)
    return ss, sd, sh


def momentum(ue, un, dxx_x, dsh_y, dsh_x, dyy_y, uo, vo, wx, wy, cover, mass):
    force_east = 0.25 * dxx_x + 0.5 * dsh_y
    force_north = 0.5 * dsh_x + 0.25 * dyy_y
    a = uo - ue
    b = vo - un
    drag = cover * root(a * a + b * b)
    inv = 1.0 / (mass + 0.5 * drag)
    tenth = 0.1 * mass
    east = mass * ue + 0.5 * (force_east + cover * wx + drag * uo) + tenth * un
    north = mass * un + 0.5 * (force_north + cover * wy + drag * vo) - tenth * ue
    return east * inv, north * inv


def quads(x0, x1, x2, x3, group):
    low = (group % 2) == 0
    y0 = jnp.where(low, x0, rot(x1, 32, 1))
    y1 = jnp.where(low, rot(x0, -32, 1), x1)
    y2 = jnp.where(low, x2, rot(x3, 32, 1))
    y3 = jnp.where(low, rot(x2, -32, 1), x3)
    low = group < 2
    return (
        jnp.where(low, y0, rot(y2, 64, 1)),
        jnp.where(low, y1, rot(y3, 64, 1)),
        jnp.where(low, rot(y0, -64, 1), y2),
        jnp.where(low, rot(y1, -64, 1), y3),
    )


def kernel(
    tgt, state, thick, conc, mask, forc, ice_out, ocean_out,
    tgt_s, tgt_v, idx_v, idx_s, dst_v, dst_s,
    r_state, r_thick, r_conc, r_mask, fv, outb, arr, tagm,
    st, sc, fo, sp, spc, spf,
    t7, e7, t4, e4, t5, e5, h5,
    dr, sb, out2, ret, ice_v,
    in_sem, loc_sem, a_sem, r_sem, x_send, x_recv,
):
    gx, gy = lax.axis_index("gx"), lax.axis_index("gy")
    me = gx * 4 + gy
    y, z, core, x = gx // 8, (gx // 2) % 4, gx % 2, gy
    sx, sz, sy = 1 - 2 * (x % 2), 1 - 2 * (z % 2), 1 - 2 * (y % 2)

    def peer(k):
        k = (k * 37) % 128
        px = (x + sx * (k % 4) + 4) % 4
        pc = (core + (k // 4) % 2) % 2
        pz = (z + sz * ((k // 8) % 4) + 4) % 4
        py = (y + sy * (k // 32) + 4) % 4
        return (py * 4 + pz) * 2 + pc, px

    loads = [
        pltpu.make_async_copy(src, dst, in_sem.at[i])
        for i, (src, dst) in enumerate(
            [(tgt, tgt_v), (tgt, tgt_s), (thick, r_thick), (conc, r_conc), (mask, r_mask), (state, r_state), (forc, fv)]
        )
    ]
    for load in loads:
        load.start()

    barrier = pltpu.get_barrier_semaphore()

    def greet(k, carry):
        d = (me + k) % NDEV
        pl.semaphore_signal(barrier, inc=1, device_id=at(d), device_id_type=MESH)
        return carry

    lax.fori_loop(1, NDEV, greet, 0)

    square = (NDEV, NDEV)
    lane_sq, sub_sq = iota(square, 1), iota(square, 0)
    loads[0].wait()
    loads[1].wait()
    row = jnp.broadcast_to(tgt_v[...].astype(F32), square)
    column = jnp.sum(jnp.where(lane_sq == sub_sq, row, 0.0), axis=1, keepdims=True)
    target = jnp.broadcast_to(column, square).astype(jnp.int32)
    hit = (target >= 0) & (target // 32 == lane_sq)
    listed = jnp.sum(jnp.where(hit, sub_sq.astype(F32), 0.0), axis=0, keepdims=True)
    place = jnp.sum(jnp.where(hit, (target % 32 + 1).astype(F32), 0.0), axis=0, keepdims=True) - 1.0
    idx_v[0:1, :] = listed.astype(jnp.int32)
    idx_v[1:2, :] = place.astype(jnp.int32)
    to_smem = pltpu.make_async_copy(idx_v, idx_s, loc_sem.at[0])
    to_smem.start()

    for load in loads[2:6]:
        load.wait()

    def relay(n, carry):
        lb, chunk = n // 8, n % 8
        rows, lanes = pl.ds(pl.multiple_of(lb * 8, 8), 8), pl.ds(pl.multiple_of(chunk * 128, 128), 128)
        dst = pl.ds(OWN + lb * 64 + chunk, 8, stride=8)
        cover = jnp.zeros((8, 128), F32)
        volume = jnp.zeros((8, 128), F32)
        for cat in range(5):
            part = r_conc[cat, rows, lanes] * r_mask[cat, rows, lanes].astype(F32)
            cover = cover + part
            volume = volume + r_thick[cat, rows, lanes] * part
        sc[0, dst, :] = cover
        sc[1, dst, :] = volume
        for ch in range(5):
            st[ch, dst, :] = r_state[ch, rows, lanes]
        return carry

    lax.fori_loop(0, 32, relay, 0)

    lane8, sub8 = iota((8, 128), 1), iota((8, 128), 0)

    def turned(v):
        for bit in (1, 2, 4):
            v = jnp.where((sub8 // bit) % 2 == 1, rot(v, bit, 0), rot(v, -bit, 0))
        for bit in (1, 2, 4):
            v = jnp.where((lane8 // bit) % 2 == 1, rot(v, bit, 1), rot(v, -bit, 1))
        return v

    def tops(dst, first, src, signs):
        def group(g, carry):
            start = OWN + (24 - 8 * g) * 8 + 7
            for ch, sign in enumerate(signs):
                v = turned(src[ch, pl.ds(start, 8, stride=8), :])
                dst[first + ch, pl.ds(pl.multiple_of(g * 8, 8), 8), :] = v if sign > 0 else -v
            return carry

        lax.fori_loop(0, 4, group, 0)

    def strip(dst, src, ext, first, count):
        for ch in range(count):
            for b in range(PER):
                own = rot(src[ch, pl.ds(b * 8 + 7, 8, stride=8 * PER), :], -H, 1)
                far = ext[first + ch, pl.ds(b, 8, stride=PER), :]
                dst[ch, b * 8 : b * 8 + 8, :] = jnp.where(lane8 < 128 - H, own, far)

    def merge():
        for ch in range(5):
            for b in range(PER):
                where = pl.ds(b * 8 + 7, 8, stride=8 * PER)
                new = rot(sp[ch, b * 8 : b * 8 + 8, :], H, 1)
                st[ch, where, :] = jnp.where(lane8 >= 128 - H, new, st[ch, where, :])

    tops(t7, 0, st, (-1, -1, 1, 1, 1))
    tops(t7, 5, sc, (1, 1))

    west, east = (me + NDEV - 1) % NDEV, (me + 1) % NDEV
    over, over_east, over_west = NDEV - 1 - me, (NDEV - me) % NDEV, (2 * NDEV - 2 - me) % NDEV

    def remote(src, dst, d, i):
        return pltpu.make_async_remote_copy(
            src_ref=src, dst_ref=dst, send_sem=x_send.at[i], recv_sem=x_recv.at[i],
            device_id=at(d), device_id_type=MESH,
        )

    def beside(ref, to_west, to_east, i):
        return [
            (remote(ref.at[:, pl.ds(OWN, OWN)], to_west, west, i), None, None),
            (remote(ref.at[:, pl.ds(END - OWN, OWN)], to_east, east, i + 1), None, None),
        ]

    def across(t, e, i):
        parts = []
        for n, (d, src, dst) in enumerate(
            [
                (over, t, e.at[:, pl.ds(H, NLON)]),
                (over_east, t.at[:, pl.ds(NLON - H, H)], e.at[:, pl.ds(0, H)]),
                (over_west, t.at[:, pl.ds(0, H)], e.at[:, pl.ds(NLON + H, H)]),
            ]
        ):
            here = pltpu.make_async_copy(src, dst, x_recv.at[i + n]) if n else None
            parts.append((remote(src, dst, d, i + n), here, d))
        return parts

    def start(copies):
        for copy, here, d in copies:
            if here is None:
                copy.start()
            else:
                pl.when(d != me)(copy.start)
                pl.when(d == me)(here.start)

    def landed(copies):
        for copy, _, _ in copies:
            copy.wait_recv()

    def left(copies):
        for copy, here, d in copies:
            if here is None:
                copy.wait_send()
            else:
                pl.when(d != me)(copy.wait_send)

    first = (
        beside(st, st.at[:, pl.ds(END, OWN)], st.at[:, pl.ds(0, OWN)], 0)
        + beside(
            sc.at[pl.ds(0, 2)],
            sc.at[pl.ds(0, 2), pl.ds(END, OWN)],
            sc.at[pl.ds(0, 2), pl.ds(0, OWN)],
            2,
        )
        + across(t7, e7, 4)
    )
    second = beside(fo, fo.at[:, pl.ds(END, OWN)], fo.at[:, pl.ds(0, OWN)], 7) + across(t4, e4, 9)
    third = beside(st, h5.at[1], h5.at[0], 12) + across(t5, e5, 14)

    to_smem.wait()
    loads[6].wait()

    def pack(c, carry):
        outb[c, 0:32, :] = fv[within(idx_s[0, c], NDEV)]
        outb[c, 32:33, :] = jnp.full((1, 128), idx_s[1, c].astype(F32))
        return carry

    lax.fori_loop(0, NDEV, pack, 0, unroll=4)

    pl.semaphore_wait(barrier, NDEV - 1)
    start(first)

    def send(k, carry):
        a, b = peer(k)
        pltpu.make_async_remote_copy(
            src_ref=outb.at[a * 4 + b], dst_ref=arr.at[me], send_sem=a_sem.at[0], recv_sem=a_sem.at[1],
            device_id=(a, b), device_id_type=MESH,
        ).start()
        return carry

    lax.fori_loop(1, NDEV, send, 0)
    own_block = pltpu.make_async_copy(outb.at[me], arr.at[me], loc_sem.at[1])
    own_block.start()

    shape2 = (2, 8, 128)
    lane2, sub2 = iota(shape2, 2), iota(shape2, 1)

    def get(ref, ch, r):
        return ref[ch, pl.ds(pl.multiple_of(r, 8), 16), :].reshape(shape2)

    def put(ref, ch, r, v):
        ref[ch, pl.ds(pl.multiple_of(r, 8), 16), :] = v.reshape(16, 128)

    def diff_lon(ref, ch, r):
        return get(ref, ch, r + 8) - get(ref, ch, r - 8)

    def diff_lat(v):
        up = rot(v, -1, 2)
        up = jnp.where(lane2 == 127, rot(up, -1, 1), up)
        down = rot(v, 1, 2)
        down = jnp.where(lane2 == 0, jnp.where(sub2 == 0, 0.0, rot(down, 1, 1)), down)
        return up - down

    def strip_lon(v):
        upper = jnp.concatenate([v[1:], rot(v[:1], -1, 1)], axis=0)
        lower = jnp.concatenate([rot(v[-1:], 1, 1), v[:-1]], axis=0)
        return upper - lower

    def strip_lat(v):
        return rot(v, -1, 2) - rot(v, 1, 2)

    def whole(ref, ch):
        return ref[ch].reshape(PER, 8, 128)

    def keep(ref, ch, v):
        ref[ch] = v.reshape(PER * 8, 128)

    def sweep(lo, hi, body):
        def step(n, carry):
            body((lo + 2 * n) * 8)
            return carry

        lax.fori_loop(0, (hi - lo) // 2, step, 0)

    def strength_of(volume, cover):
        return volume * jnp.exp(-2.0 * (1.0 - cover))

    def stress_step(m):
        def body(r):
            ue, un = get(st, 0, r), get(st, 1, r)
            new = stress(
                diff_lon(st, 0, r), diff_lat(un), diff_lat(ue), diff_lon(st, 1, r),
                get(st, 2, r), get(st, 3, r), get(st, 4, r), get(sc, 2, r),
            )
            for ch in range(3):
                put(st, 2 + ch, r, new[ch])

        sweep(1 + 2 * m, W - 1 - 2 * m, body)
        ue, un = whole(sp, 0), whole(sp, 1)
        new = stress(
            strip_lon(ue), strip_lat(un), strip_lat(ue), strip_lon(un),
            whole(sp, 2), whole(sp, 3), whole(sp, 4), whole(spc, 2),
        )
        for ch in range(3):
            keep(sp, 2 + ch, new[ch])

    def momentum_step(m):
        def body(r):
            ss, sd, sh = get(st, 2, r), get(st, 3, r), get(st, 4, r)
            dxx = diff_lon(st, 2, r) + diff_lon(st, 3, r)
            new = momentum(
                get(st, 0, r), get(st, 1, r), dxx, diff_lat(sh), diff_lon(st, 4, r), diff_lat(ss - sd),
                get(fo, 0, r), get(fo, 1, r), get(fo, 2, r), get(fo, 3, r), get(sc, 0, r), get(sc, 1, r),
            )
            put(st, 0, r, new[0])
            put(st, 1, r, new[1])

        sweep(2 + 2 * m, W - 2 - 2 * m, body)
        ss, sd, sh = whole(sp, 2), whole(sp, 3), whole(sp, 4)
        new = momentum(
            whole(sp, 0), whole(sp, 1), strip_lon(ss + sd), strip_lat(sh), strip_lon(sh), strip_lat(ss - sd),
            whole(spf, 0), whole(spf, 1), whole(spf, 2), whole(spf, 3), whole(spc, 0), whole(spc, 1),
        )
        keep(sp, 0, new[0])
        keep(sp, 1, new[1])

    landed(first)
    left(first)
    strip(sp, st, e7, 0, 5)
    strip(spc, sc, e7, 5, 2)

    def statics(r):
        cover, volume = get(sc, 0, r), get(sc, 1, r)
        put(sc, 1, r, volume + 0.5)
        put(sc, 2, r, strength_of(volume, cover))

    sweep(0, W, statics)
    cover, volume = whole(spc, 0), whole(spc, 1)
    keep(spc, 1, volume + 0.5)
    keep(spc, 2, strength_of(volume, cover))
    stress_step(0)

    own_block.wait()
    some = pltpu.make_async_remote_copy(
        src_ref=outb.at[pl.ds(0, NDEV - 1)], dst_ref=arr.at[pl.ds(0, NDEV - 1)],
        send_sem=a_sem.at[0], recv_sem=a_sem.at[1], device_id=(gx, gy), device_id_type=MESH,
    )
    some.wait_recv()

    def tag(s, carry):
        tagm[pl.ds(s, 1), :] = arr[s, 32:33, :]
        return carry

    lax.fori_loop(0, NDEV, tag, 0, unroll=8)
    tags = tagm[...]
    origin = jnp.sum(jnp.where(tags.astype(jnp.int32) == lane_sq, sub_sq.astype(F32), 0.0), axis=0, keepdims=True)
    back = jnp.sum(jnp.where(sub_sq == lane_sq, tags, 0.0), axis=0, keepdims=True)
    dst_v[0:1, :] = origin.astype(jnp.int32)
    dst_v[1:2, :] = jnp.maximum(back, 0.0).astype(jnp.int32)
    to_smem = pltpu.make_async_copy(dst_v, dst_s, loc_sem.at[2])
    to_smem.start()
    to_smem.wait()

    group8 = lane8 // 32

    def place_rows(chunk, carry):
        sources = [within(dst_s[0, chunk * 4 + j], NDEV) for j in range(4)]
        for ch in range(4):
            rows = quads(*[arr[s, pl.ds(ch, 8, stride=4), :] for s in sources], group8)
            for p in range(4):
                fo[ch, pl.ds(OWN + p * 8 + chunk, 8, stride=32), :] = rows[p]
        return carry

    lax.fori_loop(0, 8, place_rows, 0)
    tops(t4, 0, fo, (-1, -1, -1, -1))
    start(second)
    landed(second)
    strip(spf, fo, e4, 0, 4)

    momentum_step(0)
    for m in range(1, HALF):
        stress_step(m)
        momentum_step(m)

    merge()
    tops(t5, 0, st, (-1, -1, 1, 1, 1))
    start(third)
    landed(third)
    left(third)
    for ch in range(5):
        st[ch, 0:OWN, :] = h5[0, ch]
        st[ch, END:, :] = h5[1, ch]
    strip(sp, st, e5, 0, 5)
    for m in range(HALF):
        stress_step(m)
        momentum_step(m)
    merge()

    def drag(r):
        a = get(st, 0, r) - get(fo, 0, r)
        b = get(st, 1, r) - get(fo, 1, r)
        rate = get(sc, 0, r) * root(a * a + b * b)
        put(dr, 0, r - OWN, rate * a)
        put(dr, 1, r - OWN, rate * b)

    sweep(H, H + NLON, drag)

    def blocks(chunk, carry):
        for ch in range(2):
            rows = quads(*[dr[ch, pl.ds(p * 8 + chunk, 8, stride=32), :] for p in range(4)], group8)
            for j in range(4):
                sb[chunk * 4 + j, pl.ds(ch, 8, stride=2), :] = rows[j]
        return carry

    lax.fori_loop(0, 8, blocks, 0)

    def give(k, carry):
        a, b = peer(k)
        d = a * 4 + b
        out2[d] = sb[within(dst_s[1, d], 32)]
        pltpu.make_async_remote_copy(
            src_ref=out2.at[d], dst_ref=ret.at[me], send_sem=r_sem.at[0], recv_sem=r_sem.at[1],
            device_id=(a, b), device_id_type=MESH,
        ).start()
        return carry

    lax.fori_loop(1, NDEV, give, 0)
    ret[me] = sb[within(dst_s[1, me], 32)]

    def lay_out(n, carry):
        lb, chunk = n // 8, n % 8
        rows, lanes = pl.ds(pl.multiple_of(lb * 8, 8), 8), pl.ds(pl.multiple_of(chunk * 128, 128), 128)
        for ch in range(5):
            ice_v[ch, rows, lanes] = st[ch, pl.ds(OWN + lb * 64 + chunk, 8, stride=8), :]
        return carry

    lax.fori_loop(0, 32, lay_out, 0)
    store = pltpu.make_async_copy(ice_v, ice_out, loc_sem.at[3])
    store.start()

    left(second)
    some.wait_send()
    some = pltpu.make_async_remote_copy(
        src_ref=out2.at[pl.ds(0, NDEV - 1)], dst_ref=ret.at[pl.ds(0, NDEV - 1)],
        send_sem=r_sem.at[0], recv_sem=r_sem.at[1], device_id=(gx, gy), device_id_type=MESH,
    )
    some.wait_recv()

    def unpack(b, carry):
        t = tgt_s[0, b]
        v = ret[within(t // 32, NDEV)]
        ocean_out[b] = jnp.where(t >= 0, v, 0.0)
        return carry

    lax.fori_loop(0, NDEV, unpack, 0, unroll=4)
    store.wait()
    some.wait_send()


def local(ice_state, thickness, concentration, cat_mask, forcing, ice_target):
    blocks = forcing.reshape(NDEV, 4, 8, 128).transpose(0, 2, 1, 3).reshape(NDEV, 32, 128)
    hbm = pl.BlockSpec(memory_space=pl.ANY)
    vmem, dma = pltpu.VMEM, pltpu.SemaphoreType.DMA

    def v(*shape, dtype=F32):
        return vmem(shape, dtype)

    raw = (5, NLON, 1024)
    rows = W * 8
    ice, ocean = pl.pallas_call(
        kernel,
        out_shape=(
            jax.ShapeDtypeStruct(raw, F32),
            jax.ShapeDtypeStruct((NDEV, 16, 128), F32),
        ),
        in_specs=[hbm] * 6,
        out_specs=(hbm, pl.BlockSpec(memory_space=vmem)),
        scratch_shapes=[
            pltpu.SMEM((1, 128), jnp.int32), v(1, 128, dtype=jnp.int32),
            v(8, 128, dtype=jnp.int32), pltpu.SMEM((8, 128), jnp.int32),
            v(8, 128, dtype=jnp.int32), pltpu.SMEM((8, 128), jnp.int32),
            v(*raw), v(*raw), v(*raw), v(*raw, dtype=jnp.int32),
            v(NDEV, 32, 128), v(NDEV, RB, 128), v(NDEV, RB, 128), v(NDEV, 128),
            v(5, rows, 128), v(3, rows, 128), v(4, rows, 128),
            v(5, W, 128), v(3, W, 128), v(4, W, 128),
            v(7, NLON, 128), v(7, W, 128), v(4, NLON, 128), v(4, W, 128), v(5, NLON, 128), v(5, W, 128),
            v(2, 5, OWN, 128),
            v(2, NLON * 8, 128), v(32, 16, 128), v(NDEV, 16, 128), v(NDEV, 16, 128), v(*raw),
            dma((7,)), dma((4,)), dma((2,)), dma((2,)), dma((17,)), dma((17,)),
        ],
        compiler_params=pltpu.CompilerParams(
            collective_id=0, has_side_effects=True, vmem_limit_bytes=48 * 2**20
        ),
        name="ice",
    )(ice_target.reshape(1, NDEV), ice_state[0], thickness[0], concentration[0], cat_mask[0], blocks)
    ocean = ocean.reshape(NDEV, 8, 2, 128).transpose(0, 2, 1, 3).reshape(NDEV, 2, 1024)
    return ice[None], ocean


def solution(mesh):
    lead = ("gx", "gy")
    four, three = P(lead, None, None, None), P(lead, None, None)
    return jax.shard_map(
        local,
        mesh=mesh,
        in_specs=(four, four, four, four, three, P(lead)),
        out_specs=(four, three),
        check_vma=False,
    )
```

```python
import jax
import jax.numpy as jnp
from jax import lax
from jax.experimental import pallas as pl
from jax.experimental.pallas import tpu as pltpu
from jax.sharding import PartitionSpec as P

MESH = pl.DeviceIdType.MESH
SUB = 8
HALF = 4
H = 2 * HALF
NLON = 32
W = NLON + 2 * H
OWN = H * 8
END = OWN + NLON * 8
NDEV = 128
RB = 33
PER = W // 8
F32 = jnp.float32


def at(d):
    return (d // 4, d % 4)


def rot(x, shift, axis):
    return pltpu.roll(x, shift % x.shape[axis], axis)


def iota(shape, axis):
    return lax.broadcasted_iota(jnp.int32, shape, axis)


def within(i, count):
    return jnp.minimum(jnp.maximum(i, 0), count - 1)


def root(x):
    return x * lax.rsqrt(jnp.maximum(x, 1e-30))


def stress(due_x, dun_y, due_y, dun_x, ss, sd, sh, strength):
    plus = due_x + dun_y
    minus = due_x - dun_y
    cross = due_y + dun_x
    deform = 0.5 * root(plus * plus + 0.25 * (minus * minus + cross * cross)) + 0.05
    ss = strength * (ss + 0.25 * plus - 0.5 * deform) / (strength + 0.5 * deform)
    scaled = strength / (strength + 2.0 * deform)
    sd = scaled * (sd + 0.25 * minus)
    sh = scaled * (sh + 0.125 * cross)
    return ss, sd, sh


def momentum(ue, un, dxx_x, dsh_y, dsh_x, dyy_y, uo, vo, wx, wy, cover, mass):
    force_east = 0.25 * dxx_x + 0.5 * dsh_y
    force_north = 0.5 * dsh_x + 0.25 * dyy_y
    a = uo - ue
    b = vo - un
    drag = cover * root(a * a + b * b)
    inv = 1.0 / (mass + 0.5 * drag)
    tenth = 0.1 * mass
    east = mass * ue + 0.5 * (force_east + cover * wx + drag * uo) + tenth * un
    north = mass * un + 0.5 * (force_north + cover * wy + drag * vo) - tenth * ue
    return east * inv, north * inv


def quads(x0, x1, x2, x3, group):
    low = (group % 2) == 0
    y0 = jnp.where(low, x0, rot(x1, 32, 1))
    y1 = jnp.where(low, rot(x0, -32, 1), x1)
    y2 = jnp.where(low, x2, rot(x3, 32, 1))
    y3 = jnp.where(low, rot(x2, -32, 1), x3)
    low = group < 2
    return (
        jnp.where(low, y0, rot(y2, 64, 1)),
        jnp.where(low, y1, rot(y3, 64, 1)),
        jnp.where(low, rot(y0, -64, 1), y2),
        jnp.where(low, rot(y1, -64, 1), y3),
    )


def kernel(
    tgt, state, thick, conc, mask, forc, ice_out, ocean_out,
    tgt_s, tgt_v, idx_v, idx_s, dst_v, dst_s,
    r_state, r_thick, r_conc, r_mask, fv, outb, arr, tagm,
    st, sc, fo, sp, spc, spf,
    t7, p7, t4, p4, t5, p5, ext, edge, h5,
    dr, sb, out2, ret, ice_v,
    in_sem, loc_sem, a_sem, r_sem, x_send, x_recv,
):
    gx, gy = lax.axis_index("gx"), lax.axis_index("gy")
    me = gx * 4 + gy
    y, z, core, x = gx // 8, (gx // 2) % 4, gx % 2, gy

    def flipped(bit, by):
        return 1 - bit if by else bit

    low = []
    for n in range(16):
        n = (n * 5) % 16
        px = 2 * flipped(x // 2, (n // 2) % 2) + flipped(x % 2, n % 2)
        low.append((2 * flipped(z % 2, (n // 8) % 2) + flipped(core, (n // 4) % 2), px))

    def for_peers(act):
        def turn(q, carry):
            high = []
            for r in range(8):
                m = (q + r) % 8
                z1 = (z // 2 + m) % 2
                y0 = (y + m // 2) % 2
                y1 = (y // 2 + m // 4) % 2
                high.append(8 * (2 * y1 + y0) + 4 * z1)
            for n in range(16):
                a, b = high[(3 * n) % 8] + low[n][0], low[n][1]
                if n:
                    act(a, b)
                else:
                    pl.when(q != 0)(lambda a=a, b=b: act(a, b))
            return carry

        lax.fori_loop(0, 8, turn, 0)

    loads = [
        pltpu.make_async_copy(src, dst, in_sem.at[i])
        for i, (src, dst) in enumerate(
            [(tgt, tgt_v), (tgt, tgt_s), (thick, r_thick), (conc, r_conc), (mask, r_mask), (state, r_state), (forc, fv)]
        )
    ]
    for load in loads:
        load.start()

    barrier = pltpu.get_barrier_semaphore()

    def greet(a, b):
        pl.semaphore_signal(barrier, inc=1, device_id=(a, b), device_id_type=MESH)

    for b in range(1, 4):
        greet(gx, (gy + b) % 4)

    def greet_all(k, carry):
        a = (gx + k) % 32
        for b in range(4):
            greet(a, b)
        return carry

    lax.fori_loop(1, 32, greet_all, 0)

    square = (NDEV, NDEV)
    lane_sq, sub_sq = iota(square, 1), iota(square, 0)
    loads[0].wait()
    loads[1].wait()
    row = jnp.broadcast_to(tgt_v[...].astype(F32), square)
    column = jnp.sum(jnp.where(lane_sq == sub_sq, row, 0.0), axis=1, keepdims=True)
    target = jnp.broadcast_to(column, square).astype(jnp.int32)
    hit = (target >= 0) & (target // 32 == lane_sq)
    listed = jnp.sum(jnp.where(hit, sub_sq.astype(F32), 0.0), axis=0, keepdims=True)
    place = jnp.sum(jnp.where(hit, (target % 32 + 1).astype(F32), 0.0), axis=0, keepdims=True) - 1.0
    idx_v[0:1, :] = listed.astype(jnp.int32)
    idx_v[1:2, :] = place.astype(jnp.int32)
    to_smem = pltpu.make_async_copy(idx_v, idx_s, loc_sem.at[0])
    to_smem.start()

    for load in loads[2:6]:
        load.wait()

    def relay(n, carry):
        lb, chunk = n // 8, n % 8
        rows, lanes = pl.ds(pl.multiple_of(lb * 8, 8), 8), pl.ds(pl.multiple_of(chunk * 128, 128), 128)
        dst = pl.ds(OWN + lb * 64 + chunk, 8, stride=8)
        cover = jnp.zeros((8, 128), F32)
        volume = jnp.zeros((8, 128), F32)
        for cat in range(5):
            part = r_conc[cat, rows, lanes] * r_mask[cat, rows, lanes].astype(F32)
            cover = cover + part
            volume = volume + r_thick[cat, rows, lanes] * part
        sc[0, dst, :] = cover
        sc[1, dst, :] = volume
        for ch in range(5):
            st[ch, dst, :] = r_state[ch, rows, lanes]
        return carry

    lax.fori_loop(0, 32, relay, 0)

    lane8, sub8 = iota((8, 128), 1), iota((8, 128), 0)

    def turned(v):
        for bit in (1, 2, 4):
            v = jnp.where((sub8 // bit) % 2 == 1, rot(v, bit, 0), rot(v, -bit, 0))
        for bit in (1, 2, 4):
            v = jnp.where((lane8 // bit) % 2 == 1, rot(v, bit, 1), rot(v, -bit, 1))
        return v

    def tops(dst, parts):
        full = []
        for n, (src, ch, sign) in enumerate([part for part in parts for _ in range(4)]):
            g, q = n % 4, n % 16
            v = rot(src[ch, pl.ds(OWN + (24 - 8 * g) * 8 + 7, 8, stride=8), :], 8 * q + 8, 1)
            v = v if sign > 0 else -v
            if q == 0:
                full.append(v)
            else:
                full[-1] = jnp.where(lane8 // 8 == q, v, full[-1])
        for n, v in enumerate(full):
            dst[8 * n : 8 * n + 8, :] = turned(v)

    def beyond(packed, count):
        for ch in range(count):
            for k in range(6):
                source, g = (1, 3) if k == 0 else (2, 0) if k == 5 else (0, k - 1)
                n = ch * 4 + g
                v = packed[source, 8 * (n // 16) : 8 * (n // 16) + 8, :]
                ext[ch, 8 * k : 8 * k + 8, :] = rot(v, 120 - 8 * (n % 16), 1)

    def strip_own(dst, src, count, fresh=None):
        for ch in range(count):
            for b in range(PER):
                v = rot(src[ch, pl.ds(b * 8 + 7, 8, stride=8 * PER), :], -H, 1)
                if fresh is not None:
                    lon = sub8 * PER + b
                    v = jnp.where((lon < H) | (lon >= H + NLON), v, dst[ch, b * 8 : b * 8 + 8, :])
                dst[ch, b * 8 : b * 8 + 8, :] = v

    def strip_far(dst, first, count):
        for ch in range(count):
            for b in range(PER):
                where = slice(b * 8, b * 8 + 8)
                far = ext[first + ch, pl.ds(b, 8, stride=PER), :]
                dst[ch, where, :] = jnp.where(lane8 < 128 - H, dst[ch, where, :], far)

    def merge():
        for ch in range(5):
            for b in range(PER):
                where = pl.ds(b * 8 + 7, 8, stride=8 * PER)
                new = rot(sp[ch, b * 8 : b * 8 + 8, :], H, 1)
                st[ch, where, :] = jnp.where(lane8 >= 128 - H, new, st[ch, where, :])

    state_parts = [(st, 0, -1), (st, 1, -1), (st, 2, 1), (st, 3, 1), (st, 4, 1)]
    tops(t7, state_parts + [(sc, 0, 1), (sc, 1, 1)])

    west, east = (me + NDEV - 1) % NDEV, (me + 1) % NDEV
    over, over_east, over_west = NDEV - 1 - me, (NDEV - me) % NDEV, (2 * NDEV - 2 - me) % NDEV

    def remote(src, dst, d, i):
        return pltpu.make_async_remote_copy(
            src_ref=src, dst_ref=dst, send_sem=x_send.at[i], recv_sem=x_recv.at[i],
            device_id=at(d), device_id_type=MESH,
        )

    def beside(to_west, to_east, at_west, at_east, i):
        return [
            (remote(to_west, at_east, west, i), None, None),
            (remote(to_east, at_west, east, i + 1), None, None),
        ]

    def halo(ref, count, i):
        def part(lon):
            return ref.at[pl.ds(0, count), pl.ds(lon * 8, OWN)]

        return beside(part(H), part(NLON), part(0), part(H + NLON), i)

    def across(t, p, i):
        parts = []
        for n, d in enumerate([over, over_east, over_west]):
            here = pltpu.make_async_copy(t, p.at[n], x_recv.at[i + n]) if n else None
            parts.append((remote(t, p.at[n], d, i + n), here, d))
        return parts

    def start(copies):
        for copy, here, d in copies:
            if here is None:
                copy.start()
            else:
                pl.when(d != me)(copy.start)
                pl.when(d == me)(here.start)

    def landed(copies):
        for copy, _, _ in copies:
            copy.wait_recv()

    def left(copies):
        for copy, here, d in copies:
            if here is None:
                copy.wait_send()
            else:
                pl.when(d != me)(copy.wait_send)

    first = halo(st, 5, 0) + halo(sc, 2, 2) + across(t7, p7, 4)
    second = halo(fo, 4, 7) + across(t4, p4, 9)
    third = beside(edge.at[0], edge.at[1], h5.at[0], h5.at[1], 12) + across(t5, p5, 14)

    to_smem.wait()
    loads[6].wait()

    def pack(c, carry):
        outb[c, 0:32, :] = fv[within(idx_s[0, c], NDEV)]
        outb[c, 32:33, :] = jnp.full((1, 128), idx_s[1, c].astype(F32))
        return carry

    lax.fori_loop(0, NDEV, pack, 0, unroll=4)

    pl.semaphore_wait(barrier, NDEV - 1)
    start(first)

    def send(a, b):
        pltpu.make_async_remote_copy(
            src_ref=outb.at[a * 4 + b], dst_ref=arr.at[me], send_sem=a_sem.at[0], recv_sem=a_sem.at[1],
            device_id=(a, b), device_id_type=MESH,
        ).start()

    for_peers(send)
    own_block = pltpu.make_async_copy(outb.at[me], arr.at[me], loc_sem.at[1])
    own_block.start()

    def get(ref, ch, r, n, shift=0):
        return ref[ch, pl.ds(pl.multiple_of(r, 8) + shift, 8 * n), :]

    def put(ref, ch, r, n, v):
        ref[ch, pl.ds(pl.multiple_of(r, 8), 8 * n), :] = v

    def diff_lon(ref, ch, r, n):
        return get(ref, ch, r + 8, n) - get(ref, ch, r - 8, n)

    def diff_lat(ref, ch, r, n):
        v = get(ref, ch, r, n)
        lane, sub = iota(v.shape, 1), iota(v.shape, 0) % 8
        up = jnp.where(lane == 0, get(ref, ch, r, n, 1), v)
        down = jnp.where(sub == 0, 0.0, get(ref, ch, r, n, -1))
        down = jnp.where(lane == 127, down, v)
        return rot(up, -1, 1) - rot(down, 1, 1)

    def strip_lon(v):
        upper = jnp.concatenate([v[1:], rot(v[:1], -1, 1)], axis=0)
        lower = jnp.concatenate([rot(v[-1:], 1, 1), v[:-1]], axis=0)
        return upper - lower

    def strip_lat(v):
        return rot(v, -1, 2) - rot(v, 1, 2)

    def whole(ref, ch):
        return ref[ch].reshape(PER, 8, 128)

    def keep(ref, ch, v):
        ref[ch] = v.reshape(PER * 8, 128)

    def sweep(lo, hi, body):
        def step(i, carry):
            body((lo + 4 * i) * 8, 4)
            return carry

        count = (hi - lo) // 4
        if count:
            lax.fori_loop(0, count, step, 0)
        if (hi - lo) % 4:
            body((lo + 4 * count) * 8, (hi - lo) % 4)

    def strength_of(volume, cover):
        return volume * jnp.exp(-2.0 * (1.0 - cover))

    def stress_at(r, n):
        new = stress(
            diff_lon(st, 0, r, n), diff_lat(st, 1, r, n), diff_lat(st, 0, r, n), diff_lon(st, 1, r, n),
            get(st, 2, r, n), get(st, 3, r, n), get(st, 4, r, n), get(sc, 2, r, n),
        )
        for ch in range(3):
            put(st, 2 + ch, r, n, new[ch])
        put(st, 5, r, n, new[0] - new[1])

    def stress_strip():
        ue, un = whole(sp, 0), whole(sp, 1)
        new = stress(
            strip_lon(ue), strip_lat(un), strip_lat(ue), strip_lon(un),
            whole(sp, 2), whole(sp, 3), whole(sp, 4), whole(spc, 2),
        )
        for ch in range(3):
            keep(sp, 2 + ch, new[ch])

    def momentum_at(r, n):
        dxx = diff_lon(st, 2, r, n) + diff_lon(st, 3, r, n)
        new = momentum(
            get(st, 0, r, n), get(st, 1, r, n),
            dxx, diff_lat(st, 4, r, n), diff_lon(st, 4, r, n), diff_lat(st, 5, r, n),
            get(fo, 0, r, n), get(fo, 1, r, n), get(fo, 2, r, n), get(fo, 3, r, n), get(sc, 0, r, n), get(sc, 1, r, n),
        )
        put(st, 0, r, n, new[0])
        put(st, 1, r, n, new[1])

    def momentum_strip():
        ss, sd, sh = whole(sp, 2), whole(sp, 3), whole(sp, 4)
        new = momentum(
            whole(sp, 0), whole(sp, 1), strip_lon(ss + sd), strip_lat(sh), strip_lon(sh), strip_lat(ss - sd),
            whole(spf, 0), whole(spf, 1), whole(spf, 2), whole(spf, 3), whole(spc, 0), whole(spc, 1),
        )
        keep(sp, 0, new[0])
        keep(sp, 1, new[1])

    landed(first)
    left(first)
    beyond(p7, 7)
    strip_own(sp, st, 5)
    strip_far(sp, 0, 5)
    strip_own(spc, sc, 2)
    strip_far(spc, 5, 2)

    def statics(r, n):
        cover, volume = get(sc, 0, r, n), get(sc, 1, r, n)
        put(sc, 1, r, n, volume + 0.5)
        put(sc, 2, r, n, strength_of(volume, cover))

    sweep(0, W, statics)
    cover, volume = whole(spc, 0), whole(spc, 1)
    keep(spc, 1, volume + 0.5)
    keep(spc, 2, strength_of(volume, cover))
    sweep(1, W - 1, stress_at)
    stress_strip()

    own_block.wait()
    some = pltpu.make_async_remote_copy(
        src_ref=outb.at[pl.ds(0, NDEV - 1)], dst_ref=arr.at[pl.ds(0, NDEV - 1)],
        send_sem=a_sem.at[0], recv_sem=a_sem.at[1], device_id=(gx, gy), device_id_type=MESH,
    )
    some.wait_recv()

    def tag(s, carry):
        tagm[pl.ds(s, 1), :] = arr[s, 32:33, :]
        return carry

    lax.fori_loop(0, NDEV, tag, 0, unroll=8)
    tags = tagm[...]
    origin = jnp.sum(jnp.where(tags.astype(jnp.int32) == lane_sq, sub_sq.astype(F32), 0.0), axis=0, keepdims=True)
    back = jnp.sum(jnp.where(sub_sq == lane_sq, tags, 0.0), axis=0, keepdims=True)
    dst_v[0:1, :] = origin.astype(jnp.int32)
    dst_v[1:2, :] = jnp.maximum(back, 0.0).astype(jnp.int32)
    to_smem = pltpu.make_async_copy(dst_v, dst_s, loc_sem.at[2])
    to_smem.start()
    to_smem.wait()

    group8 = lane8 // 32

    def place_rows(chunk, carry):
        sources = [within(dst_s[0, chunk * 4 + j], NDEV) for j in range(4)]
        for ch in range(4):
            rows = quads(*[arr[s, pl.ds(ch, 8, stride=4), :] for s in sources], group8)
            for p in range(4):
                fo[ch, pl.ds(OWN + p * 8 + chunk, 8, stride=32), :] = rows[p]
        return carry

    lax.fori_loop(0, 8, place_rows, 0)
    tops(t4, [(fo, 0, -1), (fo, 1, -1), (fo, 2, -1), (fo, 3, -1)])
    start(second)

    sweep(H, H + NLON, momentum_at)
    for m in range(1, HALF):
        sweep(H - 1 + 2 * m, W - H + 1 - 2 * m, stress_at)
        sweep(H + 2 * m, W - H - 2 * m, momentum_at)

    landed(second)
    beyond(p4, 4)
    strip_own(spf, fo, 4)
    strip_far(spf, 0, 4)

    def rims(first_lon, width, body):
        for lon in (first_lon, W - first_lon - width):
            for n in range(0, width, 4):
                body((lon + n) * 8, min(4, width - n))

    rims(2, H - 2, momentum_at)
    momentum_strip()

    def rest_one(m, carry):
        rims(1 + 2 * m, H - 2, stress_at)
        stress_strip()
        rims(2 + 2 * m, H - 2, momentum_at)
        momentum_strip()
        return carry

    lax.fori_loop(1, HALF, rest_one, 0)

    merge()
    tops(t5, state_parts)
    for ch in range(5):
        edge[0, ch] = st[ch, OWN : 2 * OWN, :]
        edge[1, ch] = st[ch, END - OWN : END, :]
    start(third)
    strip_own(sp, st, 5)
    for m in range(HALF):
        sweep(H + 1 + 2 * m, W - H - 1 - 2 * m, stress_at)
        sweep(H + 2 + 2 * m, W - H - 2 - 2 * m, momentum_at)

    landed(third)
    for ch in range(5):
        st[ch, 0:OWN, :] = h5[0, ch]
        st[ch, END:, :] = h5[1, ch]
    beyond(p5, 5)
    strip_own(sp, st, 5, True)
    strip_far(sp, 0, 5)

    def rest_two(m, carry):
        rims(1 + 2 * m, H, stress_at)
        stress_strip()
        rims(2 + 2 * m, H, momentum_at)
        momentum_strip()
        return carry

    lax.fori_loop(0, HALF, rest_two, 0)
    merge()

    def drag(r, n):
        a = get(st, 0, r, n) - get(fo, 0, r, n)
        b = get(st, 1, r, n) - get(fo, 1, r, n)
        rate = get(sc, 0, r, n) * root(a * a + b * b)
        put(dr, 0, r - OWN, n, rate * a)
        put(dr, 1, r - OWN, n, rate * b)

    sweep(H, H + NLON, drag)

    def blocks(chunk, carry):
        for ch in range(2):
            rows = quads(*[dr[ch, pl.ds(p * 8 + chunk, 8, stride=32), :] for p in range(4)], group8)
            for j in range(4):
                sb[chunk * 4 + j, pl.ds(ch, 8, stride=2), :] = rows[j]
        return carry

    lax.fori_loop(0, 8, blocks, 0)

    def give(a, b):
        d = a * 4 + b
        out2[d] = sb[within(dst_s[1, d], 32)]
        pltpu.make_async_remote_copy(
            src_ref=out2.at[d], dst_ref=ret.at[me], send_sem=r_sem.at[0], recv_sem=r_sem.at[1],
            device_id=(a, b), device_id_type=MESH,
        ).start()

    for_peers(give)
    ret[me] = sb[within(dst_s[1, me], 32)]

    def lay_out(n, carry):
        lb, chunk = n // 8, n % 8
        rows, lanes = pl.ds(pl.multiple_of(lb * 8, 8), 8), pl.ds(pl.multiple_of(chunk * 128, 128), 128)
        for ch in range(5):
            ice_v[ch, rows, lanes] = st[ch, pl.ds(OWN + lb * 64 + chunk, 8, stride=8), :]
        return carry

    lax.fori_loop(0, 32, lay_out, 0)
    store = pltpu.make_async_copy(ice_v, ice_out, loc_sem.at[3])
    store.start()

    left(second)
    left(third)
    some.wait_send()
    some = pltpu.make_async_remote_copy(
        src_ref=out2.at[pl.ds(0, NDEV - 1)], dst_ref=ret.at[pl.ds(0, NDEV - 1)],
        send_sem=r_sem.at[0], recv_sem=r_sem.at[1], device_id=(gx, gy), device_id_type=MESH,
    )
    some.wait_recv()

    def unpack(b, carry):
        t = tgt_s[0, b]
        v = ret[within(t // 32, NDEV)]
        ocean_out[b] = jnp.where(t >= 0, v, 0.0)
        return carry

    lax.fori_loop(0, NDEV, unpack, 0, unroll=4)
    store.wait()
    some.wait_send()


def local(ice_state, thickness, concentration, cat_mask, forcing, ice_target):
    blocks = forcing.reshape(NDEV, 4, 8, 128).transpose(0, 2, 1, 3).reshape(NDEV, 32, 128)
    hbm = pl.BlockSpec(memory_space=pltpu.HBM)
    vmem, dma = pltpu.VMEM, pltpu.SemaphoreType.DMA

    def v(*shape, dtype=F32):
        return vmem(shape, dtype)

    raw = (5, NLON, 1024)
    rows = W * 8
    ice, ocean = pl.pallas_call(
        kernel,
        out_shape=(
            jax.ShapeDtypeStruct(raw, F32),
            jax.ShapeDtypeStruct((NDEV, 16, 128), F32),
        ),
        in_specs=[hbm] * 6,
        out_specs=(pl.BlockSpec(memory_space=pl.ANY), pl.BlockSpec(memory_space=vmem)),
        scratch_shapes=[
            pltpu.SMEM((1, 128), jnp.int32), v(1, 128, dtype=jnp.int32),
            v(8, 128, dtype=jnp.int32), pltpu.SMEM((8, 128), jnp.int32),
            v(8, 128, dtype=jnp.int32), pltpu.SMEM((8, 128), jnp.int32),
            v(*raw), v(*raw), v(*raw), v(*raw, dtype=jnp.int32),
            v(NDEV, 32, 128), v(NDEV, RB, 128), v(NDEV, RB, 128), v(NDEV, 128),
            v(6, rows, 128), v(3, rows, 128), v(4, rows, 128),
            v(5, W, 128), v(3, W, 128), v(4, W, 128),
            v(16, 128), v(3, 16, 128), v(8, 128), v(3, 8, 128), v(16, 128), v(3, 16, 128), v(7, W, 128),
            v(2, 5, OWN, 128), v(2, 5, OWN, 128),
            v(2, NLON * 8, 128), v(32, 16, 128), v(NDEV, 16, 128), v(NDEV, 16, 128), v(*raw),
            dma((7,)), dma((4,)), dma((2,)), dma((2,)), dma((17,)), dma((17,)),
        ],
        compiler_params=pltpu.CompilerParams(
            collective_id=0, has_side_effects=True, vmem_limit_bytes=58 * 2**20
        ),
        name="ice",
    )(ice_target.reshape(1, NDEV), ice_state[0], thickness[0], concentration[0], cat_mask[0], blocks)
    ocean = ocean.reshape(NDEV, 8, 2, 128).transpose(0, 2, 1, 3).reshape(NDEV, 2, 1024)
    return ice[None], ocean


def solution(mesh):
    lead = ("gx", "gy")
    four, three = P(lead, None, None, None), P(lead, None, None)
    return jax.shard_map(
        local,
        mesh=mesh,
        in_specs=(four, four, four, four, three, P(lead)),
        out_specs=(four, three),
        check_vma=False,
    )
```

```python
import jax
import jax.numpy as jnp
from jax import lax
from jax.experimental import pallas as pl
from jax.experimental.pallas import tpu as pltpu
from jax.sharding import PartitionSpec as P

MESH = pl.DeviceIdType.MESH
SUB = 8
HALF = 4
H = 2 * HALF
NLON = 32
W = NLON + 2 * H
OWN = H * 8
END = OWN + NLON * 8
NDEV = 128
RB = 33
PER = W // 8
F32 = jnp.float32


def at(d):
    return (d // 4, d % 4)


def rot(x, shift, axis):
    return pltpu.roll(x, shift % x.shape[axis], axis)


def iota(shape, axis):
    return lax.broadcasted_iota(jnp.int32, shape, axis)


def within(i, count):
    return jnp.minimum(jnp.maximum(i, 0), count - 1)


def root(x):
    return x * lax.rsqrt(jnp.maximum(x, 1e-30))


def stress(due_x, dun_y, due_y, dun_x, ss, sd, sh, strength):
    plus = due_x + dun_y
    minus = due_x - dun_y
    cross = due_y + dun_x
    deform = 0.5 * root(plus * plus + 0.25 * (minus * minus + cross * cross)) + 0.05
    ss = strength * (ss + 0.25 * plus - 0.5 * deform) / (strength + 0.5 * deform)
    scaled = strength / (strength + 2.0 * deform)
    sd = scaled * (sd + 0.25 * minus)
    sh = scaled * (sh + 0.125 * cross)
    return ss, sd, sh


def momentum(ue, un, dxx_x, dsh_y, dsh_x, dyy_y, uo, vo, wx, wy, cover, mass):
    force_east = 0.25 * dxx_x + 0.5 * dsh_y
    force_north = 0.5 * dsh_x + 0.25 * dyy_y
    a = uo - ue
    b = vo - un
    drag = cover * root(a * a + b * b)
    inv = 1.0 / (mass + 0.5 * drag)
    tenth = 0.1 * mass
    east = mass * ue + 0.5 * (force_east + cover * wx + drag * uo) + tenth * un
    north = mass * un + 0.5 * (force_north + cover * wy + drag * vo) - tenth * ue
    return east * inv, north * inv


def quads(x0, x1, x2, x3, group):
    low = (group % 2) == 0
    y0 = jnp.where(low, x0, rot(x1, 32, 1))
    y1 = jnp.where(low, rot(x0, -32, 1), x1)
    y2 = jnp.where(low, x2, rot(x3, 32, 1))
    y3 = jnp.where(low, rot(x2, -32, 1), x3)
    low = group < 2
    return (
        jnp.where(low, y0, rot(y2, 64, 1)),
        jnp.where(low, y1, rot(y3, 64, 1)),
        jnp.where(low, rot(y0, -64, 1), y2),
        jnp.where(low, rot(y1, -64, 1), y3),
    )


def kernel(
    tgt, state, thick, conc, mask, forc, ice_out, ret,
    tgt_v, idx_v, idx_s, dst_v, dst_s,
    r_state, r_thick, r_conc, r_mask, fv, outb, arr, tagm,
    st, sc, fo, sp, spc, spf,
    t7, p7, t4, p4, t5, p5, ext, edge, h5, edge7, h7,
    dr, sb, out2, ice_v,
    in_sem, loc_sem, a_sem, r_sem, x_send, x_recv,
):
    gx, gy = lax.axis_index("gx"), lax.axis_index("gy")
    me = gx * 4 + gy
    y, z, core, x = gx // 8, (gx // 2) % 4, gx % 2, gy

    def flipped(bit, by):
        return 1 - bit if by else bit

    low = []
    for n in range(16):
        n = (n * 11) % 16
        px = 2 * flipped(x // 2, (n // 2) % 2) + flipped(x % 2, n % 2)
        low.append((2 * flipped(z % 2, (n // 8) % 2) + flipped(core, (n // 4) % 2), px))

    def for_peers(act):
        def turn(q, carry):
            high = []
            for r in range(8):
                m = (q + r) % 8
                z1 = (z // 2 + m) % 2
                y0 = (y + m // 2) % 2
                y1 = (y // 2 + m // 4) % 2
                high.append(8 * (2 * y1 + y0) + 4 * z1)
            for n in range(16):
                a, b = high[(3 * n) % 8] + low[n][0], low[n][1]
                if n:
                    act(a, b)
                else:
                    pl.when(q != 0)(lambda a=a, b=b: act(a, b))
            return carry

        lax.fori_loop(0, 8, turn, 0)

    loads = [
        pltpu.make_async_copy(src, dst, in_sem.at[i])
        for i, (src, dst) in enumerate(
            [(tgt, tgt_v), (thick, r_thick), (conc, r_conc), (mask, r_mask), (state, r_state), (forc, fv)]
        )
    ]
    for load in loads:
        load.start()

    barrier = pltpu.get_barrier_semaphore()

    def greet(a, b):
        pl.semaphore_signal(barrier, inc=1, device_id=(a, b), device_id_type=MESH)

    for b in range(1, 4):
        greet(gx, (gy + b) % 4)

    def greet_all(k, carry):
        a = (gx + k) % 32
        for b in range(4):
            greet(a, b)
        return carry

    lax.fori_loop(1, 32, greet_all, 0)

    square = (NDEV, NDEV)
    lane_sq, sub_sq = iota(square, 1), iota(square, 0)
    loads[0].wait()
    row = jnp.broadcast_to(tgt_v[...].astype(F32), square)
    column = jnp.sum(jnp.where(lane_sq == sub_sq, row, 0.0), axis=1, keepdims=True)
    target = jnp.broadcast_to(column, square).astype(jnp.int32)
    hit = (target >= 0) & (target // 32 == lane_sq)
    listed = jnp.sum(jnp.where(hit, sub_sq.astype(F32), 0.0), axis=0, keepdims=True)
    place = jnp.sum(jnp.where(hit, (target % 32 + 1).astype(F32), 0.0), axis=0, keepdims=True) - 1.0
    idx_v[0:1, :] = listed.astype(jnp.int32)
    idx_v[1:2, :] = place.astype(jnp.int32)
    to_smem = pltpu.make_async_copy(idx_v, idx_s, loc_sem.at[0])
    to_smem.start()

    for load in loads[1:5]:
        load.wait()

    def relay(n, carry):
        lb, chunk = n // 8, n % 8
        rows, lanes = pl.ds(pl.multiple_of(lb * 8, 8), 8), pl.ds(pl.multiple_of(chunk * 128, 128), 128)
        dst = pl.ds(OWN + lb * 64 + chunk, 8, stride=8)
        cover = jnp.zeros((8, 128), F32)
        volume = jnp.zeros((8, 128), F32)
        for cat in range(5):
            part = r_conc[cat, rows, lanes] * r_mask[cat, rows, lanes].astype(F32)
            cover = cover + part
            volume = volume + r_thick[cat, rows, lanes] * part
        sc[0, dst, :] = cover
        sc[1, dst, :] = volume
        for ch in range(5):
            st[ch, dst, :] = r_state[ch, rows, lanes]
        return carry

    lax.fori_loop(0, 32, relay, 0)

    lane8, sub8 = iota((8, 128), 1), iota((8, 128), 0)

    def turned(v):
        for bit in (1, 2, 4):
            v = jnp.where((sub8 // bit) % 2 == 1, rot(v, bit, 0), rot(v, -bit, 0))
        for bit in (1, 2, 4):
            v = jnp.where((lane8 // bit) % 2 == 1, rot(v, bit, 1), rot(v, -bit, 1))
        return v

    def tops(dst, parts):
        full = []
        for n, (src, ch, sign) in enumerate([part for part in parts for _ in range(4)]):
            g, q = n % 4, n % 16
            v = rot(src[ch, pl.ds(OWN + (24 - 8 * g) * 8 + 7, 8, stride=8), :], 8 * q + 8, 1)
            v = v if sign > 0 else -v
            if q == 0:
                full.append(v)
            else:
                full[-1] = jnp.where(lane8 // 8 == q, v, full[-1])
        for n, v in enumerate(full):
            dst[8 * n : 8 * n + 8, :] = turned(v)

    def beyond(packed, count):
        for ch in range(count):
            for k in range(6):
                source, g = (1, 3) if k == 0 else (2, 0) if k == 5 else (0, k - 1)
                n = ch * 4 + g
                v = packed[source, 8 * (n // 16) : 8 * (n // 16) + 8, :]
                ext[ch, 8 * k : 8 * k + 8, :] = rot(v, 120 - 8 * (n % 16), 1)

    def strip_own(dst, src, count, fresh=None):
        for ch in range(count):
            for b in range(PER):
                v = rot(src[ch, pl.ds(b * 8 + 7, 8, stride=8 * PER), :], -H, 1)
                if fresh is not None:
                    lon = sub8 * PER + b
                    v = jnp.where((lon < H) | (lon >= H + NLON), v, dst[ch, b * 8 : b * 8 + 8, :])
                dst[ch, b * 8 : b * 8 + 8, :] = v

    def strip_far(dst, first, count):
        for ch in range(count):
            for b in range(PER):
                where = slice(b * 8, b * 8 + 8)
                far = ext[first + ch, pl.ds(b, 8, stride=PER), :]
                dst[ch, where, :] = jnp.where(lane8 < 128 - H, dst[ch, where, :], far)

    def merge():
        for ch in range(5):
            for b in range(PER):
                where = pl.ds(b * 8 + 7, 8, stride=8 * PER)
                new = rot(sp[ch, b * 8 : b * 8 + 8, :], H, 1)
                st[ch, where, :] = jnp.where(lane8 >= 128 - H, new, st[ch, where, :])

    state_parts = [(st, 0, -1), (st, 1, -1), (st, 2, 1), (st, 3, 1), (st, 4, 1)]
    tops(t7, state_parts + [(sc, 0, 1), (sc, 1, 1)])
    for ch in range(7):
        src, n = (st, ch) if ch < 5 else (sc, ch - 5)
        edge7[0, ch] = src[n, OWN : 2 * OWN, :]
        edge7[1, ch] = src[n, END - OWN : END, :]

    west, east = (me + NDEV - 1) % NDEV, (me + 1) % NDEV
    over, over_east, over_west = NDEV - 1 - me, (NDEV - me) % NDEV, (2 * NDEV - 2 - me) % NDEV

    def remote(src, dst, d, i):
        return pltpu.make_async_remote_copy(
            src_ref=src, dst_ref=dst, send_sem=x_send.at[i], recv_sem=x_recv.at[i],
            device_id=at(d), device_id_type=MESH,
        )

    def beside(to_west, to_east, at_west, at_east, i):
        return [
            (remote(to_west, at_east, west, i), None, None),
            (remote(to_east, at_west, east, i + 1), None, None),
        ]

    def halo(ref, count, i):
        def part(lon):
            return ref.at[pl.ds(0, count), pl.ds(lon * 8, OWN)]

        return beside(part(H), part(NLON), part(0), part(H + NLON), i)

    def across(t, p, i):
        parts = []
        for n, d in enumerate([over, over_east, over_west]):
            here = pltpu.make_async_copy(t, p.at[n], x_recv.at[i + n]) if n else None
            parts.append((remote(t, p.at[n], d, i + n), here, d))
        return parts

    def start(copies):
        for copy, here, d in copies:
            if here is None:
                copy.start()
            else:
                pl.when(d != me)(copy.start)
                pl.when(d == me)(here.start)

    def landed(copies):
        for copy, _, _ in copies:
            copy.wait_recv()

    def left(copies):
        for copy, here, d in copies:
            if here is None:
                copy.wait_send()
            else:
                pl.when(d != me)(copy.wait_send)

    first = beside(edge7.at[0], edge7.at[1], h7.at[0], h7.at[1], 0) + across(t7, p7, 4)
    second = halo(fo, 4, 7) + across(t4, p4, 9)
    third = beside(edge.at[0], edge.at[1], h5.at[0], h5.at[1], 12) + across(t5, p5, 14)

    to_smem.wait()
    loads[5].wait()

    def pack(c, carry):
        outb[c, 0:32, :] = fv[within(idx_s[0, c], NDEV)]
        outb[c, 32:33, :] = jnp.full((1, 128), idx_s[1, c].astype(F32))
        return carry

    lax.fori_loop(0, NDEV, pack, 0, unroll=4)

    pl.semaphore_wait(barrier, NDEV - 1)

    def send(a, b):
        pltpu.make_async_remote_copy(
            src_ref=outb.at[a * 4 + b], dst_ref=arr.at[me], send_sem=a_sem.at[0], recv_sem=a_sem.at[1],
            device_id=(a, b), device_id_type=MESH,
        ).start()

    for_peers(send)
    start(first)
    own_block = pltpu.make_async_copy(outb.at[me], arr.at[me], loc_sem.at[1])
    own_block.start()

    def get(ref, ch, r, n, shift=0):
        return ref[ch, pl.ds(pl.multiple_of(r, 8) + shift, 8 * n), :]

    def put(ref, ch, r, n, v):
        ref[ch, pl.ds(pl.multiple_of(r, 8), 8 * n), :] = v

    def diff_lon(ref, ch, r, n):
        return get(ref, ch, r + 8, n) - get(ref, ch, r - 8, n)

    def diff_lat(ref, ch, r, n):
        v = get(ref, ch, r, n)
        lane, sub = iota(v.shape, 1), iota(v.shape, 0) % 8
        up = jnp.where(lane == 0, get(ref, ch, r, n, 1), v)
        down = jnp.where(sub == 0, 0.0, get(ref, ch, r, n, -1))
        down = jnp.where(lane == 127, down, v)
        return rot(up, -1, 1) - rot(down, 1, 1)

    def strip_lon(v):
        upper = jnp.concatenate([v[1:], rot(v[:1], -1, 1)], axis=0)
        lower = jnp.concatenate([rot(v[-1:], 1, 1), v[:-1]], axis=0)
        return upper - lower

    def strip_lat(v):
        return rot(v, -1, 2) - rot(v, 1, 2)

    def whole(ref, ch):
        return ref[ch].reshape(PER, 8, 128)

    def keep(ref, ch, v):
        ref[ch] = v.reshape(PER * 8, 128)

    def sweep(lo, hi, body):
        def step(i, carry):
            body((lo + 4 * i) * 8, 4)
            return carry

        count = (hi - lo) // 4
        if count:
            lax.fori_loop(0, count, step, 0)
        if (hi - lo) % 4:
            body((lo + 4 * count) * 8, (hi - lo) % 4)

    def strength_of(volume, cover):
        return volume * jnp.exp(-2.0 * (1.0 - cover))

    def stress_at(r, n):
        new = stress(
            diff_lon(st, 0, r, n), diff_lat(st, 1, r, n), diff_lat(st, 0, r, n), diff_lon(st, 1, r, n),
            get(st, 2, r, n), get(st, 3, r, n), get(st, 4, r, n), get(sc, 2, r, n),
        )
        for ch in range(3):
            put(st, 2 + ch, r, n, new[ch])
        put(st, 5, r, n, new[0] - new[1])

    def stress_strip():
        ue, un = whole(sp, 0), whole(sp, 1)
        new = stress(
            strip_lon(ue), strip_lat(un), strip_lat(ue), strip_lon(un),
            whole(sp, 2), whole(sp, 3), whole(sp, 4), whole(spc, 2),
        )
        for ch in range(3):
            keep(sp, 2 + ch, new[ch])

    def momentum_at(r, n):
        dxx = diff_lon(st, 2, r, n) + diff_lon(st, 3, r, n)
        new = momentum(
            get(st, 0, r, n), get(st, 1, r, n),
            dxx, diff_lat(st, 4, r, n), diff_lon(st, 4, r, n), diff_lat(st, 5, r, n),
            get(fo, 0, r, n), get(fo, 1, r, n), get(fo, 2, r, n), get(fo, 3, r, n), get(sc, 0, r, n), get(sc, 1, r, n),
        )
        put(st, 0, r, n, new[0])
        put(st, 1, r, n, new[1])

    def momentum_strip():
        ss, sd, sh = whole(sp, 2), whole(sp, 3), whole(sp, 4)
        new = momentum(
            whole(sp, 0), whole(sp, 1), strip_lon(ss + sd), strip_lat(sh), strip_lon(sh), strip_lat(ss - sd),
            whole(spf, 0), whole(spf, 1), whole(spf, 2), whole(spf, 3), whole(spc, 0), whole(spc, 1),
        )
        keep(sp, 0, new[0])
        keep(sp, 1, new[1])

    def statics(r, n):
        cover, volume = get(sc, 0, r, n), get(sc, 1, r, n)
        put(sc, 1, r, n, volume + 0.5)
        put(sc, 2, r, n, strength_of(volume, cover))

    def rims(first_lon, width, body):
        for lon in (first_lon, W - first_lon - width):
            for n in range(0, width, 4):
                body((lon + n) * 8, min(4, width - n))

    def inner(done):
        for m in range(HALF):
            if m or not done:
                sweep(H + 1 + 2 * m, W - H - 1 - 2 * m, stress_at)
            sweep(H + 2 + 2 * m, W - H - 2 - 2 * m, momentum_at)

    def outer(m, carry):
        rims(1 + 2 * m, H, stress_at)
        stress_strip()
        rims(2 + 2 * m, H, momentum_at)
        momentum_strip()
        return carry

    strip_own(sp, st, 5)
    strip_own(spc, sc, 2)
    sweep(H, H + NLON, statics)
    sweep(H + 1, W - H - 1, stress_at)

    own_block.wait()
    some = pltpu.make_async_remote_copy(
        src_ref=outb.at[pl.ds(0, NDEV - 1)], dst_ref=arr.at[pl.ds(0, NDEV - 1)],
        send_sem=a_sem.at[0], recv_sem=a_sem.at[1], device_id=(gx, gy), device_id_type=MESH,
    )
    some.wait_recv()

    def tag(s, carry):
        tagm[pl.ds(s, 1), :] = arr[s, 32:33, :]
        return carry

    lax.fori_loop(0, NDEV, tag, 0, unroll=8)
    tags = tagm[...]
    origin = jnp.sum(jnp.where(tags.astype(jnp.int32) == lane_sq, sub_sq.astype(F32), 0.0), axis=0, keepdims=True)
    back = jnp.sum(jnp.where(sub_sq == lane_sq, tags, 0.0), axis=0, keepdims=True)
    dst_v[0:1, :] = origin.astype(jnp.int32)
    dst_v[1:2, :] = jnp.maximum(back, 0.0).astype(jnp.int32)
    to_smem = pltpu.make_async_copy(dst_v, dst_s, loc_sem.at[2])
    to_smem.start()
    to_smem.wait()

    group8 = lane8 // 32

    def place_rows(chunk, carry):
        sources = [within(dst_s[0, chunk * 4 + j], NDEV) for j in range(4)]
        for ch in range(4):
            rows = quads(*[arr[s, pl.ds(ch, 8, stride=4), :] for s in sources], group8)
            for p in range(4):
                fo[ch, pl.ds(OWN + p * 8 + chunk, 8, stride=32), :] = rows[p]
        return carry

    lax.fori_loop(0, 8, place_rows, 0, unroll=2)
    tops(t4, [(fo, 0, -1), (fo, 1, -1), (fo, 2, -1), (fo, 3, -1)])
    start(second)

    inner(1)

    landed(first)
    for ch in range(7):
        dst, n = (st, ch) if ch < 5 else (sc, ch - 5)
        dst[n, 0:OWN, :] = h7[0, ch]
        dst[n, END:, :] = h7[1, ch]
    beyond(p7, 7)
    strip_own(sp, st, 5, True)
    strip_far(sp, 0, 5)
    strip_own(spc, sc, 2, True)
    strip_far(spc, 5, 2)
    rims(0, H, statics)
    cover, volume = whole(spc, 0), whole(spc, 1)
    keep(spc, 1, volume + 0.5)
    keep(spc, 2, strength_of(volume, cover))
    landed(second)
    beyond(p4, 4)
    strip_own(spf, fo, 4)
    strip_far(spf, 0, 4)

    lax.fori_loop(0, HALF, outer, 0)
    merge()
    tops(t5, state_parts)
    for ch in range(5):
        edge[0, ch] = st[ch, OWN : 2 * OWN, :]
        edge[1, ch] = st[ch, END - OWN : END, :]
    start(third)
    strip_own(sp, st, 5)
    inner(0)

    landed(third)
    for ch in range(5):
        st[ch, 0:OWN, :] = h5[0, ch]
        st[ch, END:, :] = h5[1, ch]
    beyond(p5, 5)
    strip_own(sp, st, 5, True)
    strip_far(sp, 0, 5)

    lax.fori_loop(0, HALF, outer, 0)
    merge()

    def drag(r, n):
        a = get(st, 0, r, n) - get(fo, 0, r, n)
        b = get(st, 1, r, n) - get(fo, 1, r, n)
        rate = get(sc, 0, r, n) * root(a * a + b * b)
        put(dr, 0, r - OWN, n, rate * a)
        put(dr, 1, r - OWN, n, rate * b)

    sweep(H, H + NLON, drag)

    def blocks(chunk, carry):
        for ch in range(2):
            rows = quads(*[dr[ch, pl.ds(p * 8 + chunk, 8, stride=32), :] for p in range(4)], group8)
            for j in range(4):
                sb[chunk * 4 + j, pl.ds(ch, 8, stride=2), :] = rows[j]
        return carry

    lax.fori_loop(0, 8, blocks, 0, unroll=4)

    def give(a, b):
        d = a * 4 + b
        out2[d] = sb[within(dst_s[1, d], 32)]
        pltpu.make_async_remote_copy(
            src_ref=out2.at[d], dst_ref=ret.at[me], send_sem=r_sem.at[0], recv_sem=r_sem.at[1],
            device_id=(a, b), device_id_type=MESH,
        ).start()

    for_peers(give)
    out2[me] = sb[within(dst_s[1, me], 32)]
    own_stress = pltpu.make_async_copy(out2.at[me], ret.at[me], loc_sem.at[1])
    own_stress.start()

    def lay_out(n, carry):
        lb, chunk = n // 8, n % 8
        rows, lanes = pl.ds(pl.multiple_of(lb * 8, 8), 8), pl.ds(pl.multiple_of(chunk * 128, 128), 128)
        for ch in range(5):
            ice_v[ch, rows, lanes] = st[ch, pl.ds(OWN + lb * 64 + chunk, 8, stride=8), :]
        return carry

    lax.fori_loop(0, 32, lay_out, 0)
    store = pltpu.make_async_copy(ice_v, ice_out, loc_sem.at[3])
    store.start()

    left(first)
    left(second)
    left(third)
    some.wait_send()
    some = pltpu.make_async_remote_copy(
        src_ref=out2.at[pl.ds(0, NDEV - 1)], dst_ref=ret.at[pl.ds(0, NDEV - 1)],
        send_sem=r_sem.at[0], recv_sem=r_sem.at[1], device_id=(gx, gy), device_id_type=MESH,
    )
    some.wait_recv()

    own_stress.wait()
    store.wait()
    some.wait_send()


def hand_out(tgt, ice, ret, ice_out, ocean_out, tgt_s, ret_v, ice_v, ocean_v, sem):
    loads = [
        pltpu.make_async_copy(src, dst, sem.at[i])
        for i, (src, dst) in enumerate([(tgt, tgt_s), (ret, ret_v), (ice, ice_v)])
    ]
    for load in loads:
        load.start()
    store = pltpu.make_async_copy(ice_v, ice_out, sem.at[3])
    loads[2].wait()
    store.start()
    loads[0].wait()
    loads[1].wait()

    def unpack(b, carry):
        t = tgt_s[0, b]
        v = ret_v[within(t // 32, NDEV)]
        ocean_v[b] = jnp.where(t >= 0, v, 0.0)
        return carry

    parts = []
    for n in range(4):
        lax.fori_loop(32 * n, 32 * n + 32, unpack, 0, unroll=8)
        part = pl.ds(32 * n, 32)
        parts.append(pltpu.make_async_copy(ocean_v.at[part], ocean_out.at[part], sem.at[4 + n]))
        parts[-1].start()
    store.wait()
    for part in parts:
        part.wait()


def local(ice_state, thickness, concentration, cat_mask, forcing, ice_target):
    blocks = forcing.reshape(NDEV, 4, 8, 128).transpose(0, 2, 1, 3).reshape(NDEV, 32, 128)
    hbm = pl.BlockSpec(memory_space=pl.ANY)
    vmem, dma = pltpu.VMEM, pltpu.SemaphoreType.DMA

    def v(*shape, dtype=F32):
        return vmem(shape, dtype)

    raw = (5, NLON, 1024)
    rows = W * 8
    listed = ice_target.reshape(1, NDEV)
    outs = (jax.ShapeDtypeStruct(raw, F32), jax.ShapeDtypeStruct((NDEV, 16, 128), F32))
    ice, back = pl.pallas_call(
        kernel,
        out_shape=outs,
        in_specs=[hbm] * 6,
        out_specs=(hbm, hbm),
        scratch_shapes=[
            v(1, 128, dtype=jnp.int32),
            v(8, 128, dtype=jnp.int32), pltpu.SMEM((8, 128), jnp.int32),
            v(8, 128, dtype=jnp.int32), pltpu.SMEM((8, 128), jnp.int32),
            v(*raw), v(*raw), v(*raw), v(*raw, dtype=jnp.int32),
            v(NDEV, 32, 128), v(NDEV, RB, 128), v(NDEV, RB, 128), v(NDEV, 128),
            v(6, rows, 128), v(3, rows, 128), v(4, rows, 128),
            v(5, W, 128), v(3, W, 128), v(4, W, 128),
            v(16, 128), v(3, 16, 128), v(8, 128), v(3, 8, 128), v(16, 128), v(3, 16, 128), v(7, W, 128),
            v(2, 5, OWN, 128), v(2, 5, OWN, 128), v(2, 7, OWN, 128), v(2, 7, OWN, 128),
            v(2, NLON * 8, 128), v(32, 16, 128), v(NDEV, 16, 128), v(*raw),
            dma((7,)), dma((4,)), dma((2,)), dma((2,)), dma((17,)), dma((17,)),
        ],
        compiler_params=pltpu.CompilerParams(
            collective_id=0, has_side_effects=True, vmem_limit_bytes=58 * 2**20
        ),
        name="ice",
    )(listed, ice_state[0], thickness[0], concentration[0], cat_mask[0], blocks)
    ice, ocean = pl.pallas_call(
        hand_out,
        out_shape=outs,
        in_specs=[hbm] * 3,
        out_specs=(hbm, hbm),
        scratch_shapes=[
            pltpu.SMEM((1, 128), jnp.int32), v(NDEV, 16, 128), v(*raw), v(NDEV, 16, 128), dma((8,)),
        ],
        compiler_params=pltpu.CompilerParams(vmem_limit_bytes=58 * 2**20),
        name="hand_out",
    )(listed, ice, back)
    ocean = ocean.reshape(NDEV, 8, 2, 128).transpose(0, 2, 1, 3).reshape(NDEV, 2, 1024)
    return ice[None], ocean


def solution(mesh):
    lead = ("gx", "gy")
    four, three = P(lead, None, None, None), P(lead, None, None)
    return jax.shard_map(
        local,
        mesh=mesh,
        in_specs=(four, four, four, four, three, P(lead)),
        out_specs=(four, three),
        check_vma=False,
    )
```

```python
import jax
import jax.numpy as jnp
from jax import lax
from jax.experimental import pallas as pl
from jax.experimental.pallas import tpu as pltpu
from jax.sharding import PartitionSpec as P

MESH = pl.DeviceIdType.MESH
SUB = 8
HALF = 4
H = 2 * HALF
NLON = 32
W = NLON + 2 * H
OWN = H * 8
END = OWN + NLON * 8
NDEV = 128
RB = 33
PER = W // 8
F32 = jnp.float32
BODY = 16


def at(d):
    return (d // 4, d % 4)


def rot(x, shift, axis):
    return pltpu.roll(x, shift % x.shape[axis], axis)


def iota(shape, axis):
    return lax.broadcasted_iota(jnp.int32, shape, axis)


def within(i, count):
    return jnp.minimum(jnp.maximum(i, 0), count - 1)


def root(x):
    return x * lax.rsqrt(jnp.maximum(x, 1e-30))


def stress(due_x, dun_y, due_y, dun_x, ss, sd, sh, strength):
    plus = due_x + dun_y
    minus = due_x - dun_y
    cross = due_y + dun_x
    deform = 0.5 * root(plus * plus + 0.25 * (minus * minus + cross * cross)) + 0.05
    ss = strength * (ss + 0.25 * plus - 0.5 * deform) / (strength + 0.5 * deform)
    scaled = strength / (strength + 2.0 * deform)
    sd = scaled * (sd + 0.25 * minus)
    sh = scaled * (sh + 0.125 * cross)
    return ss, sd, sh


def momentum(ue, un, dxx_x, dsh_y, dsh_x, dyy_y, uo, vo, wx, wy, cover, mass):
    force_east = 0.25 * dxx_x + 0.5 * dsh_y
    force_north = 0.5 * dsh_x + 0.25 * dyy_y
    a = uo - ue
    b = vo - un
    drag = cover * root(a * a + b * b)
    inv = 1.0 / (mass + 0.5 * drag)
    tenth = 0.1 * mass
    east = mass * ue + 0.5 * (force_east + cover * wx + drag * uo) + tenth * un
    north = mass * un + 0.5 * (force_north + cover * wy + drag * vo) - tenth * ue
    return east * inv, north * inv


def quads(x0, x1, x2, x3, group):
    low = (group % 2) == 0
    y0 = jnp.where(low, x0, rot(x1, 32, 1))
    y1 = jnp.where(low, rot(x0, -32, 1), x1)
    y2 = jnp.where(low, x2, rot(x3, 32, 1))
    y3 = jnp.where(low, rot(x2, -32, 1), x3)
    low = group < 2
    return (
        jnp.where(low, y0, rot(y2, 64, 1)),
        jnp.where(low, y1, rot(y3, 64, 1)),
        jnp.where(low, rot(y0, -64, 1), y2),
        jnp.where(low, rot(y1, -64, 1), y3),
    )


def kernel(
    tgt, state, thick, conc, mask, forc, ice_out, ret,
    tgt_v, idx_v, idx_s, dst_v, dst_s,
    r_state, r_thick, r_conc, r_mask, fv, outb, arr, tagm,
    st, sc, fo, sp, spc, spf,
    t7, p7, t4, p4, t5, p5, ext, edge, h5, edge7, h7,
    dr, sb, out2, ice_v,
    in_sem, loc_sem, a_sem, r_sem, x_send, x_recv,
):
    gx, gy = lax.axis_index("gx"), lax.axis_index("gy")
    me = gx * 4 + gy
    y, z, core, x = gx // 8, (gx // 2) % 4, gx % 2, gy

    def flipped(bit, by):
        return 1 - bit if by else bit

    low = []
    for n in range(16):
        n = (n * 11) % 16
        px = 2 * flipped(x // 2, (n // 2) % 2) + flipped(x % 2, n % 2)
        low.append((2 * flipped(z % 2, (n // 8) % 2) + flipped(core, (n // 4) % 2), px))

    def for_peers(act):
        def turn(q, carry):
            high = []
            for r in range(8):
                m = (q + r) % 8
                z1 = (z // 2 + m) % 2
                y0 = (y + m // 2) % 2
                y1 = (y // 2 + m // 4) % 2
                high.append(8 * (2 * y1 + y0) + 4 * z1)
            for n in range(16):
                a, b = high[(3 * n) % 8] + low[n][0], low[n][1]
                if n:
                    act(a, b)
                else:
                    pl.when(q != 0)(lambda a=a, b=b: act(a, b))
            return carry

        lax.fori_loop(0, 8, turn, 0)

    loads = [
        pltpu.make_async_copy(src, dst, in_sem.at[i])
        for i, (src, dst) in enumerate(
            [(tgt, tgt_v), (thick, r_thick), (conc, r_conc), (mask, r_mask), (state, r_state), (forc, fv)]
        )
    ]
    for load in loads:
        load.start()

    barrier = pltpu.get_barrier_semaphore()

    def greet(a, b):
        pl.semaphore_signal(barrier, inc=1, device_id=(a, b), device_id_type=MESH)

    for b in range(1, 4):
        greet(gx, (gy + b) % 4)

    def greet_all(k, carry):
        a = (gx + k) % 32
        for b in range(4):
            greet(a, b)
        return carry

    lax.fori_loop(1, 32, greet_all, 0)

    square = (NDEV, NDEV)
    lane_sq, sub_sq = iota(square, 1), iota(square, 0)
    loads[0].wait()
    row = jnp.broadcast_to(tgt_v[...].astype(F32), square)
    column = jnp.sum(jnp.where(lane_sq == sub_sq, row, 0.0), axis=1, keepdims=True)
    target = jnp.broadcast_to(column, square).astype(jnp.int32)
    hit = (target >= 0) & (target // 32 == lane_sq)
    listed = jnp.sum(jnp.where(hit, sub_sq.astype(F32), 0.0), axis=0, keepdims=True)
    place = jnp.sum(jnp.where(hit, (target % 32 + 1).astype(F32), 0.0), axis=0, keepdims=True) - 1.0
    idx_v[0:1, :] = listed.astype(jnp.int32)
    idx_v[1:2, :] = place.astype(jnp.int32)
    to_smem = pltpu.make_async_copy(idx_v, idx_s, loc_sem.at[0])
    to_smem.start()

    for load in loads[1:5]:
        load.wait()

    def relay(n, carry):
        lb, chunk = n // 8, n % 8
        rows, lanes = pl.ds(pl.multiple_of(lb * 8, 8), 8), pl.ds(pl.multiple_of(chunk * 128, 128), 128)
        dst = pl.ds(OWN + lb * 64 + chunk, 8, stride=8)
        cover = jnp.zeros((8, 128), F32)
        volume = jnp.zeros((8, 128), F32)
        for cat in range(5):
            part = r_conc[cat, rows, lanes] * r_mask[cat, rows, lanes].astype(F32)
            cover = cover + part
            volume = volume + r_thick[cat, rows, lanes] * part
        sc[0, dst, :] = cover
        sc[1, dst, :] = volume
        for ch in range(5):
            st[ch, dst, :] = r_state[ch, rows, lanes]
        return carry

    lax.fori_loop(0, 32, relay, 0)

    lane8, sub8 = iota((8, 128), 1), iota((8, 128), 0)

    def turned(v):
        for bit in (1, 2, 4):
            v = jnp.where((sub8 // bit) % 2 == 1, rot(v, bit, 0), rot(v, -bit, 0))
        for bit in (1, 2, 4):
            v = jnp.where((lane8 // bit) % 2 == 1, rot(v, bit, 1), rot(v, -bit, 1))
        return v

    def tops(dst, parts):
        full = []
        for n, (src, ch, sign) in enumerate([part for part in parts for _ in range(4)]):
            g, q = n % 4, n % 16
            v = rot(src[ch, pl.ds(OWN + (24 - 8 * g) * 8 + 7, 8, stride=8), :], 8 * q + 8, 1)
            v = v if sign > 0 else -v
            if q == 0:
                full.append(v)
            else:
                full[-1] = jnp.where(lane8 // 8 == q, v, full[-1])
        for n, v in enumerate(full):
            dst[8 * n : 8 * n + 8, :] = turned(v)

    def beyond(packed, count):
        for ch in range(count):
            for k in range(6):
                source, g = (1, 3) if k == 0 else (2, 0) if k == 5 else (0, k - 1)
                n = ch * 4 + g
                v = packed[source, 8 * (n // 16) : 8 * (n // 16) + 8, :]
                ext[ch, 8 * k : 8 * k + 8, :] = rot(v, 120 - 8 * (n % 16), 1)

    def strip_own(dst, src, count, fresh=None):
        for ch in range(count):
            for b in range(PER):
                v = rot(src[ch, pl.ds(b * 8 + 7, 8, stride=8 * PER), :], -H, 1)
                if fresh is not None:
                    lon = sub8 * PER + b
                    v = jnp.where((lon < H) | (lon >= H + NLON), v, dst[ch, b * 8 : b * 8 + 8, :])
                dst[ch, b * 8 : b * 8 + 8, :] = v

    def strip_far(dst, first, count):
        for ch in range(count):
            for b in range(PER):
                where = slice(b * 8, b * 8 + 8)
                far = ext[first + ch, pl.ds(b, 8, stride=PER), :]
                dst[ch, where, :] = jnp.where(lane8 < 128 - H, dst[ch, where, :], far)

    def merge():
        for ch in range(5):
            for b in range(PER):
                where = pl.ds(b * 8 + 7, 8, stride=8 * PER)
                new = rot(sp[ch, b * 8 : b * 8 + 8, :], H, 1)
                st[ch, where, :] = jnp.where(lane8 >= 128 - H, new, st[ch, where, :])

    state_parts = [(st, 0, -1), (st, 1, -1), (st, 2, 1), (st, 3, 1), (st, 4, 1)]
    tops(t7, state_parts + [(sc, 0, 1), (sc, 1, 1)])
    for ch in range(7):
        src, n = (st, ch) if ch < 5 else (sc, ch - 5)
        edge7[0, ch] = src[n, OWN : 2 * OWN, :]
        edge7[1, ch] = src[n, END - OWN : END, :]

    west, east = (me + NDEV - 1) % NDEV, (me + 1) % NDEV
    over, over_east, over_west = NDEV - 1 - me, (NDEV - me) % NDEV, (2 * NDEV - 2 - me) % NDEV

    def remote(src, dst, d, i):
        return pltpu.make_async_remote_copy(
            src_ref=src, dst_ref=dst, send_sem=x_send.at[i], recv_sem=x_recv.at[i],
            device_id=at(d), device_id_type=MESH,
        )

    def beside(to_west, to_east, at_west, at_east, i):
        return [
            (remote(to_west, at_east, west, i), None, None),
            (remote(to_east, at_west, east, i + 1), None, None),
        ]

    def halo(ref, count, i):
        def part(lon):
            return ref.at[pl.ds(0, count), pl.ds(lon * 8, OWN)]

        return beside(part(H), part(NLON), part(0), part(H + NLON), i)

    def across(t, p, i):
        parts = []
        for n, d in enumerate([over, over_east, over_west]):
            here = pltpu.make_async_copy(t, p.at[n], x_recv.at[i + n]) if n else None
            parts.append((remote(t, p.at[n], d, i + n), here, d))
        return parts

    def start(copies):
        for copy, here, d in copies:
            if here is None:
                copy.start()
            else:
                pl.when(d != me)(copy.start)
                pl.when(d == me)(here.start)

    def landed(copies):
        for copy, _, _ in copies:
            copy.wait_recv()

    def left(copies):
        for copy, here, d in copies:
            if here is None:
                copy.wait_send()
            else:
                pl.when(d != me)(copy.wait_send)

    first = across(t7, p7, 4) + beside(edge7.at[0], edge7.at[1], h7.at[0], h7.at[1], 0)
    second = across(t4, p4, 9) + halo(fo, 4, 7)
    third = across(t5, p5, 14) + beside(edge.at[0], edge.at[1], h5.at[0], h5.at[1], 12)

    to_smem.wait()
    loads[5].wait()

    def pack(c, carry):
        outb[c, 0:32, :] = fv[within(idx_s[0, c], NDEV)]
        outb[c, 32:33, :] = jnp.full((1, 128), idx_s[1, c].astype(F32))
        return carry

    lax.fori_loop(0, NDEV, pack, 0, unroll=4)

    pl.semaphore_wait(barrier, NDEV - 1)

    def send(a, b):
        pltpu.make_async_remote_copy(
            src_ref=outb.at[a * 4 + b], dst_ref=arr.at[me], send_sem=a_sem.at[0], recv_sem=a_sem.at[1],
            device_id=(a, b), device_id_type=MESH,
        ).start()

    for_peers(send)
    start(first)
    own_block = pltpu.make_async_copy(outb.at[me], arr.at[me], loc_sem.at[1])
    own_block.start()

    def get(ref, ch, r, n, shift=0):
        return ref[ch, pl.ds(pl.multiple_of(r, 8) + shift, 8 * n), :]

    def put(ref, ch, r, n, v):
        ref[ch, pl.ds(pl.multiple_of(r, 8), 8 * n), :] = v

    def diff_lon(ref, ch, r, n):
        return get(ref, ch, r + 8, n) - get(ref, ch, r - 8, n)

    def diff_lat(ref, ch, r, n):
        v = get(ref, ch, r, n)
        lane, sub = iota(v.shape, 1), iota(v.shape, 0) % 8
        up = jnp.where(lane == 0, get(ref, ch, r, n, 1), v)
        down = jnp.where(sub == 0, 0.0, get(ref, ch, r, n, -1))
        down = jnp.where(lane == 127, down, v)
        return rot(up, -1, 1) - rot(down, 1, 1)

    def strip_lon(v):
        upper = jnp.concatenate([v[1:], rot(v[:1], -1, 1)], axis=0)
        lower = jnp.concatenate([rot(v[-1:], 1, 1), v[:-1]], axis=0)
        return upper - lower

    def strip_lat(v):
        return rot(v, -1, 2) - rot(v, 1, 2)

    def whole(ref, ch):
        return ref[ch].reshape(PER, 8, 128)

    def keep(ref, ch, v):
        ref[ch] = v.reshape(PER * 8, 128)

    def sweep(lo, hi, body):
        def step(i, carry):
            body((lo + BODY * i) * 8, BODY)
            return carry

        count = (hi - lo) // BODY
        if count > 1:
            lax.fori_loop(0, count, step, 0)
        elif count:
            body(lo * 8, BODY)
        if (hi - lo) % BODY:
            body((lo + BODY * count) * 8, (hi - lo) % BODY)

    def stress_of(r, n):
        return (
            diff_lon(st, 0, r, n), diff_lat(st, 1, r, n), diff_lat(st, 0, r, n), diff_lon(st, 1, r, n),
            get(st, 2, r, n), get(st, 3, r, n), get(st, 4, r, n), get(sc, 2, r, n),
        )

    def stress_to(r, n, new):
        for ch in range(3):
            put(st, 2 + ch, r, n, new[ch])
        put(st, 5, r, n, new[0] - new[1])

    def stress_at(r, n):
        stress_to(r, n, stress(*stress_of(r, n)))

    def momentum_of(r, n):
        dxx = diff_lon(st, 2, r, n) + diff_lon(st, 3, r, n)
        return (
            get(st, 0, r, n), get(st, 1, r, n),
            dxx, diff_lat(st, 4, r, n), diff_lon(st, 4, r, n), diff_lat(st, 5, r, n),
            get(fo, 0, r, n), get(fo, 1, r, n), get(fo, 2, r, n), get(fo, 3, r, n), get(sc, 0, r, n), get(sc, 1, r, n),
        )

    def momentum_to(r, n, new):
        put(st, 0, r, n, new[0])
        put(st, 1, r, n, new[1])

    def momentum_at(r, n):
        momentum_to(r, n, momentum(*momentum_of(r, n)))

    def stress_of_strip():
        ue, un = whole(sp, 0), whole(sp, 1)
        return (
            strip_lon(ue), strip_lat(un), strip_lat(ue), strip_lon(un),
            whole(sp, 2), whole(sp, 3), whole(sp, 4), whole(spc, 2),
        )

    def momentum_of_strip():
        ss, sd, sh = whole(sp, 2), whole(sp, 3), whole(sp, 4)
        return (
            whole(sp, 0), whole(sp, 1), strip_lon(ss + sd), strip_lat(sh), strip_lon(sh), strip_lat(ss - sd),
            whole(spf, 0), whole(spf, 1), whole(spf, 2), whole(spf, 3), whole(spc, 0), whole(spc, 1),
        )

    def rims(lon, of, of_strip, step, to, channel):
        near, far = lon * 8, (W - lon - H) * 8
        parts = zip(of(near, H), of(far, H), of_strip(), strict=True)
        new = step(*[jnp.concatenate([a, b, c.reshape(PER * 8, 128)], axis=0) for a, b, c in parts])
        to(near, H, [v[0:OWN] for v in new])
        to(far, H, [v[OWN : 2 * OWN] for v in new])
        for n, v in enumerate(new):
            sp[channel + n] = v[2 * OWN :]

    def strength_of(volume, cover):
        return volume * jnp.exp(-2.0 * (1.0 - cover))

    def statics(r, n):
        cover, volume = get(sc, 0, r, n), get(sc, 1, r, n)
        put(sc, 1, r, n, volume + 0.5)
        put(sc, 2, r, n, strength_of(volume, cover))

    def inner(done):
        for m in range(HALF):
            if m or not done:
                sweep(H + 1 + 2 * m, W - H - 1 - 2 * m, stress_at)
            sweep(H + 2 + 2 * m, W - H - 2 - 2 * m, momentum_at)

    def outer(m, carry):
        rims(1 + 2 * m, stress_of, stress_of_strip, stress, stress_to, 2)
        rims(2 + 2 * m, momentum_of, momentum_of_strip, momentum, momentum_to, 0)
        return carry

    strip_own(sp, st, 5)
    strip_own(spc, sc, 2)
    sweep(H, H + NLON, statics)
    sweep(H + 1, W - H - 1, stress_at)

    own_block.wait()
    some = pltpu.make_async_remote_copy(
        src_ref=outb.at[pl.ds(0, NDEV - 1)], dst_ref=arr.at[pl.ds(0, NDEV - 1)],
        send_sem=a_sem.at[0], recv_sem=a_sem.at[1], device_id=(gx, gy), device_id_type=MESH,
    )
    some.wait_recv()

    def tag(s, carry):
        tagm[pl.ds(s, 1), :] = arr[s, 32:33, :]
        return carry

    lax.fori_loop(0, NDEV, tag, 0, unroll=8)
    tags = tagm[...]
    origin = jnp.sum(jnp.where(tags.astype(jnp.int32) == lane_sq, sub_sq.astype(F32), 0.0), axis=0, keepdims=True)
    back = jnp.sum(jnp.where(sub_sq == lane_sq, tags, 0.0), axis=0, keepdims=True)
    dst_v[0:1, :] = origin.astype(jnp.int32)
    dst_v[1:2, :] = jnp.maximum(back, 0.0).astype(jnp.int32)
    to_smem = pltpu.make_async_copy(dst_v, dst_s, loc_sem.at[2])
    to_smem.start()
    to_smem.wait()

    group8 = lane8 // 32

    def place_rows(chunk, carry):
        sources = [within(dst_s[0, chunk * 4 + j], NDEV) for j in range(4)]
        for ch in range(4):
            rows = quads(*[arr[s, pl.ds(ch, 8, stride=4), :] for s in sources], group8)
            for p in range(4):
                fo[ch, pl.ds(OWN + p * 8 + chunk, 8, stride=32), :] = rows[p]
        return carry

    lax.fori_loop(0, 8, place_rows, 0, unroll=2)
    tops(t4, [(fo, 0, -1), (fo, 1, -1), (fo, 2, -1), (fo, 3, -1)])
    start(second)

    inner(1)

    landed(first)
    for ch in range(7):
        dst, n = (st, ch) if ch < 5 else (sc, ch - 5)
        dst[n, 0:OWN, :] = h7[0, ch]
        dst[n, END:, :] = h7[1, ch]
    beyond(p7, 7)
    strip_own(sp, st, 5, True)
    strip_far(sp, 0, 5)
    strip_own(spc, sc, 2, True)
    strip_far(spc, 5, 2)
    statics(0, H)
    statics(END, H)
    cover, volume = whole(spc, 0), whole(spc, 1)
    keep(spc, 1, volume + 0.5)
    keep(spc, 2, strength_of(volume, cover))
    landed(second)
    beyond(p4, 4)
    strip_own(spf, fo, 4)
    strip_far(spf, 0, 4)

    lax.fori_loop(0, HALF, outer, 0)
    merge()
    tops(t5, state_parts)
    for ch in range(5):
        edge[0, ch] = st[ch, OWN : 2 * OWN, :]
        edge[1, ch] = st[ch, END - OWN : END, :]
    start(third)
    strip_own(sp, st, 5)
    inner(0)

    landed(third)
    for ch in range(5):
        st[ch, 0:OWN, :] = h5[0, ch]
        st[ch, END:, :] = h5[1, ch]
    beyond(p5, 5)
    strip_own(sp, st, 5, True)
    strip_far(sp, 0, 5)

    lax.fori_loop(0, HALF, outer, 0)
    merge()

    def drag(r, n):
        a = get(st, 0, r, n) - get(fo, 0, r, n)
        b = get(st, 1, r, n) - get(fo, 1, r, n)
        rate = get(sc, 0, r, n) * root(a * a + b * b)
        put(dr, 0, r - OWN, n, rate * a)
        put(dr, 1, r - OWN, n, rate * b)

    sweep(H, H + NLON, drag)

    def blocks(chunk, carry):
        for ch in range(2):
            rows = quads(*[dr[ch, pl.ds(p * 8 + chunk, 8, stride=32), :] for p in range(4)], group8)
            for j in range(4):
                sb[chunk * 4 + j, pl.ds(ch, 8, stride=2), :] = rows[j]
        return carry

    lax.fori_loop(0, 8, blocks, 0, unroll=4)

    def give(a, b):
        d = a * 4 + b
        out2[d] = sb[within(dst_s[1, d], 32)]
        pltpu.make_async_remote_copy(
            src_ref=out2.at[d], dst_ref=ret.at[me], send_sem=r_sem.at[0], recv_sem=r_sem.at[1],
            device_id=(a, b), device_id_type=MESH,
        ).start()

    for_peers(give)
    out2[me] = sb[within(dst_s[1, me], 32)]
    own_stress = pltpu.make_async_copy(out2.at[me], ret.at[me], loc_sem.at[1])
    own_stress.start()

    def lay_out(n, carry):
        lb, chunk = n // 8, n % 8
        rows, lanes = pl.ds(pl.multiple_of(lb * 8, 8), 8), pl.ds(pl.multiple_of(chunk * 128, 128), 128)
        for ch in range(5):
            ice_v[ch, rows, lanes] = st[ch, pl.ds(OWN + lb * 64 + chunk, 8, stride=8), :]
        return carry

    lax.fori_loop(0, 32, lay_out, 0)
    store = pltpu.make_async_copy(ice_v, ice_out, loc_sem.at[3])
    store.start()

    left(first)
    left(second)
    left(third)
    some.wait_send()
    some = pltpu.make_async_remote_copy(
        src_ref=out2.at[pl.ds(0, NDEV - 1)], dst_ref=ret.at[pl.ds(0, NDEV - 1)],
        send_sem=r_sem.at[0], recv_sem=r_sem.at[1], device_id=(gx, gy), device_id_type=MESH,
    )
    some.wait_recv()

    own_stress.wait()
    store.wait()
    some.wait_send()


def hand_out(tgt, ice, ret, ice_out, ocean_out, tgt_s, ret_v, ice_v, ocean_v, sem):
    loads = [
        pltpu.make_async_copy(src, dst, sem.at[i])
        for i, (src, dst) in enumerate([(tgt, tgt_s), (ret, ret_v), (ice, ice_v)])
    ]
    for load in loads:
        load.start()
    store = pltpu.make_async_copy(ice_v, ice_out, sem.at[3])
    loads[2].wait()
    store.start()
    loads[0].wait()
    loads[1].wait()

    def unpack(b, carry):
        t = tgt_s[0, b]
        v = ret_v[within(t // 32, NDEV)]
        ocean_v[b] = jnp.where(t >= 0, v, 0.0)
        return carry

    parts = []
    for n in range(4):
        lax.fori_loop(32 * n, 32 * n + 32, unpack, 0, unroll=8)
        part = pl.ds(32 * n, 32)
        parts.append(pltpu.make_async_copy(ocean_v.at[part], ocean_out.at[part], sem.at[4 + n]))
        parts[-1].start()
    store.wait()
    for part in parts:
        part.wait()


def local(ice_state, thickness, concentration, cat_mask, forcing, ice_target):
    blocks = forcing.reshape(NDEV, 4, 8, 128).transpose(0, 2, 1, 3).reshape(NDEV, 32, 128)
    hbm = pl.BlockSpec(memory_space=pl.ANY)
    vmem, dma = pltpu.VMEM, pltpu.SemaphoreType.DMA

    def v(*shape, dtype=F32):
        return vmem(shape, dtype)

    raw = (5, NLON, 1024)
    rows = W * 8
    listed = ice_target.reshape(1, NDEV)
    outs = (jax.ShapeDtypeStruct(raw, F32), jax.ShapeDtypeStruct((NDEV, 16, 128), F32))
    ice, back = pl.pallas_call(
        kernel,
        out_shape=outs,
        in_specs=[hbm] * 6,
        out_specs=(hbm, hbm),
        scratch_shapes=[
            v(1, 128, dtype=jnp.int32),
            v(8, 128, dtype=jnp.int32), pltpu.SMEM((8, 128), jnp.int32),
            v(8, 128, dtype=jnp.int32), pltpu.SMEM((8, 128), jnp.int32),
            v(*raw), v(*raw), v(*raw), v(*raw, dtype=jnp.int32),
            v(NDEV, 32, 128), v(NDEV, RB, 128), v(NDEV, RB, 128), v(NDEV, 128),
            v(6, rows, 128), v(3, rows, 128), v(4, rows, 128),
            v(5, W, 128), v(3, W, 128), v(4, W, 128),
            v(16, 128), v(3, 16, 128), v(8, 128), v(3, 8, 128), v(16, 128), v(3, 16, 128), v(7, W, 128),
            v(2, 5, OWN, 128), v(2, 5, OWN, 128), v(2, 7, OWN, 128), v(2, 7, OWN, 128),
            v(2, NLON * 8, 128), v(32, 16, 128), v(NDEV, 16, 128), v(*raw),
            dma((7,)), dma((4,)), dma((2,)), dma((2,)), dma((17,)), dma((17,)),
        ],
        compiler_params=pltpu.CompilerParams(
            collective_id=0, has_side_effects=True, vmem_limit_bytes=58 * 2**20
        ),
        name="ice",
    )(listed, ice_state[0], thickness[0], concentration[0], cat_mask[0], blocks)
    ice, ocean = pl.pallas_call(
        hand_out,
        out_shape=outs,
        in_specs=[hbm] * 3,
        out_specs=(hbm, hbm),
        scratch_shapes=[
            pltpu.SMEM((1, 128), jnp.int32), v(NDEV, 16, 128), v(*raw), v(NDEV, 16, 128), dma((8,)),
        ],
        compiler_params=pltpu.CompilerParams(vmem_limit_bytes=58 * 2**20),
        name="hand_out",
    )(listed, ice, back)
    ocean = ocean.reshape(NDEV, 8, 2, 128).transpose(0, 2, 1, 3).reshape(NDEV, 2, 1024)
    return ice[None], ocean


def solution(mesh):
    lead = ("gx", "gy")
    four, three = P(lead, None, None, None), P(lead, None, None)
    return jax.shard_map(
        local,
        mesh=mesh,
        in_specs=(four, four, four, four, three, P(lead)),
        out_specs=(four, three),
        check_vma=False,
    )
```

```python
import jax
import jax.numpy as jnp
from jax import lax
from jax.experimental import pallas as pl
from jax.experimental.pallas import tpu as pltpu
from jax.sharding import PartitionSpec as P

MESH = pl.DeviceIdType.MESH
SUB = 8
HALF = 4
H = 2 * HALF
NLON = 32
W = NLON + 2 * H
OWN = H * 8
END = OWN + NLON * 8
NDEV = 128
RB = 33
PER = W // 8
F32 = jnp.float32
BODY = 16


def spread():
    hops = (0, 1, 2, 1)
    ways = [(n * 37) % NDEV for n in range(1, NDEV)]
    return sorted(ways, key=lambda k: -(hops[k % 4] + hops[k // 8 % 4] + hops[k // 32]))


ORDER = spread()


def at(d):
    return (d // 4, d % 4)


def rot(x, shift, axis):
    return pltpu.roll(x, shift % x.shape[axis], axis)


def iota(shape, axis):
    return lax.broadcasted_iota(jnp.int32, shape, axis)


def within(i, count):
    return jnp.minimum(jnp.maximum(i, 0), count - 1)


def root(x):
    return x * lax.rsqrt(jnp.maximum(x, 1e-30))


def stress(due_x, dun_y, due_y, dun_x, ss, sd, sh, strength):
    plus = due_x + dun_y
    minus = due_x - dun_y
    cross = due_y + dun_x
    deform = 0.5 * root(plus * plus + 0.25 * (minus * minus + cross * cross)) + 0.05
    ss = strength * (ss + 0.25 * plus - 0.5 * deform) / (strength + 0.5 * deform)
    scaled = strength / (strength + 2.0 * deform)
    sd = scaled * (sd + 0.25 * minus)
    sh = scaled * (sh + 0.125 * cross)
    return ss, sd, sh


def momentum(ue, un, dxx_x, dsh_y, dsh_x, dyy_y, uo, vo, wx, wy, cover, mass):
    force_east = 0.25 * dxx_x + 0.5 * dsh_y
    force_north = 0.5 * dsh_x + 0.25 * dyy_y
    a = uo - ue
    b = vo - un
    drag = cover * root(a * a + b * b)
    inv = 1.0 / (mass + 0.5 * drag)
    tenth = 0.1 * mass
    east = mass * ue + 0.5 * (force_east + cover * wx + drag * uo) + tenth * un
    north = mass * un + 0.5 * (force_north + cover * wy + drag * vo) - tenth * ue
    return east * inv, north * inv


def quads(x0, x1, x2, x3, group):
    low = (group % 2) == 0
    y0 = jnp.where(low, x0, rot(x1, 32, 1))
    y1 = jnp.where(low, rot(x0, -32, 1), x1)
    y2 = jnp.where(low, x2, rot(x3, 32, 1))
    y3 = jnp.where(low, rot(x2, -32, 1), x3)
    low = group < 2
    return (
        jnp.where(low, y0, rot(y2, 64, 1)),
        jnp.where(low, y1, rot(y3, 64, 1)),
        jnp.where(low, rot(y0, -64, 1), y2),
        jnp.where(low, rot(y1, -64, 1), y3),
    )


def kernel(
    tgt, state, thick, conc, mask, forc, ice_out, ret,
    tgt_v, idx_v, idx_s, dst_v, dst_s,
    r_state, r_thick, r_conc, r_mask, fv, outb, arr, tagm,
    st, sc, fo, sp, spc, spf,
    t7, p7, t4, p4, t5, p5, ext, edge, h5, edge7, h7,
    dr, sb, out2, ice_v,
    in_sem, loc_sem, a_sem, r_sem, x_send, x_recv,
):
    gx, gy = lax.axis_index("gx"), lax.axis_index("gy")
    me = gx * 4 + gy
    y, z, core, x = gx // 8, (gx // 2) % 4, gx % 2, gy

    def flipped(bit, by):
        return 1 - bit if by else bit

    xs = [2 * flipped(x // 2, n // 2) + flipped(x % 2, n % 2) for n in range(4)]
    zs = [4 * flipped(z // 2, n // 2) + 2 * flipped(z % 2, n % 2) for n in range(4)]
    ys = [16 * flipped(y // 2, n // 2) + 8 * flipped(y % 2, n % 2) for n in range(4)]
    cs = [core, 1 - core]

    def for_peers(act):
        for k in ORDER:
            act(ys[k // 32] + zs[k // 8 % 4] + cs[k // 4 % 2], xs[k % 4])

    loads = [
        pltpu.make_async_copy(src, dst, in_sem.at[i])
        for i, (src, dst) in enumerate(
            [(tgt, tgt_v), (thick, r_thick), (conc, r_conc), (mask, r_mask), (state, r_state), (forc, fv)]
        )
    ]
    for load in loads:
        load.start()

    barrier = pltpu.get_barrier_semaphore()

    def greet(a, b):
        pl.semaphore_signal(barrier, inc=1, device_id=(a, b), device_id_type=MESH)

    for b in range(1, 4):
        greet(gx, (gy + b) % 4)

    def greet_all(k, carry):
        a = (gx + k) % 32
        for b in range(4):
            greet(a, b)
        return carry

    lax.fori_loop(1, 32, greet_all, 0)

    square = (NDEV, NDEV)
    lane_sq, sub_sq = iota(square, 1), iota(square, 0)
    loads[0].wait()
    row = jnp.broadcast_to(tgt_v[...].astype(F32), square)
    column = jnp.sum(jnp.where(lane_sq == sub_sq, row, 0.0), axis=1, keepdims=True)
    target = jnp.broadcast_to(column, square).astype(jnp.int32)
    hit = (target >= 0) & (target // 32 == lane_sq)
    listed = jnp.sum(jnp.where(hit, sub_sq.astype(F32), 0.0), axis=0, keepdims=True)
    place = jnp.sum(jnp.where(hit, (target % 32 + 1).astype(F32), 0.0), axis=0, keepdims=True) - 1.0
    idx_v[0:1, :] = listed.astype(jnp.int32)
    idx_v[1:2, :] = place.astype(jnp.int32)
    to_smem = pltpu.make_async_copy(idx_v, idx_s, loc_sem.at[0])
    to_smem.start()

    for load in loads[1:5]:
        load.wait()

    def relay(n, carry):
        lb, chunk = n // 8, n % 8
        rows, lanes = pl.ds(pl.multiple_of(lb * 8, 8), 8), pl.ds(pl.multiple_of(chunk * 128, 128), 128)
        dst = pl.ds(OWN + lb * 64 + chunk, 8, stride=8)
        cover = jnp.zeros((8, 128), F32)
        volume = jnp.zeros((8, 128), F32)
        for cat in range(5):
            part = r_conc[cat, rows, lanes] * r_mask[cat, rows, lanes].astype(F32)
            cover = cover + part
            volume = volume + r_thick[cat, rows, lanes] * part
        sc[0, dst, :] = cover
        sc[1, dst, :] = volume
        for ch in range(5):
            st[ch, dst, :] = r_state[ch, rows, lanes]
        return carry

    lax.fori_loop(0, 32, relay, 0)

    lane8, sub8 = iota((8, 128), 1), iota((8, 128), 0)

    def turned(v):
        for bit in (1, 2, 4):
            v = jnp.where((sub8 // bit) % 2 == 1, rot(v, bit, 0), rot(v, -bit, 0))
        for bit in (1, 2, 4):
            v = jnp.where((lane8 // bit) % 2 == 1, rot(v, bit, 1), rot(v, -bit, 1))
        return v

    def tops(dst, parts):
        full = []
        for n, (src, ch, sign) in enumerate([part for part in parts for _ in range(4)]):
            g, q = n % 4, n % 16
            v = rot(src[ch, pl.ds(OWN + (24 - 8 * g) * 8 + 7, 8, stride=8), :], 8 * q + 8, 1)
            v = v if sign > 0 else -v
            if q == 0:
                full.append(v)
            else:
                full[-1] = jnp.where(lane8 // 8 == q, v, full[-1])
        for n, v in enumerate(full):
            dst[8 * n : 8 * n + 8, :] = turned(v)

    def beyond(packed, count):
        for ch in range(count):
            for k in range(6):
                source, g = (1, 3) if k == 0 else (2, 0) if k == 5 else (0, k - 1)
                n = ch * 4 + g
                v = packed[source, 8 * (n // 16) : 8 * (n // 16) + 8, :]
                ext[ch, 8 * k : 8 * k + 8, :] = rot(v, 120 - 8 * (n % 16), 1)

    def strip_own(dst, src, count, fresh=None):
        for ch in range(count):
            for b in range(PER):
                v = rot(src[ch, pl.ds(b * 8 + 7, 8, stride=8 * PER), :], -H, 1)
                if fresh is not None:
                    lon = sub8 * PER + b
                    v = jnp.where((lon < H) | (lon >= H + NLON), v, dst[ch, b * 8 : b * 8 + 8, :])
                dst[ch, b * 8 : b * 8 + 8, :] = v

    def strip_far(dst, first, count):
        for ch in range(count):
            for b in range(PER):
                where = slice(b * 8, b * 8 + 8)
                far = ext[first + ch, pl.ds(b, 8, stride=PER), :]
                dst[ch, where, :] = jnp.where(lane8 < 128 - H, dst[ch, where, :], far)

    def merge():
        for ch in range(5):
            for b in range(PER):
                where = pl.ds(b * 8 + 7, 8, stride=8 * PER)
                new = rot(sp[ch, b * 8 : b * 8 + 8, :], H, 1)
                st[ch, where, :] = jnp.where(lane8 >= 128 - H, new, st[ch, where, :])

    state_parts = [(st, 0, -1), (st, 1, -1), (st, 2, 1), (st, 3, 1), (st, 4, 1)]
    tops(t7, state_parts + [(sc, 0, 1), (sc, 1, 1)])
    for ch in range(7):
        src, n = (st, ch) if ch < 5 else (sc, ch - 5)
        edge7[0, ch] = src[n, OWN : 2 * OWN, :]
        edge7[1, ch] = src[n, END - OWN : END, :]

    west, east = (me + NDEV - 1) % NDEV, (me + 1) % NDEV
    over, over_east, over_west = NDEV - 1 - me, (NDEV - me) % NDEV, (2 * NDEV - 2 - me) % NDEV

    def remote(src, dst, d, i):
        return pltpu.make_async_remote_copy(
            src_ref=src, dst_ref=dst, send_sem=x_send.at[i], recv_sem=x_recv.at[i],
            device_id=at(d), device_id_type=MESH,
        )

    def beside(to_west, to_east, at_west, at_east, i):
        return [
            (remote(to_west, at_east, west, i), None, None),
            (remote(to_east, at_west, east, i + 1), None, None),
        ]

    def halo(ref, count, width, i):
        def part(lon):
            return ref.at[pl.ds(0, count), pl.ds(lon * 8, width * 8)]

        return beside(part(H), part(H + NLON - width), part(H - width), part(H + NLON), i)

    def across(t, p, i):
        parts = []
        for n, d in enumerate([over, over_east, over_west]):
            here = pltpu.make_async_copy(t, p.at[n], x_recv.at[i + n]) if n else None
            parts.append((remote(t, p.at[n], d, i + n), here, d))
        return parts

    def start(copies):
        for copy, here, d in copies:
            if here is None:
                copy.start()
            else:
                pl.when(d != me)(copy.start)
                pl.when(d == me)(here.start)

    def landed(copies):
        for copy, _, _ in copies:
            copy.wait_recv()

    def left(copies):
        for copy, here, d in copies:
            if here is None:
                copy.wait_send()
            else:
                pl.when(d != me)(copy.wait_send)

    first = across(t7, p7, 4) + beside(edge7.at[0], edge7.at[1], h7.at[0], h7.at[1], 0)
    second = across(t4, p4, 9) + halo(fo, 4, H - 2, 7)
    third = across(t5, p5, 14) + beside(edge.at[0], edge.at[1], h5.at[0], h5.at[1], 12)

    to_smem.wait()
    loads[5].wait()

    def pack(c, carry):
        outb[c, 0:32, :] = fv[within(idx_s[0, c], NDEV)]
        outb[c, 32:33, :] = jnp.full((1, 128), idx_s[1, c].astype(F32))
        return carry

    lax.fori_loop(0, NDEV, pack, 0, unroll=4)

    pl.semaphore_wait(barrier, NDEV - 1)

    def send(a, b):
        pltpu.make_async_remote_copy(
            src_ref=outb.at[a * 4 + b], dst_ref=arr.at[me], send_sem=a_sem.at[0], recv_sem=a_sem.at[1],
            device_id=(a, b), device_id_type=MESH,
        ).start()

    for_peers(send)
    start(first)
    own_block = pltpu.make_async_copy(outb.at[me], arr.at[me], loc_sem.at[1])
    own_block.start()

    def get(ref, ch, r, n, shift=0):
        return ref[ch, pl.ds(pl.multiple_of(r, 8) + shift, 8 * n), :]

    def put(ref, ch, r, n, v):
        ref[ch, pl.ds(pl.multiple_of(r, 8), 8 * n), :] = v

    def diff_lon(ref, ch, r, n):
        return get(ref, ch, r + 8, n) - get(ref, ch, r - 8, n)

    def diff_lat(ref, ch, r, n):
        v = get(ref, ch, r, n)
        lane, sub = iota(v.shape, 1), iota(v.shape, 0) % 8
        up = jnp.where(lane == 0, get(ref, ch, r, n, 1), v)
        down = jnp.where(sub == 0, 0.0, get(ref, ch, r, n, -1))
        down = jnp.where(lane == 127, down, v)
        return rot(up, -1, 1) - rot(down, 1, 1)

    def strip_lon(v):
        upper = jnp.concatenate([v[1:], rot(v[:1], -1, 1)], axis=0)
        lower = jnp.concatenate([rot(v[-1:], 1, 1), v[:-1]], axis=0)
        return upper - lower

    def strip_lat(v):
        return rot(v, -1, 2) - rot(v, 1, 2)

    def whole(ref, ch):
        return ref[ch].reshape(PER, 8, 128)

    def keep(ref, ch, v):
        ref[ch] = v.reshape(PER * 8, 128)

    def sweep(lo, hi, body):
        def step(i, carry):
            body((lo + BODY * i) * 8, BODY)
            return carry

        count = (hi - lo) // BODY
        if count > 1:
            lax.fori_loop(0, count, step, 0)
        elif count:
            body(lo * 8, BODY)
        if (hi - lo) % BODY:
            body((lo + BODY * count) * 8, (hi - lo) % BODY)

    def stress_of(r, n):
        return (
            diff_lon(st, 0, r, n), diff_lat(st, 1, r, n), diff_lat(st, 0, r, n), diff_lon(st, 1, r, n),
            get(st, 2, r, n), get(st, 3, r, n), get(st, 4, r, n), get(sc, 2, r, n),
        )

    def stress_to(r, n, new):
        for ch in range(3):
            put(st, 2 + ch, r, n, new[ch])
        put(st, 5, r, n, new[0] - new[1])

    def stress_at(r, n):
        stress_to(r, n, stress(*stress_of(r, n)))

    def momentum_of(r, n):
        dxx = diff_lon(st, 2, r, n) + diff_lon(st, 3, r, n)
        return (
            get(st, 0, r, n), get(st, 1, r, n),
            dxx, diff_lat(st, 4, r, n), diff_lon(st, 4, r, n), diff_lat(st, 5, r, n),
            get(fo, 0, r, n), get(fo, 1, r, n), get(fo, 2, r, n), get(fo, 3, r, n), get(sc, 0, r, n), get(sc, 1, r, n),
        )

    def momentum_to(r, n, new):
        put(st, 0, r, n, new[0])
        put(st, 1, r, n, new[1])

    def momentum_at(r, n):
        momentum_to(r, n, momentum(*momentum_of(r, n)))

    def stress_of_strip():
        ue, un = whole(sp, 0), whole(sp, 1)
        return (
            strip_lon(ue), strip_lat(un), strip_lat(ue), strip_lon(un),
            whole(sp, 2), whole(sp, 3), whole(sp, 4), whole(spc, 2),
        )

    def momentum_of_strip():
        ss, sd, sh = whole(sp, 2), whole(sp, 3), whole(sp, 4)
        return (
            whole(sp, 0), whole(sp, 1), strip_lon(ss + sd), strip_lat(sh), strip_lon(sh), strip_lat(ss - sd),
            whole(spf, 0), whole(spf, 1), whole(spf, 2), whole(spf, 3), whole(spc, 0), whole(spc, 1),
        )

    def rims(lon, of, of_strip, step, to, channel):
        near, far = lon * 8, (W - lon - H) * 8
        parts = zip(of(near, H), of(far, H), of_strip(), strict=True)
        new = step(*[jnp.concatenate([a, b, c.reshape(PER * 8, 128)], axis=0) for a, b, c in parts])
        to(near, H, [v[0:OWN] for v in new])
        to(far, H, [v[OWN : 2 * OWN] for v in new])
        for n, v in enumerate(new):
            sp[channel + n] = v[2 * OWN :]

    def strength_of(volume, cover):
        return volume * jnp.exp(-2.0 * (1.0 - cover))

    def statics(r, n):
        cover, volume = get(sc, 0, r, n), get(sc, 1, r, n)
        put(sc, 1, r, n, volume + 0.5)
        put(sc, 2, r, n, strength_of(volume, cover))

    def inner(done):
        for m in range(HALF):
            if m or not done:
                sweep(H + 1 + 2 * m, W - H - 1 - 2 * m, stress_at)
            sweep(H + 2 + 2 * m, W - H - 2 - 2 * m, momentum_at)

    def outer(m, carry):
        rims(1 + 2 * m, stress_of, stress_of_strip, stress, stress_to, 2)
        rims(2 + 2 * m, momentum_of, momentum_of_strip, momentum, momentum_to, 0)
        return carry

    strip_own(sp, st, 5)
    strip_own(spc, sc, 2)
    sweep(H, H + NLON, statics)
    sweep(H + 1, W - H - 1, stress_at)

    own_block.wait()
    some = pltpu.make_async_remote_copy(
        src_ref=outb.at[pl.ds(0, NDEV - 1)], dst_ref=arr.at[pl.ds(0, NDEV - 1)],
        send_sem=a_sem.at[0], recv_sem=a_sem.at[1], device_id=(gx, gy), device_id_type=MESH,
    )
    some.wait_recv()

    def tag(s, carry):
        tagm[pl.ds(s, 1), :] = arr[s, 32:33, :]
        return carry

    lax.fori_loop(0, NDEV, tag, 0, unroll=8)
    tags = tagm[...]
    origin = jnp.sum(jnp.where(tags.astype(jnp.int32) == lane_sq, sub_sq.astype(F32), 0.0), axis=0, keepdims=True)
    back = jnp.sum(jnp.where(sub_sq == lane_sq, tags, 0.0), axis=0, keepdims=True)
    dst_v[0:1, :] = origin.astype(jnp.int32)
    dst_v[1:2, :] = jnp.maximum(back, 0.0).astype(jnp.int32)
    to_smem = pltpu.make_async_copy(dst_v, dst_s, loc_sem.at[2])
    to_smem.start()
    to_smem.wait()

    group8 = lane8 // 32

    def place_rows(chunk, carry):
        sources = [within(dst_s[0, chunk * 4 + j], NDEV) for j in range(4)]
        for ch in range(4):
            rows = quads(*[arr[s, pl.ds(ch, 8, stride=4), :] for s in sources], group8)
            for p in range(4):
                fo[ch, pl.ds(OWN + p * 8 + chunk, 8, stride=32), :] = rows[p]
        return carry

    place_rows(7, 0)
    tops(t4, [(fo, 0, -1), (fo, 1, -1), (fo, 2, -1), (fo, 3, -1)])
    start(second[:3])
    lax.fori_loop(0, 7, place_rows, 0, unroll=7)
    start(second[3:])

    inner(1)

    landed(first)
    for ch in range(7):
        dst, n = (st, ch) if ch < 5 else (sc, ch - 5)
        dst[n, 0:OWN, :] = h7[0, ch]
        dst[n, END:, :] = h7[1, ch]
    beyond(p7, 7)
    strip_own(sp, st, 5, True)
    strip_far(sp, 0, 5)
    strip_own(spc, sc, 2, True)
    strip_far(spc, 5, 2)
    statics(0, H)
    statics(END, H)
    cover, volume = whole(spc, 0), whole(spc, 1)
    keep(spc, 1, volume + 0.5)
    keep(spc, 2, strength_of(volume, cover))
    landed(second)
    beyond(p4, 4)
    strip_own(spf, fo, 4)
    strip_far(spf, 0, 4)

    lax.fori_loop(0, HALF, outer, 0)
    merge()
    tops(t5, state_parts)
    start(third[:3])
    for ch in range(5):
        edge[0, ch] = st[ch, OWN : 2 * OWN, :]
        edge[1, ch] = st[ch, END - OWN : END, :]
    start(third[3:])
    strip_own(sp, st, 5)
    inner(0)

    landed(third)
    for ch in range(5):
        st[ch, 0:OWN, :] = h5[0, ch]
        st[ch, END:, :] = h5[1, ch]
    beyond(p5, 5)
    strip_own(sp, st, 5, True)
    strip_far(sp, 0, 5)

    lax.fori_loop(0, HALF, outer, 0)
    merge()

    def drag(r, n):
        a = get(st, 0, r, n) - get(fo, 0, r, n)
        b = get(st, 1, r, n) - get(fo, 1, r, n)
        rate = get(sc, 0, r, n) * root(a * a + b * b)
        put(dr, 0, r - OWN, n, rate * a)
        put(dr, 1, r - OWN, n, rate * b)

    sweep(H, H + NLON, drag)

    def blocks(chunk, carry):
        for ch in range(2):
            rows = quads(*[dr[ch, pl.ds(p * 8 + chunk, 8, stride=32), :] for p in range(4)], group8)
            for j in range(4):
                sb[chunk * 4 + j, pl.ds(ch, 8, stride=2), :] = rows[j]
        return carry

    lax.fori_loop(0, 8, blocks, 0, unroll=8)

    def give(a, b):
        d = a * 4 + b
        out2[d] = sb[within(dst_s[1, d], 32)]
        pltpu.make_async_remote_copy(
            src_ref=out2.at[d], dst_ref=ret.at[me], send_sem=r_sem.at[0], recv_sem=r_sem.at[1],
            device_id=(a, b), device_id_type=MESH,
        ).start()

    for_peers(give)
    out2[me] = sb[within(dst_s[1, me], 32)]
    own_stress = pltpu.make_async_copy(out2.at[me], ret.at[me], loc_sem.at[1])
    own_stress.start()

    def lay_out(n, carry):
        lb, chunk = n // 8, n % 8
        rows, lanes = pl.ds(pl.multiple_of(lb * 8, 8), 8), pl.ds(pl.multiple_of(chunk * 128, 128), 128)
        for ch in range(5):
            ice_v[ch, rows, lanes] = st[ch, pl.ds(OWN + lb * 64 + chunk, 8, stride=8), :]
        return carry

    lax.fori_loop(0, 32, lay_out, 0)
    store = pltpu.make_async_copy(ice_v, ice_out, loc_sem.at[3])
    store.start()

    left(first)
    left(second)
    left(third)
    some.wait_send()
    some = pltpu.make_async_remote_copy(
        src_ref=out2.at[pl.ds(0, NDEV - 1)], dst_ref=ret.at[pl.ds(0, NDEV - 1)],
        send_sem=r_sem.at[0], recv_sem=r_sem.at[1], device_id=(gx, gy), device_id_type=MESH,
    )
    some.wait_recv()

    own_stress.wait()
    store.wait()
    some.wait_send()


def hand_out(tgt, ice, ret, ice_out, ocean_out, tgt_s, ret_v, ice_v, ocean_v, sem):
    loads = [
        pltpu.make_async_copy(src, dst, sem.at[i])
        for i, (src, dst) in enumerate([(tgt, tgt_s), (ret, ret_v), (ice, ice_v)])
    ]
    for load in loads:
        load.start()
    store = pltpu.make_async_copy(ice_v, ice_out, sem.at[3])
    loads[2].wait()
    store.start()
    loads[0].wait()
    loads[1].wait()

    def unpack(b, carry):
        t = tgt_s[0, b]
        v = ret_v[within(t // 32, NDEV)]
        ocean_v[b] = jnp.where(t >= 0, v, 0.0)
        return carry

    parts = []
    for n in range(4):
        lax.fori_loop(32 * n, 32 * n + 32, unpack, 0, unroll=8)
        part = pl.ds(32 * n, 32)
        parts.append(pltpu.make_async_copy(ocean_v.at[part], ocean_out.at[part], sem.at[4 + n]))
        parts[-1].start()
    store.wait()
    for part in parts:
        part.wait()


def local(ice_state, thickness, concentration, cat_mask, forcing, ice_target):
    blocks = forcing.reshape(NDEV, 4, 8, 128).transpose(0, 2, 1, 3).reshape(NDEV, 32, 128)
    hbm = pl.BlockSpec(memory_space=pl.ANY)
    vmem, dma = pltpu.VMEM, pltpu.SemaphoreType.DMA

    def v(*shape, dtype=F32):
        return vmem(shape, dtype)

    raw = (5, NLON, 1024)
    rows = W * 8
    listed = ice_target.reshape(1, NDEV)
    outs = (jax.ShapeDtypeStruct(raw, F32), jax.ShapeDtypeStruct((NDEV, 16, 128), F32))
    ice, back = pl.pallas_call(
        kernel,
        out_shape=outs,
        in_specs=[hbm] * 6,
        out_specs=(hbm, hbm),
        scratch_shapes=[
            v(1, 128, dtype=jnp.int32),
            v(8, 128, dtype=jnp.int32), pltpu.SMEM((8, 128), jnp.int32),
            v(8, 128, dtype=jnp.int32), pltpu.SMEM((8, 128), jnp.int32),
            v(*raw), v(*raw), v(*raw), v(*raw, dtype=jnp.int32),
            v(NDEV, 32, 128), v(NDEV, RB, 128), v(NDEV, RB, 128), v(NDEV, 128),
            v(6, rows, 128), v(3, rows, 128), v(4, rows, 128),
            v(5, W, 128), v(3, W, 128), v(4, W, 128),
            v(16, 128), v(3, 16, 128), v(8, 128), v(3, 8, 128), v(16, 128), v(3, 16, 128), v(7, W, 128),
            v(2, 5, OWN, 128), v(2, 5, OWN, 128), v(2, 7, OWN, 128), v(2, 7, OWN, 128),
            v(2, NLON * 8, 128), v(32, 16, 128), v(NDEV, 16, 128), v(*raw),
            dma((7,)), dma((4,)), dma((2,)), dma((2,)), dma((17,)), dma((17,)),
        ],
        compiler_params=pltpu.CompilerParams(
            collective_id=0, has_side_effects=True, vmem_limit_bytes=58 * 2**20
        ),
        name="ice",
    )(listed, ice_state[0], thickness[0], concentration[0], cat_mask[0], blocks)
    ice, ocean = pl.pallas_call(
        hand_out,
        out_shape=outs,
        in_specs=[hbm] * 3,
        out_specs=(hbm, hbm),
        scratch_shapes=[
            pltpu.SMEM((1, 128), jnp.int32), v(NDEV, 16, 128), v(*raw), v(NDEV, 16, 128), dma((8,)),
        ],
        compiler_params=pltpu.CompilerParams(vmem_limit_bytes=58 * 2**20),
        name="hand_out",
    )(listed, ice, back)
    ocean = ocean.reshape(NDEV, 8, 2, 128).transpose(0, 2, 1, 3).reshape(NDEV, 2, 1024)
    return ice[None], ocean


def solution(mesh):
    lead = ("gx", "gy")
    four, three = P(lead, None, None, None), P(lead, None, None)
    return jax.shard_map(
        local,
        mesh=mesh,
        in_specs=(four, four, four, four, three, P(lead)),
        out_specs=(four, three),
        check_vma=False,
    )
```

```python
import jax
import jax.numpy as jnp
from jax import lax
from jax.experimental import pallas as pl
from jax.experimental.pallas import tpu as pltpu
from jax.sharding import PartitionSpec as P

MESH = pl.DeviceIdType.MESH
SUB = 8
HALF = 4
H = 2 * HALF
NLON = 32
W = NLON + 2 * H
OWN = H * 8
END = OWN + NLON * 8
NDEV = 128
RB = 33
PER = W // 8
F32 = jnp.float32
BODY = 16


def spread():
    hops = (0, 1, 2, 1)
    ways = [(n * 53) % NDEV for n in range(1, NDEV)]

    def far(k):
        return 2 * (hops[k % 4] + hops[k // 8 % 4] + hops[k // 32]) + k // 4 % 2

    return sorted(ways, key=far, reverse=True)


ORDER = spread()


def at(d):
    return (d // 4, d % 4)


def rot(x, shift, axis):
    return pltpu.roll(x, shift % x.shape[axis], axis)


def iota(shape, axis):
    return lax.broadcasted_iota(jnp.int32, shape, axis)


def within(i, count):
    return jnp.minimum(jnp.maximum(i, 0), count - 1)


def root(x):
    return x * lax.rsqrt(jnp.maximum(x, 1e-30))


def stress(due_x, dun_y, due_y, dun_x, ss, sd, sh, strength):
    plus = due_x + dun_y
    minus = due_x - dun_y
    cross = due_y + dun_x
    deform = 0.5 * root(plus * plus + 0.25 * (minus * minus + cross * cross)) + 0.05
    ss = strength * (ss + 0.25 * plus - 0.5 * deform) / (strength + 0.5 * deform)
    scaled = strength / (strength + 2.0 * deform)
    sd = scaled * (sd + 0.25 * minus)
    sh = scaled * (sh + 0.125 * cross)
    return ss, sd, sh


def momentum(ue, un, dxx_x, dsh_y, dsh_x, dyy_y, uo, vo, wx, wy, cover, mass):
    force_east = 0.25 * dxx_x + 0.5 * dsh_y
    force_north = 0.5 * dsh_x + 0.25 * dyy_y
    a = uo - ue
    b = vo - un
    drag = cover * root(a * a + b * b)
    inv = 1.0 / (mass + 0.5 * drag)
    tenth = 0.1 * mass
    east = mass * ue + 0.5 * (force_east + cover * wx + drag * uo) + tenth * un
    north = mass * un + 0.5 * (force_north + cover * wy + drag * vo) - tenth * ue
    return east * inv, north * inv


def quads(x0, x1, x2, x3, group):
    low = (group % 2) == 0
    y0 = jnp.where(low, x0, rot(x1, 32, 1))
    y1 = jnp.where(low, rot(x0, -32, 1), x1)
    y2 = jnp.where(low, x2, rot(x3, 32, 1))
    y3 = jnp.where(low, rot(x2, -32, 1), x3)
    low = group < 2
    return (
        jnp.where(low, y0, rot(y2, 64, 1)),
        jnp.where(low, y1, rot(y3, 64, 1)),
        jnp.where(low, rot(y0, -64, 1), y2),
        jnp.where(low, rot(y1, -64, 1), y3),
    )


def kernel(
    tgt, state, thick, conc, mask, forc, ice_out, ret,
    tgt_v, idx_v, idx_s, dst_v, dst_s,
    r_state, r_thick, r_conc, r_mask, fv, outb, arr, tagm,
    st, sc, fo, sp, spc, spf,
    t7, p7, t4, p4, t5, p5, ext, edge, h5, edge7, h7,
    dr, sb, out2, ice_v,
    in_sem, loc_sem, a_sem, r_sem, x_send, x_recv,
):
    gx, gy = lax.axis_index("gx"), lax.axis_index("gy")
    me = gx * 4 + gy
    y, z, core, x = gx // 8, (gx // 2) % 4, gx % 2, gy

    def flipped(bit, by):
        return 1 - bit if by else bit

    xs = [2 * flipped(x // 2, n // 2) + flipped(x % 2, n % 2) for n in range(4)]
    zs = [4 * flipped(z // 2, n // 2) + 2 * flipped(z % 2, n % 2) for n in range(4)]
    ys = [16 * flipped(y // 2, n // 2) + 8 * flipped(y % 2, n % 2) for n in range(4)]
    cs = [core, 1 - core]

    def for_peers(act):
        for k in ORDER:
            act(ys[k // 32] + zs[k // 8 % 4] + cs[k // 4 % 2], xs[k % 4])

    loads = [
        pltpu.make_async_copy(src, dst, in_sem.at[i])
        for i, (src, dst) in enumerate(
            [(tgt, tgt_v), (thick, r_thick), (conc, r_conc), (mask, r_mask), (state, r_state), (forc, fv)]
        )
    ]
    for load in loads:
        load.start()

    barrier = pltpu.get_barrier_semaphore()

    def greet(a, b):
        pl.semaphore_signal(barrier, inc=1, device_id=(a, b), device_id_type=MESH)

    for_peers(greet)

    square = (NDEV, NDEV)
    lane_sq, sub_sq = iota(square, 1), iota(square, 0)
    loads[0].wait()
    row = jnp.broadcast_to(tgt_v[...].astype(F32), square)
    column = jnp.sum(jnp.where(lane_sq == sub_sq, row, 0.0), axis=1, keepdims=True)
    target = jnp.broadcast_to(column, square).astype(jnp.int32)
    hit = (target >= 0) & (target // 32 == lane_sq)
    listed = jnp.sum(jnp.where(hit, sub_sq.astype(F32), 0.0), axis=0, keepdims=True)
    place = jnp.sum(jnp.where(hit, (target % 32 + 1).astype(F32), 0.0), axis=0, keepdims=True) - 1.0
    idx_v[0:1, :] = listed.astype(jnp.int32)
    idx_v[1:2, :] = place.astype(jnp.int32)
    to_smem = pltpu.make_async_copy(idx_v, idx_s, loc_sem.at[0])
    to_smem.start()

    for load in loads[1:5]:
        load.wait()

    def relay(n, carry):
        lb, chunk = n // 8, n % 8
        rows, lanes = pl.ds(pl.multiple_of(lb * 8, 8), 8), pl.ds(pl.multiple_of(chunk * 128, 128), 128)
        dst = pl.ds(OWN + lb * 64 + chunk, 8, stride=8)
        cover = jnp.zeros((8, 128), F32)
        volume = jnp.zeros((8, 128), F32)
        for cat in range(5):
            part = r_conc[cat, rows, lanes] * r_mask[cat, rows, lanes].astype(F32)
            cover = cover + part
            volume = volume + r_thick[cat, rows, lanes] * part
        sc[0, dst, :] = cover
        sc[1, dst, :] = volume
        for ch in range(5):
            st[ch, dst, :] = r_state[ch, rows, lanes]
        return carry

    lax.fori_loop(0, 32, relay, 0)

    lane8, sub8 = iota((8, 128), 1), iota((8, 128), 0)

    def turned(v):
        for bit in (1, 2, 4):
            v = jnp.where((sub8 // bit) % 2 == 1, rot(v, bit, 0), rot(v, -bit, 0))
        for bit in (1, 2, 4):
            v = jnp.where((lane8 // bit) % 2 == 1, rot(v, bit, 1), rot(v, -bit, 1))
        return v

    def tops(dst, parts):
        full = []
        for n, (src, ch, sign) in enumerate([part for part in parts for _ in range(4)]):
            g, q = n % 4, n % 16
            v = rot(src[ch, pl.ds(OWN + (24 - 8 * g) * 8 + 7, 8, stride=8), :], 8 * q + 8, 1)
            v = v if sign > 0 else -v
            if q == 0:
                full.append(v)
            else:
                full[-1] = jnp.where(lane8 // 8 == q, v, full[-1])
        for n, v in enumerate(full):
            dst[8 * n : 8 * n + 8, :] = turned(v)

    def beyond(packed, count):
        for ch in range(count):
            for k in range(6):
                source, g = (1, 3) if k == 0 else (2, 0) if k == 5 else (0, k - 1)
                n = ch * 4 + g
                v = packed[source, 8 * (n // 16) : 8 * (n // 16) + 8, :]
                ext[ch, 8 * k : 8 * k + 8, :] = rot(v, 120 - 8 * (n % 16), 1)

    def strip_own(dst, src, count, fresh=None):
        for ch in range(count):
            for b in range(PER):
                v = rot(src[ch, pl.ds(b * 8 + 7, 8, stride=8 * PER), :], -H, 1)
                if fresh is not None:
                    lon = sub8 * PER + b
                    v = jnp.where((lon < H) | (lon >= H + NLON), v, dst[ch, b * 8 : b * 8 + 8, :])
                dst[ch, b * 8 : b * 8 + 8, :] = v

    def strip_far(dst, first, count):
        for ch in range(count):
            for b in range(PER):
                where = slice(b * 8, b * 8 + 8)
                far = ext[first + ch, pl.ds(b, 8, stride=PER), :]
                dst[ch, where, :] = jnp.where(lane8 < 128 - H, dst[ch, where, :], far)

    def merge():
        for ch in range(5):
            for b in range(PER):
                where = pl.ds(b * 8 + 7, 8, stride=8 * PER)
                new = rot(sp[ch, b * 8 : b * 8 + 8, :], H, 1)
                st[ch, where, :] = jnp.where(lane8 >= 128 - H, new, st[ch, where, :])

    state_parts = [(st, 0, -1), (st, 1, -1), (st, 2, 1), (st, 3, 1), (st, 4, 1)]
    tops(t7, state_parts + [(sc, 0, 1), (sc, 1, 1)])
    for ch in range(7):
        src, n = (st, ch) if ch < 5 else (sc, ch - 5)
        edge7[0, ch] = src[n, OWN : 2 * OWN, :]
        edge7[1, ch] = src[n, END - OWN : END, :]

    west, east = (me + NDEV - 1) % NDEV, (me + 1) % NDEV
    over, over_east, over_west = NDEV - 1 - me, (NDEV - me) % NDEV, (2 * NDEV - 2 - me) % NDEV

    def remote(src, dst, d, i):
        return pltpu.make_async_remote_copy(
            src_ref=src, dst_ref=dst, send_sem=x_send.at[i], recv_sem=x_recv.at[i],
            device_id=at(d), device_id_type=MESH,
        )

    def beside(to_west, to_east, at_west, at_east, i):
        return [
            (remote(to_west, at_east, west, i), None, None),
            (remote(to_east, at_west, east, i + 1), None, None),
        ]

    def halo(ref, count, width, i):
        def part(lon):
            return ref.at[pl.ds(0, count), pl.ds(lon * 8, width * 8)]

        return beside(part(H), part(H + NLON - width), part(H - width), part(H + NLON), i)

    def across(t, p, i):
        parts = []
        for n, d in enumerate([over, over_east, over_west]):
            here = pltpu.make_async_copy(t, p.at[n], x_recv.at[i + n]) if n else None
            parts.append((remote(t, p.at[n], d, i + n), here, d))
        return parts

    def start(copies):
        for copy, here, d in copies:
            if here is None:
                copy.start()
            else:
                pl.when(d != me)(copy.start)
                pl.when(d == me)(here.start)

    def landed(copies):
        for copy, _, _ in copies:
            copy.wait_recv()

    def left(copies):
        for copy, here, d in copies:
            if here is None:
                copy.wait_send()
            else:
                pl.when(d != me)(copy.wait_send)

    first = across(t7, p7, 4) + beside(edge7.at[0], edge7.at[1], h7.at[0], h7.at[1], 0)
    second = across(t4, p4, 9) + halo(fo, 4, H - 2, 7)
    third = across(t5, p5, 14) + beside(edge.at[0], edge.at[1], h5.at[0], h5.at[1], 12)

    to_smem.wait()
    loads[5].wait()

    def pack(c, carry):
        outb[c, 0:32, :] = fv[within(idx_s[0, c], NDEV)]
        outb[c, 32:33, :] = jnp.full((1, 128), idx_s[1, c].astype(F32))
        return carry

    lax.fori_loop(0, NDEV, pack, 0, unroll=4)

    pl.semaphore_wait(barrier, NDEV - 1)

    def send(a, b):
        pltpu.make_async_remote_copy(
            src_ref=outb.at[a * 4 + b], dst_ref=arr.at[me], send_sem=a_sem.at[0], recv_sem=a_sem.at[1],
            device_id=(a, b), device_id_type=MESH,
        ).start()

    for_peers(send)
    start(first)
    own_block = pltpu.make_async_copy(outb.at[me], arr.at[me], loc_sem.at[1])
    own_block.start()

    def get(ref, ch, r, n, shift=0):
        return ref[ch, pl.ds(pl.multiple_of(r, 8) + shift, 8 * n), :]

    def put(ref, ch, r, n, v):
        ref[ch, pl.ds(pl.multiple_of(r, 8), 8 * n), :] = v

    def diff_lon(ref, ch, r, n):
        return get(ref, ch, r + 8, n) - get(ref, ch, r - 8, n)

    def diff_lat(ref, ch, r, n):
        v = get(ref, ch, r, n)
        lane, sub = iota(v.shape, 1), iota(v.shape, 0) % 8
        up = jnp.where(lane == 0, get(ref, ch, r, n, 1), v)
        down = jnp.where(sub == 0, 0.0, get(ref, ch, r, n, -1))
        down = jnp.where(lane == 127, down, v)
        return rot(up, -1, 1) - rot(down, 1, 1)

    def strip_lon(v):
        upper = jnp.concatenate([v[1:], rot(v[:1], -1, 1)], axis=0)
        lower = jnp.concatenate([rot(v[-1:], 1, 1), v[:-1]], axis=0)
        return upper - lower

    def strip_lat(v):
        return rot(v, -1, 2) - rot(v, 1, 2)

    def whole(ref, ch):
        return ref[ch].reshape(PER, 8, 128)

    def keep(ref, ch, v):
        ref[ch] = v.reshape(PER * 8, 128)

    def sweep(lo, hi, body):
        def step(i, carry):
            body((lo + BODY * i) * 8, BODY)
            return carry

        count = (hi - lo) // BODY
        if count > 1:
            lax.fori_loop(0, count, step, 0)
        elif count:
            body(lo * 8, BODY)
        if (hi - lo) % BODY:
            body((lo + BODY * count) * 8, (hi - lo) % BODY)

    def stress_of(r, n):
        return (
            diff_lon(st, 0, r, n), diff_lat(st, 1, r, n), diff_lat(st, 0, r, n), diff_lon(st, 1, r, n),
            get(st, 2, r, n), get(st, 3, r, n), get(st, 4, r, n), get(sc, 2, r, n),
        )

    def stress_to(r, n, new):
        for ch in range(3):
            put(st, 2 + ch, r, n, new[ch])
        put(st, 5, r, n, new[0] - new[1])

    def stress_at(r, n):
        stress_to(r, n, stress(*stress_of(r, n)))

    def momentum_of(r, n):
        dxx = diff_lon(st, 2, r, n) + diff_lon(st, 3, r, n)
        return (
            get(st, 0, r, n), get(st, 1, r, n),
            dxx, diff_lat(st, 4, r, n), diff_lon(st, 4, r, n), diff_lat(st, 5, r, n),
            get(fo, 0, r, n), get(fo, 1, r, n), get(fo, 2, r, n), get(fo, 3, r, n), get(sc, 0, r, n), get(sc, 1, r, n),
        )

    def momentum_to(r, n, new):
        put(st, 0, r, n, new[0])
        put(st, 1, r, n, new[1])

    def momentum_at(r, n):
        momentum_to(r, n, momentum(*momentum_of(r, n)))

    def stress_of_strip():
        ue, un = whole(sp, 0), whole(sp, 1)
        return (
            strip_lon(ue), strip_lat(un), strip_lat(ue), strip_lon(un),
            whole(sp, 2), whole(sp, 3), whole(sp, 4), whole(spc, 2),
        )

    def momentum_of_strip():
        ss, sd, sh = whole(sp, 2), whole(sp, 3), whole(sp, 4)
        return (
            whole(sp, 0), whole(sp, 1), strip_lon(ss + sd), strip_lat(sh), strip_lon(sh), strip_lat(ss - sd),
            whole(spf, 0), whole(spf, 1), whole(spf, 2), whole(spf, 3), whole(spc, 0), whole(spc, 1),
        )

    def rims(lon, of, of_strip, step, to, channel):
        near, far = lon * 8, (W - lon - H) * 8
        parts = zip(of(near, H), of(far, H), of_strip(), strict=True)
        new = step(*[jnp.concatenate([a, b, c.reshape(PER * 8, 128)], axis=0) for a, b, c in parts])
        to(near, H, [v[0:OWN] for v in new])
        to(far, H, [v[OWN : 2 * OWN] for v in new])
        for n, v in enumerate(new):
            sp[channel + n] = v[2 * OWN :]

    def strength_of(volume, cover):
        return volume * jnp.exp(-2.0 * (1.0 - cover))

    def statics(r, n):
        cover, volume = get(sc, 0, r, n), get(sc, 1, r, n)
        put(sc, 1, r, n, volume + 0.5)
        put(sc, 2, r, n, strength_of(volume, cover))

    def inner(done):
        for m in range(HALF):
            if m or not done:
                sweep(H + 1 + 2 * m, W - H - 1 - 2 * m, stress_at)
            sweep(H + 2 + 2 * m, W - H - 2 - 2 * m, momentum_at)

    def outer(m, carry):
        rims(1 + 2 * m, stress_of, stress_of_strip, stress, stress_to, 2)
        rims(2 + 2 * m, momentum_of, momentum_of_strip, momentum, momentum_to, 0)
        return carry

    strip_own(sp, st, 5)
    strip_own(spc, sc, 2)
    sweep(H, H + NLON, statics)
    sweep(H + 1, W - H - 1, stress_at)

    own_block.wait()
    some = pltpu.make_async_remote_copy(
        src_ref=outb.at[pl.ds(0, NDEV - 1)], dst_ref=arr.at[pl.ds(0, NDEV - 1)],
        send_sem=a_sem.at[0], recv_sem=a_sem.at[1], device_id=(gx, gy), device_id_type=MESH,
    )
    some.wait_recv()

    def tag(s, carry):
        tagm[pl.ds(s, 1), :] = arr[s, 32:33, :]
        return carry

    lax.fori_loop(0, NDEV, tag, 0, unroll=8)
    tags = tagm[...]
    origin = jnp.sum(jnp.where(tags.astype(jnp.int32) == lane_sq, sub_sq.astype(F32), 0.0), axis=0, keepdims=True)
    back = jnp.sum(jnp.where(sub_sq == lane_sq, tags, 0.0), axis=0, keepdims=True)
    dst_v[0:1, :] = origin.astype(jnp.int32)
    dst_v[1:2, :] = jnp.maximum(back, 0.0).astype(jnp.int32)
    to_smem = pltpu.make_async_copy(dst_v, dst_s, loc_sem.at[2])
    to_smem.start()
    to_smem.wait()

    group8 = lane8 // 32

    def place_rows(chunk, carry):
        sources = [within(dst_s[0, chunk * 4 + j], NDEV) for j in range(4)]
        for ch in range(4):
            rows = quads(*[arr[s, pl.ds(ch, 8, stride=4), :] for s in sources], group8)
            for p in range(4):
                fo[ch, pl.ds(OWN + p * 8 + chunk, 8, stride=32), :] = rows[p]
        return carry

    place_rows(7, 0)
    tops(t4, [(fo, 0, -1), (fo, 1, -1), (fo, 2, -1), (fo, 3, -1)])
    start(second[:3])
    lax.fori_loop(0, 7, place_rows, 0, unroll=7)
    start(second[3:])

    inner(1)

    landed(first)
    for ch in range(7):
        dst, n = (st, ch) if ch < 5 else (sc, ch - 5)
        dst[n, 0:OWN, :] = h7[0, ch]
        dst[n, END:, :] = h7[1, ch]
    beyond(p7, 7)
    strip_own(sp, st, 5, True)
    strip_far(sp, 0, 5)
    strip_own(spc, sc, 2, True)
    strip_far(spc, 5, 2)
    statics(0, H)
    statics(END, H)
    cover, volume = whole(spc, 0), whole(spc, 1)
    keep(spc, 1, volume + 0.5)
    keep(spc, 2, strength_of(volume, cover))
    landed(second[:3])
    beyond(p4, 4)
    landed(second[3:])
    strip_own(spf, fo, 4)
    strip_far(spf, 0, 4)

    lax.fori_loop(0, HALF, outer, 0)
    merge()
    tops(t5, state_parts)
    start(third[:3])
    for ch in range(5):
        edge[0, ch] = st[ch, OWN : 2 * OWN, :]
        edge[1, ch] = st[ch, END - OWN : END, :]
    start(third[3:])
    strip_own(sp, st, 5)
    inner(0)

    landed(third[:3])
    beyond(p5, 5)
    landed(third[3:])
    for ch in range(5):
        st[ch, 0:OWN, :] = h5[0, ch]
        st[ch, END:, :] = h5[1, ch]
    strip_own(sp, st, 5, True)
    strip_far(sp, 0, 5)

    lax.fori_loop(0, HALF, outer, 0)
    merge()

    def drag(r, n):
        a = get(st, 0, r, n) - get(fo, 0, r, n)
        b = get(st, 1, r, n) - get(fo, 1, r, n)
        rate = get(sc, 0, r, n) * root(a * a + b * b)
        put(dr, 0, r - OWN, n, rate * a)
        put(dr, 1, r - OWN, n, rate * b)

    sweep(H, H + NLON, drag)

    def blocks(chunk, carry):
        for ch in range(2):
            rows = quads(*[dr[ch, pl.ds(p * 8 + chunk, 8, stride=32), :] for p in range(4)], group8)
            for j in range(4):
                sb[chunk * 4 + j, pl.ds(ch, 8, stride=2), :] = rows[j]
        return carry

    lax.fori_loop(0, 8, blocks, 0, unroll=8)

    def give(a, b):
        d = a * 4 + b
        out2[d] = sb[within(dst_s[1, d], 32)]
        pltpu.make_async_remote_copy(
            src_ref=out2.at[d], dst_ref=ret.at[me], send_sem=r_sem.at[0], recv_sem=r_sem.at[1],
            device_id=(a, b), device_id_type=MESH,
        ).start()

    for_peers(give)
    out2[me] = sb[within(dst_s[1, me], 32)]
    own_stress = pltpu.make_async_copy(out2.at[me], ret.at[me], loc_sem.at[1])
    own_stress.start()

    def lay_out(n, carry):
        lb, chunk = n // 8, n % 8
        rows, lanes = pl.ds(pl.multiple_of(lb * 8, 8), 8), pl.ds(pl.multiple_of(chunk * 128, 128), 128)
        for ch in range(5):
            ice_v[ch, rows, lanes] = st[ch, pl.ds(OWN + lb * 64 + chunk, 8, stride=8), :]
        return carry

    lax.fori_loop(0, 32, lay_out, 0)
    store = pltpu.make_async_copy(ice_v, ice_out, loc_sem.at[3])
    store.start()

    left(first)
    left(second)
    left(third)
    some.wait_send()
    some = pltpu.make_async_remote_copy(
        src_ref=out2.at[pl.ds(0, NDEV - 1)], dst_ref=ret.at[pl.ds(0, NDEV - 1)],
        send_sem=r_sem.at[0], recv_sem=r_sem.at[1], device_id=(gx, gy), device_id_type=MESH,
    )
    some.wait_recv()

    own_stress.wait()
    store.wait()
    some.wait_send()


def hand_out(tgt, ice, ret, ice_out, ocean_out, tgt_s, ret_v, ice_v, ocean_v, sem):
    loads = [
        pltpu.make_async_copy(src, dst, sem.at[i])
        for i, (src, dst) in enumerate([(tgt, tgt_s), (ret, ret_v), (ice, ice_v)])
    ]
    for load in loads:
        load.start()
    store = pltpu.make_async_copy(ice_v, ice_out, sem.at[3])
    loads[2].wait()
    store.start()
    loads[0].wait()
    loads[1].wait()

    def unpack(b, carry):
        t = tgt_s[0, b]
        v = ret_v[within(t // 32, NDEV)]
        ocean_v[b] = jnp.where(t >= 0, v, 0.0)
        return carry

    parts = []
    for n in range(4):
        lax.fori_loop(32 * n, 32 * n + 32, unpack, 0, unroll=8)
        part = pl.ds(32 * n, 32)
        parts.append(pltpu.make_async_copy(ocean_v.at[part], ocean_out.at[part], sem.at[4 + n]))
        parts[-1].start()
    store.wait()
    for part in parts:
        part.wait()


def local(ice_state, thickness, concentration, cat_mask, forcing, ice_target):
    blocks = forcing.reshape(NDEV, 4, 8, 128).transpose(0, 2, 1, 3).reshape(NDEV, 32, 128)
    hbm = pl.BlockSpec(memory_space=pl.ANY)
    vmem, dma = pltpu.VMEM, pltpu.SemaphoreType.DMA

    def v(*shape, dtype=F32):
        return vmem(shape, dtype)

    raw = (5, NLON, 1024)
    rows = W * 8
    listed = ice_target.reshape(1, NDEV)
    outs = (jax.ShapeDtypeStruct(raw, F32), jax.ShapeDtypeStruct((NDEV, 16, 128), F32))
    ice, back = pl.pallas_call(
        kernel,
        out_shape=outs,
        in_specs=[hbm] * 6,
        out_specs=(hbm, hbm),
        scratch_shapes=[
            v(1, 128, dtype=jnp.int32),
            v(8, 128, dtype=jnp.int32), pltpu.SMEM((8, 128), jnp.int32),
            v(8, 128, dtype=jnp.int32), pltpu.SMEM((8, 128), jnp.int32),
            v(*raw), v(*raw), v(*raw), v(*raw, dtype=jnp.int32),
            v(NDEV, 32, 128), v(NDEV, RB, 128), v(NDEV, RB, 128), v(NDEV, 128),
            v(6, rows, 128), v(3, rows, 128), v(4, rows, 128),
            v(5, W, 128), v(3, W, 128), v(4, W, 128),
            v(16, 128), v(3, 16, 128), v(8, 128), v(3, 8, 128), v(16, 128), v(3, 16, 128), v(7, W, 128),
            v(2, 5, OWN, 128), v(2, 5, OWN, 128), v(2, 7, OWN, 128), v(2, 7, OWN, 128),
            v(2, NLON * 8, 128), v(32, 16, 128), v(NDEV, 16, 128), v(*raw),
            dma((7,)), dma((4,)), dma((2,)), dma((2,)), dma((17,)), dma((17,)),
        ],
        compiler_params=pltpu.CompilerParams(
            collective_id=0, has_side_effects=True, vmem_limit_bytes=58 * 2**20
        ),
        name="ice",
    )(listed, ice_state[0], thickness[0], concentration[0], cat_mask[0], blocks)
    ice, ocean = pl.pallas_call(
        hand_out,
        out_shape=outs,
        in_specs=[hbm] * 3,
        out_specs=(hbm, hbm),
        scratch_shapes=[
            pltpu.SMEM((1, 128), jnp.int32), v(NDEV, 16, 128), v(*raw), v(NDEV, 16, 128), dma((8,)),
        ],
        compiler_params=pltpu.CompilerParams(vmem_limit_bytes=58 * 2**20),
        name="hand_out",
    )(listed, ice, back)
    ocean = ocean.reshape(NDEV, 8, 2, 128).transpose(0, 2, 1, 3).reshape(NDEV, 2, 1024)
    return ice[None], ocean


def solution(mesh):
    lead = ("gx", "gy")
    four, three = P(lead, None, None, None), P(lead, None, None)
    return jax.shard_map(
        local,
        mesh=mesh,
        in_specs=(four, four, four, four, three, P(lead)),
        out_specs=(four, three),
        check_vma=False,
    )
```

```python
import jax
import jax.numpy as jnp
from jax import lax
from jax.experimental import pallas as pl
from jax.experimental.pallas import tpu as pltpu
from jax.sharding import PartitionSpec as P

MESH = pl.DeviceIdType.MESH
SUB = 8
HALF = 4
H = 2 * HALF
NLON = 32
W = NLON + 2 * H
OWN = H * 8
END = OWN + NLON * 8
NDEV = 128
RB = 33
PER = W // 8
F32 = jnp.float32
BODY = 16


def spread():
    hops = (0, 1, 2, 1)
    ways = [(n * 53) % NDEV for n in range(1, NDEV)]

    def far(k):
        return 2 * (hops[k % 4] + hops[k // 8 % 4] + hops[k // 32]) + k // 4 % 2

    return sorted(ways, key=far, reverse=True)


ORDER = spread()


def at(d):
    return (d // 4, d % 4)


def rot(x, shift, axis):
    return pltpu.roll(x, shift % x.shape[axis], axis)


def iota(shape, axis):
    return lax.broadcasted_iota(jnp.int32, shape, axis)


def within(i, count):
    return jnp.minimum(jnp.maximum(i, 0), count - 1)


def root(x):
    return x * lax.rsqrt(jnp.maximum(x, 1e-30))


def stress(due_x, dun_y, due_y, dun_x, ss, sd, sh, strength):
    plus = due_x + dun_y
    minus = due_x - dun_y
    cross = due_y + dun_x
    deform = 0.5 * root(plus * plus + 0.25 * (minus * minus + cross * cross)) + 0.05
    ss = strength * (ss + 0.25 * plus - 0.5 * deform) / (strength + 0.5 * deform)
    scaled = strength / (strength + 2.0 * deform)
    sd = scaled * (sd + 0.25 * minus)
    sh = scaled * (sh + 0.125 * cross)
    return ss, sd, sh


def momentum(ue, un, dxx_x, dsh_y, dsh_x, dyy_y, uo, vo, wx, wy, cover, mass):
    force_east = 0.25 * dxx_x + 0.5 * dsh_y
    force_north = 0.5 * dsh_x + 0.25 * dyy_y
    a = uo - ue
    b = vo - un
    drag = cover * root(a * a + b * b)
    inv = 1.0 / (mass + 0.5 * drag)
    tenth = 0.1 * mass
    east = mass * ue + 0.5 * (force_east + cover * wx + drag * uo) + tenth * un
    north = mass * un + 0.5 * (force_north + cover * wy + drag * vo) - tenth * ue
    return east * inv, north * inv


def quads(x0, x1, x2, x3, group):
    low = (group % 2) == 0
    y0 = jnp.where(low, x0, rot(x1, 32, 1))
    y1 = jnp.where(low, rot(x0, -32, 1), x1)
    y2 = jnp.where(low, x2, rot(x3, 32, 1))
    y3 = jnp.where(low, rot(x2, -32, 1), x3)
    low = group < 2
    return (
        jnp.where(low, y0, rot(y2, 64, 1)),
        jnp.where(low, y1, rot(y3, 64, 1)),
        jnp.where(low, rot(y0, -64, 1), y2),
        jnp.where(low, rot(y1, -64, 1), y3),
    )


def kernel(
    tgt, state, thick, conc, mask, forc, ice_out, ret,
    tgt_v, idx_v, idx_s, dst_v, dst_s, back_v, back_s,
    r_state, r_thick, r_conc, r_mask, fv, outb, arr, tagm,
    st, sc, fo, sp, spc, spf,
    t7, p7, t4, p4, t5, p5, ext, edge, h5, edge7, h7,
    dr, sb, out2, ice_v,
    in_sem, loc_sem, a_sem, r_sem, x_send, x_recv,
):
    gx, gy = lax.axis_index("gx"), lax.axis_index("gy")
    me = gx * 4 + gy
    y, z, core, x = gx // 8, (gx // 2) % 4, gx % 2, gy

    def flipped(bit, by):
        return 1 - bit if by else bit

    xs = [2 * flipped(x // 2, n // 2) + flipped(x % 2, n % 2) for n in range(4)]
    zs = [4 * flipped(z // 2, n // 2) + 2 * flipped(z % 2, n % 2) for n in range(4)]
    ys = [16 * flipped(y // 2, n // 2) + 8 * flipped(y % 2, n % 2) for n in range(4)]
    cs = [core, 1 - core]

    def for_peers(act):
        for k in ORDER:
            act(ys[k // 32] + zs[k // 8 % 4] + cs[k // 4 % 2], xs[k % 4])

    loads = [
        pltpu.make_async_copy(src, dst, in_sem.at[i])
        for i, (src, dst) in enumerate(
            [(tgt, tgt_v), (thick, r_thick), (conc, r_conc), (mask, r_mask), (state, r_state), (forc, fv)]
        )
    ]
    for load in loads:
        load.start()

    barrier = pltpu.get_barrier_semaphore()

    def greet(a, b):
        pl.semaphore_signal(barrier, inc=1, device_id=(a, b), device_id_type=MESH)

    for_peers(greet)

    square = (NDEV, NDEV)
    lane_sq, sub_sq = iota(square, 1), iota(square, 0)
    loads[0].wait()
    row = jnp.broadcast_to(tgt_v[...].astype(F32), square)
    column = jnp.sum(jnp.where(lane_sq == sub_sq, row, 0.0), axis=1, keepdims=True)
    target = jnp.broadcast_to(column, square).astype(jnp.int32)
    hit = (target >= 0) & (target // 32 == lane_sq)
    listed = jnp.sum(jnp.where(hit, sub_sq.astype(F32), 0.0), axis=0, keepdims=True)
    place = jnp.sum(jnp.where(hit, (target % 32 + 1).astype(F32), 0.0), axis=0, keepdims=True) - 1.0
    idx_v[0:1, :] = listed.astype(jnp.int32)
    idx_v[1:2, :] = place.astype(jnp.int32)
    to_smem = pltpu.make_async_copy(idx_v, idx_s, loc_sem.at[0])
    to_smem.start()

    for load in loads[1:5]:
        load.wait()

    def relay(n, carry):
        lb, chunk = n // 8, n % 8
        rows, lanes = pl.ds(pl.multiple_of(lb * 8, 8), 8), pl.ds(pl.multiple_of(chunk * 128, 128), 128)
        dst = pl.ds(OWN + lb * 64 + chunk, 8, stride=8)
        cover = jnp.zeros((8, 128), F32)
        volume = jnp.zeros((8, 128), F32)
        for cat in range(5):
            part = r_conc[cat, rows, lanes] * r_mask[cat, rows, lanes].astype(F32)
            cover = cover + part
            volume = volume + r_thick[cat, rows, lanes] * part
        sc[0, dst, :] = cover
        sc[1, dst, :] = volume
        for ch in range(5):
            st[ch, dst, :] = r_state[ch, rows, lanes]
        return carry

    lax.fori_loop(0, 32, relay, 0)

    lane8, sub8 = iota((8, 128), 1), iota((8, 128), 0)

    def turned(v):
        for bit in (1, 2, 4):
            v = jnp.where((sub8 // bit) % 2 == 1, rot(v, bit, 0), rot(v, -bit, 0))
        for bit in (1, 2, 4):
            v = jnp.where((lane8 // bit) % 2 == 1, rot(v, bit, 1), rot(v, -bit, 1))
        return v

    def tops(dst, parts):
        full = []
        for n, (src, ch, sign) in enumerate([part for part in parts for _ in range(4)]):
            g, q = n % 4, n % 16
            v = rot(src[ch, pl.ds(OWN + (24 - 8 * g) * 8 + 7, 8, stride=8), :], 8 * q + 8, 1)
            v = v if sign > 0 else -v
            if q == 0:
                full.append(v)
            else:
                full[-1] = jnp.where(lane8 // 8 == q, v, full[-1])
        for n, v in enumerate(full):
            dst[8 * n : 8 * n + 8, :] = turned(v)

    def beyond(packed, count):
        for ch in range(count):
            for k in range(6):
                source, g = (1, 3) if k == 0 else (2, 0) if k == 5 else (0, k - 1)
                n = ch * 4 + g
                v = packed[source, 8 * (n // 16) : 8 * (n // 16) + 8, :]
                ext[ch, 8 * k : 8 * k + 8, :] = rot(v, 120 - 8 * (n % 16), 1)

    def strip_own(dst, src, count, fresh=None):
        for ch in range(count):
            for b in range(PER):
                v = rot(src[ch, pl.ds(b * 8 + 7, 8, stride=8 * PER), :], -H, 1)
                if fresh is not None:
                    lon = sub8 * PER + b
                    v = jnp.where((lon < H) | (lon >= H + NLON), v, dst[ch, b * 8 : b * 8 + 8, :])
                dst[ch, b * 8 : b * 8 + 8, :] = v

    def strip_far(dst, first, count):
        for ch in range(count):
            for b in range(PER):
                where = slice(b * 8, b * 8 + 8)
                far = ext[first + ch, pl.ds(b, 8, stride=PER), :]
                dst[ch, where, :] = jnp.where(lane8 < 128 - H, dst[ch, where, :], far)

    def merge():
        for ch in range(5):
            for b in range(PER):
                where = pl.ds(b * 8 + 7, 8, stride=8 * PER)
                new = rot(sp[ch, b * 8 : b * 8 + 8, :], H, 1)
                st[ch, where, :] = jnp.where(lane8 >= 128 - H, new, st[ch, where, :])

    state_parts = [(st, 0, -1), (st, 1, -1), (st, 2, 1), (st, 3, 1), (st, 4, 1)]
    tops(t7, state_parts + [(sc, 0, 1), (sc, 1, 1)])
    for ch in range(7):
        src, n = (st, ch) if ch < 5 else (sc, ch - 5)
        edge7[0, ch] = src[n, OWN : 2 * OWN, :]
        edge7[1, ch] = src[n, END - OWN : END, :]

    west, east = (me + NDEV - 1) % NDEV, (me + 1) % NDEV
    over, over_east, over_west = NDEV - 1 - me, (NDEV - me) % NDEV, (2 * NDEV - 2 - me) % NDEV

    def remote(src, dst, d, i):
        return pltpu.make_async_remote_copy(
            src_ref=src, dst_ref=dst, send_sem=x_send.at[i], recv_sem=x_recv.at[i],
            device_id=at(d), device_id_type=MESH,
        )

    def beside(to_west, to_east, at_west, at_east, i):
        return [
            (remote(to_west, at_east, west, i), None, None),
            (remote(to_east, at_west, east, i + 1), None, None),
        ]

    def halo(ref, count, width, i):
        def part(lon):
            return ref.at[pl.ds(0, count), pl.ds(lon * 8, width * 8)]

        return beside(part(H), part(H + NLON - width), part(H - width), part(H + NLON), i)

    def across(t, p, i):
        parts = []
        for n, d in enumerate([over, over_east, over_west]):
            here = pltpu.make_async_copy(t, p.at[n], x_recv.at[i + n]) if n else None
            parts.append((remote(t, p.at[n], d, i + n), here, d))
        return parts

    def start(copies):
        for copy, here, d in copies:
            if here is None:
                copy.start()
            else:
                pl.when(d != me)(copy.start)
                pl.when(d == me)(here.start)

    def landed(copies):
        for copy, _, _ in copies:
            copy.wait_recv()

    def left(copies):
        for copy, here, d in copies:
            if here is None:
                copy.wait_send()
            else:
                pl.when(d != me)(copy.wait_send)

    first = across(t7, p7, 4) + beside(edge7.at[0], edge7.at[1], h7.at[0], h7.at[1], 0)
    second = across(t4, p4, 9) + halo(fo, 4, H - 2, 7)
    third = across(t5, p5, 14) + beside(edge.at[0], edge.at[1], h5.at[0], h5.at[1], 12)

    to_smem.wait()
    loads[5].wait()

    def pack(c, carry):
        outb[c, 0:32, :] = fv[within(idx_s[0, c], NDEV)]
        outb[c, 32:33, :] = jnp.full((1, 128), idx_s[1, c].astype(F32))
        return carry

    lax.fori_loop(0, NDEV, pack, 0, unroll=4)

    pl.semaphore_wait(barrier, NDEV - 1)

    def send(a, b):
        pltpu.make_async_remote_copy(
            src_ref=outb.at[a * 4 + b], dst_ref=arr.at[me], send_sem=a_sem.at[0], recv_sem=a_sem.at[1],
            device_id=(a, b), device_id_type=MESH,
        ).start()

    for_peers(send)
    start(first)
    own_block = pltpu.make_async_copy(outb.at[me], arr.at[me], loc_sem.at[1])
    own_block.start()

    def get(ref, ch, r, n, shift=0):
        return ref[ch, pl.ds(pl.multiple_of(r, 8) + shift, 8 * n), :]

    def put(ref, ch, r, n, v):
        ref[ch, pl.ds(pl.multiple_of(r, 8), 8 * n), :] = v

    def diff_lon(ref, ch, r, n):
        return get(ref, ch, r + 8, n) - get(ref, ch, r - 8, n)

    def diff_lat(ref, ch, r, n):
        v = get(ref, ch, r, n)
        lane, sub = iota(v.shape, 1), iota(v.shape, 0) % 8
        up = jnp.where(lane == 0, get(ref, ch, r, n, 1), v)
        down = jnp.where(sub == 0, 0.0, get(ref, ch, r, n, -1))
        down = jnp.where(lane == 127, down, v)
        return rot(up, -1, 1) - rot(down, 1, 1)

    def strip_lon(v):
        upper = jnp.concatenate([v[1:], rot(v[:1], -1, 1)], axis=0)
        lower = jnp.concatenate([rot(v[-1:], 1, 1), v[:-1]], axis=0)
        return upper - lower

    def strip_lat(v):
        return rot(v, -1, 2) - rot(v, 1, 2)

    def whole(ref, ch):
        return ref[ch].reshape(PER, 8, 128)

    def keep(ref, ch, v):
        ref[ch] = v.reshape(PER * 8, 128)

    def sweep(lo, hi, body):
        def step(i, carry):
            body((lo + BODY * i) * 8, BODY)
            return carry

        count = (hi - lo) // BODY
        if count > 1:
            lax.fori_loop(0, count, step, 0)
        elif count:
            body(lo * 8, BODY)
        if (hi - lo) % BODY:
            body((lo + BODY * count) * 8, (hi - lo) % BODY)

    def stress_of(r, n):
        return (
            diff_lon(st, 0, r, n), diff_lat(st, 1, r, n), diff_lat(st, 0, r, n), diff_lon(st, 1, r, n),
            get(st, 2, r, n), get(st, 3, r, n), get(st, 4, r, n), get(sc, 2, r, n),
        )

    def stress_to(r, n, new):
        for ch in range(3):
            put(st, 2 + ch, r, n, new[ch])
        put(st, 5, r, n, new[0] - new[1])

    def stress_at(r, n):
        stress_to(r, n, stress(*stress_of(r, n)))

    def momentum_of(r, n):
        dxx = diff_lon(st, 2, r, n) + diff_lon(st, 3, r, n)
        return (
            get(st, 0, r, n), get(st, 1, r, n),
            dxx, diff_lat(st, 4, r, n), diff_lon(st, 4, r, n), diff_lat(st, 5, r, n),
            get(fo, 0, r, n), get(fo, 1, r, n), get(fo, 2, r, n), get(fo, 3, r, n), get(sc, 0, r, n), get(sc, 1, r, n),
        )

    def momentum_to(r, n, new):
        put(st, 0, r, n, new[0])
        put(st, 1, r, n, new[1])

    def momentum_at(r, n):
        momentum_to(r, n, momentum(*momentum_of(r, n)))

    def stress_of_strip():
        ue, un = whole(sp, 0), whole(sp, 1)
        return (
            strip_lon(ue), strip_lat(un), strip_lat(ue), strip_lon(un),
            whole(sp, 2), whole(sp, 3), whole(sp, 4), whole(spc, 2),
        )

    def momentum_of_strip():
        ss, sd, sh = whole(sp, 2), whole(sp, 3), whole(sp, 4)
        return (
            whole(sp, 0), whole(sp, 1), strip_lon(ss + sd), strip_lat(sh), strip_lon(sh), strip_lat(ss - sd),
            whole(spf, 0), whole(spf, 1), whole(spf, 2), whole(spf, 3), whole(spc, 0), whole(spc, 1),
        )

    def rims(lon, of, of_strip, step, to, channel):
        near, far = lon * 8, (W - lon - H) * 8
        parts = zip(of(near, H), of(far, H), of_strip(), strict=True)
        new = step(*[jnp.concatenate([a, b, c.reshape(PER * 8, 128)], axis=0) for a, b, c in parts])
        to(near, H, [v[0:OWN] for v in new])
        to(far, H, [v[OWN : 2 * OWN] for v in new])
        for n, v in enumerate(new):
            sp[channel + n] = v[2 * OWN :]

    def strength_of(volume, cover):
        return volume * jnp.exp(-2.0 * (1.0 - cover))

    def statics(r, n):
        cover, volume = get(sc, 0, r, n), get(sc, 1, r, n)
        put(sc, 1, r, n, volume + 0.5)
        put(sc, 2, r, n, strength_of(volume, cover))

    def inner(done):
        for m in range(HALF):
            if m or not done:
                sweep(H + 1 + 2 * m, W - H - 1 - 2 * m, stress_at)
            sweep(H + 2 + 2 * m, W - H - 2 - 2 * m, momentum_at)

    def outer(m, carry):
        rims(1 + 2 * m, stress_of, stress_of_strip, stress, stress_to, 2)
        rims(2 + 2 * m, momentum_of, momentum_of_strip, momentum, momentum_to, 0)
        return carry

    strip_own(sp, st, 5)
    strip_own(spc, sc, 2)
    sweep(H, H + NLON, statics)
    sweep(H + 1, W - H - 1, stress_at)

    own_block.wait()
    some = pltpu.make_async_remote_copy(
        src_ref=outb.at[pl.ds(0, NDEV - 1)], dst_ref=arr.at[pl.ds(0, NDEV - 1)],
        send_sem=a_sem.at[0], recv_sem=a_sem.at[1], device_id=(gx, gy), device_id_type=MESH,
    )
    some.wait_recv()

    def tag(s, carry):
        tagm[pl.ds(s, 1), :] = arr[s, 32:33, :]
        return carry

    lax.fori_loop(0, NDEV, tag, 0, unroll=32)
    tags = tagm[...]
    origin = jnp.sum(jnp.where(tags.astype(jnp.int32) == lane_sq, sub_sq.astype(F32), 0.0), axis=0, keepdims=True)
    back = jnp.sum(jnp.where(sub_sq == lane_sq, tags, 0.0), axis=0, keepdims=True)
    dst_v[0:1, :] = origin.astype(jnp.int32)
    to_smem = pltpu.make_async_copy(dst_v, dst_s, loc_sem.at[2])
    to_smem.start()
    back_v[0:1, :] = jnp.maximum(back, 0.0).astype(jnp.int32)
    to_smem.wait()
    to_smem = pltpu.make_async_copy(back_v, back_s, loc_sem.at[2])
    to_smem.start()

    group8 = lane8 // 32

    def place_rows(chunk, carry):
        sources = [within(dst_s[0, chunk * 4 + j], NDEV) for j in range(4)]
        for ch in range(4):
            rows = quads(*[arr[s, pl.ds(ch, 8, stride=4), :] for s in sources], group8)
            for p in range(4):
                fo[ch, pl.ds(OWN + p * 8 + chunk, 8, stride=32), :] = rows[p]
        return carry

    place_rows(7, 0)
    tops(t4, [(fo, 0, -1), (fo, 1, -1), (fo, 2, -1), (fo, 3, -1)])
    start(second[:3])
    lax.fori_loop(0, 7, place_rows, 0, unroll=7)
    start(second[3:])

    inner(1)

    landed(first)
    for ch in range(7):
        dst, n = (st, ch) if ch < 5 else (sc, ch - 5)
        dst[n, 0:OWN, :] = h7[0, ch]
        dst[n, END:, :] = h7[1, ch]
    beyond(p7, 7)
    strip_own(sp, st, 5, True)
    strip_far(sp, 0, 5)
    strip_own(spc, sc, 2, True)
    strip_far(spc, 5, 2)
    statics(0, H)
    statics(END, H)
    cover, volume = whole(spc, 0), whole(spc, 1)
    keep(spc, 1, volume + 0.5)
    keep(spc, 2, strength_of(volume, cover))
    landed(second[:3])
    beyond(p4, 4)
    landed(second[3:])
    strip_own(spf, fo, 4)
    strip_far(spf, 0, 4)

    lax.fori_loop(0, HALF, outer, 0, unroll=2)
    merge()
    tops(t5, state_parts)
    start(third[:3])
    for ch in range(5):
        edge[0, ch] = st[ch, OWN : 2 * OWN, :]
        edge[1, ch] = st[ch, END - OWN : END, :]
    start(third[3:])
    strip_own(sp, st, 5)
    inner(0)

    landed(third[:3])
    beyond(p5, 5)
    landed(third[3:])
    for ch in range(5):
        st[ch, 0:OWN, :] = h5[0, ch]
        st[ch, END:, :] = h5[1, ch]
    strip_own(sp, st, 5, True)
    strip_far(sp, 0, 5)

    lax.fori_loop(0, HALF, outer, 0, unroll=2)
    merge()

    def drag(r, n):
        a = get(st, 0, r, n) - get(fo, 0, r, n)
        b = get(st, 1, r, n) - get(fo, 1, r, n)
        rate = get(sc, 0, r, n) * root(a * a + b * b)
        put(dr, 0, r - OWN, n, rate * a)
        put(dr, 1, r - OWN, n, rate * b)

    sweep(H, H + NLON, drag)

    def blocks(chunk, carry):
        for ch in range(2):
            rows = quads(*[dr[ch, pl.ds(p * 8 + chunk, 8, stride=32), :] for p in range(4)], group8)
            for j in range(4):
                sb[chunk * 4 + j, pl.ds(ch, 8, stride=2), :] = rows[j]
        return carry

    lax.fori_loop(0, 8, blocks, 0, unroll=8)

    to_smem.wait()

    def give(a, b):
        d = a * 4 + b
        out2[d] = sb[within(back_s[0, d], 32)]
        pltpu.make_async_remote_copy(
            src_ref=out2.at[d], dst_ref=ret.at[me], send_sem=r_sem.at[0], recv_sem=r_sem.at[1],
            device_id=(a, b), device_id_type=MESH,
        ).start()

    for_peers(give)
    out2[me] = sb[within(back_s[0, me], 32)]
    own_stress = pltpu.make_async_copy(out2.at[me], ret.at[me], loc_sem.at[1])
    own_stress.start()

    def lay_out(n, carry):
        lb, chunk = n // 8, n % 8
        rows, lanes = pl.ds(pl.multiple_of(lb * 8, 8), 8), pl.ds(pl.multiple_of(chunk * 128, 128), 128)
        for ch in range(5):
            ice_v[ch, rows, lanes] = st[ch, pl.ds(OWN + lb * 64 + chunk, 8, stride=8), :]
        return carry

    lax.fori_loop(0, 32, lay_out, 0)
    store = pltpu.make_async_copy(ice_v, ice_out, loc_sem.at[3])
    store.start()

    left(first)
    left(second)
    left(third)
    some.wait_send()
    some = pltpu.make_async_remote_copy(
        src_ref=out2.at[pl.ds(0, NDEV - 1)], dst_ref=ret.at[pl.ds(0, NDEV - 1)],
        send_sem=r_sem.at[0], recv_sem=r_sem.at[1], device_id=(gx, gy), device_id_type=MESH,
    )
    some.wait_recv()

    own_stress.wait()
    store.wait()
    some.wait_send()


def hand_out(tgt, ice, ret, ice_out, ocean_out, tgt_s, ret_v, ice_v, ocean_v, sem):
    loads = [
        pltpu.make_async_copy(src, dst, sem.at[i])
        for i, (src, dst) in enumerate([(tgt, tgt_s), (ret, ret_v), (ice, ice_v)])
    ]
    for load in loads:
        load.start()
    store = pltpu.make_async_copy(ice_v, ice_out, sem.at[3])
    loads[2].wait()
    store.start()
    loads[0].wait()
    loads[1].wait()

    def unpack(b, carry):
        t = tgt_s[0, b]
        v = ret_v[within(t // 32, NDEV)]
        ocean_v[b] = jnp.where(t >= 0, v, 0.0)
        return carry

    parts = []
    for n in range(4):
        lax.fori_loop(32 * n, 32 * n + 32, unpack, 0, unroll=8)
        part = pl.ds(32 * n, 32)
        parts.append(pltpu.make_async_copy(ocean_v.at[part], ocean_out.at[part], sem.at[4 + n]))
        parts[-1].start()
    store.wait()
    for part in parts:
        part.wait()


def local(ice_state, thickness, concentration, cat_mask, forcing, ice_target):
    blocks = forcing.reshape(NDEV, 4, 8, 128).transpose(0, 2, 1, 3).reshape(NDEV, 32, 128)
    hbm = pl.BlockSpec(memory_space=pl.ANY)
    vmem, dma = pltpu.VMEM, pltpu.SemaphoreType.DMA

    def v(*shape, dtype=F32):
        return vmem(shape, dtype)

    raw = (5, NLON, 1024)
    rows = W * 8
    listed = ice_target.reshape(1, NDEV)
    outs = (jax.ShapeDtypeStruct(raw, F32), jax.ShapeDtypeStruct((NDEV, 16, 128), F32))
    ice, back = pl.pallas_call(
        kernel,
        out_shape=outs,
        in_specs=[hbm] * 6,
        out_specs=(hbm, hbm),
        scratch_shapes=[
            v(1, 128, dtype=jnp.int32),
            v(8, 128, dtype=jnp.int32), pltpu.SMEM((8, 128), jnp.int32),
            v(8, 128, dtype=jnp.int32), pltpu.SMEM((8, 128), jnp.int32),
            v(8, 128, dtype=jnp.int32), pltpu.SMEM((8, 128), jnp.int32),
            v(*raw), v(*raw), v(*raw), v(*raw, dtype=jnp.int32),
            v(NDEV, 32, 128), v(NDEV, RB, 128), v(NDEV, RB, 128), v(NDEV, 128),
            v(6, rows, 128), v(3, rows, 128), v(4, rows, 128),
            v(5, W, 128), v(3, W, 128), v(4, W, 128),
            v(16, 128), v(3, 16, 128), v(8, 128), v(3, 8, 128), v(16, 128), v(3, 16, 128), v(7, W, 128),
            v(2, 5, OWN, 128), v(2, 5, OWN, 128), v(2, 7, OWN, 128), v(2, 7, OWN, 128),
            v(2, NLON * 8, 128), v(32, 16, 128), v(NDEV, 16, 128), v(*raw),
            dma((7,)), dma((4,)), dma((2,)), dma((2,)), dma((17,)), dma((17,)),
        ],
        compiler_params=pltpu.CompilerParams(
            collective_id=0, has_side_effects=True, vmem_limit_bytes=58 * 2**20
        ),
        name="ice",
    )(listed, ice_state[0], thickness[0], concentration[0], cat_mask[0], blocks)
    ice, ocean = pl.pallas_call(
        hand_out,
        out_shape=outs,
        in_specs=[hbm] * 3,
        out_specs=(hbm, hbm),
        scratch_shapes=[
            pltpu.SMEM((1, 128), jnp.int32), v(NDEV, 16, 128), v(*raw), v(NDEV, 16, 128), dma((8,)),
        ],
        compiler_params=pltpu.CompilerParams(vmem_limit_bytes=58 * 2**20),
        name="hand_out",
    )(listed, ice, back)
    ocean = ocean.reshape(NDEV, 8, 2, 128).transpose(0, 2, 1, 3).reshape(NDEV, 2, 1024)
    return ice[None], ocean


def solution(mesh):
    lead = ("gx", "gy")
    four, three = P(lead, None, None, None), P(lead, None, None)
    return jax.shard_map(
        local,
        mesh=mesh,
        in_specs=(four, four, four, four, three, P(lead)),
        out_specs=(four, three),
        check_vma=False,
    )
```

```python
import jax
import jax.numpy as jnp
from jax import lax
from jax.experimental import pallas as pl
from jax.experimental.pallas import tpu as pltpu
from jax.sharding import PartitionSpec as P

MESH = pl.DeviceIdType.MESH
SUB = 8
HALF = 4
H = 2 * HALF
NLON = 32
W = NLON + 2 * H
OWN = H * 8
END = OWN + NLON * 8
NDEV = 128
RB = 33
PER = W // 8
F32 = jnp.float32
BODY = 16


def spread():
    hops = (0, 1, 2, 1)
    ways = [(n * 53) % NDEV for n in range(1, NDEV)]

    def far(k):
        along = hops[k % 4], hops[k // 8 % 4], hops[k // 32]
        return 8 * sum(along) + 4 * (k // 4 % 2) + max(along)

    return sorted(ways, key=far, reverse=True)


ORDER = spread()


def at(d):
    return (d // 4, d % 4)


def rot(x, shift, axis):
    return pltpu.roll(x, shift % x.shape[axis], axis)


def iota(shape, axis):
    return lax.broadcasted_iota(jnp.int32, shape, axis)


def within(i, count):
    return jnp.minimum(jnp.maximum(i, 0), count - 1)


def root(x):
    return x * lax.rsqrt(jnp.maximum(x, 1e-30))


def stress(due_x, dun_y, due_y, dun_x, ss, sd, sh, strength):
    plus = due_x + dun_y
    minus = due_x - dun_y
    cross = due_y + dun_x
    deform = 0.5 * root(plus * plus + 0.25 * (minus * minus + cross * cross)) + 0.05
    ss = strength * (ss + 0.25 * plus - 0.5 * deform) / (strength + 0.5 * deform)
    scaled = strength / (strength + 2.0 * deform)
    sd = scaled * (sd + 0.25 * minus)
    sh = scaled * (sh + 0.125 * cross)
    return ss, sd, sh


def momentum(ue, un, dxx_x, dsh_y, dsh_x, dyy_y, uo, vo, wx, wy, cover, mass):
    force_east = 0.25 * dxx_x + 0.5 * dsh_y
    force_north = 0.5 * dsh_x + 0.25 * dyy_y
    a = uo - ue
    b = vo - un
    drag = cover * root(a * a + b * b)
    inv = 1.0 / (mass + 0.5 * drag)
    tenth = 0.1 * mass
    east = mass * ue + 0.5 * (force_east + cover * wx + drag * uo) + tenth * un
    north = mass * un + 0.5 * (force_north + cover * wy + drag * vo) - tenth * ue
    return east * inv, north * inv


def quads(x0, x1, x2, x3, group):
    low = (group % 2) == 0
    y0 = jnp.where(low, x0, rot(x1, 32, 1))
    y1 = jnp.where(low, rot(x0, -32, 1), x1)
    y2 = jnp.where(low, x2, rot(x3, 32, 1))
    y3 = jnp.where(low, rot(x2, -32, 1), x3)
    low = group < 2
    return (
        jnp.where(low, y0, rot(y2, 64, 1)),
        jnp.where(low, y1, rot(y3, 64, 1)),
        jnp.where(low, rot(y0, -64, 1), y2),
        jnp.where(low, rot(y1, -64, 1), y3),
    )


def kernel(
    tgt, state, thick, conc, mask, forc, ice_out, ret,
    tgt_v, idx_v, idx_s, dst_v, dst_s,
    r_state, r_thick, r_conc, r_mask, fv, outb, arr, tagm,
    st, sc, fo, sp, spc, spf,
    t7, p7, t4, p4, t5, p5, ext, edge, h5, edge7, h7,
    dr, sb, out2, ice_v,
    in_sem, loc_sem, a_sem, r_sem, x_send, x_recv,
):
    gx, gy = lax.axis_index("gx"), lax.axis_index("gy")
    me = gx * 4 + gy
    y, z, core, x = gx // 8, (gx // 2) % 4, gx % 2, gy

    def flipped(bit, by):
        return 1 - bit if by else bit

    xs = [2 * flipped(x // 2, n // 2) + flipped(x % 2, n % 2) for n in range(4)]
    zs = [4 * flipped(z // 2, n // 2) + 2 * flipped(z % 2, n % 2) for n in range(4)]
    ys = [16 * flipped(y // 2, n // 2) + 8 * flipped(y % 2, n % 2) for n in range(4)]
    cs = [core, 1 - core]

    def for_peers(act):
        for k in ORDER:
            act(ys[k // 32] + zs[k // 8 % 4] + cs[k // 4 % 2], xs[k % 4])

    loads = [
        pltpu.make_async_copy(src, dst, in_sem.at[i])
        for i, (src, dst) in enumerate(
            [(tgt, tgt_v), (thick, r_thick), (conc, r_conc), (mask, r_mask), (state, r_state), (forc, fv)]
        )
    ]
    for load in loads:
        load.start()

    barrier = pltpu.get_barrier_semaphore()

    def greet(a, b):
        pl.semaphore_signal(barrier, inc=1, device_id=(a, b), device_id_type=MESH)

    for_peers(greet)

    square = (NDEV, NDEV)
    lane_sq, sub_sq = iota(square, 1), iota(square, 0)
    loads[0].wait()
    row = jnp.broadcast_to(tgt_v[...].astype(F32), square)
    column = jnp.sum(jnp.where(lane_sq == sub_sq, row, 0.0), axis=1, keepdims=True)
    target = jnp.broadcast_to(column, square).astype(jnp.int32)
    hit = (target >= 0) & (target // 32 == lane_sq)
    listed = jnp.sum(jnp.where(hit, sub_sq.astype(F32), 0.0), axis=0, keepdims=True)
    place = jnp.sum(jnp.where(hit, (target % 32 + 1).astype(F32), 0.0), axis=0, keepdims=True) - 1.0
    idx_v[0:1, :] = listed.astype(jnp.int32)
    idx_v[1:2, :] = place.astype(jnp.int32)
    to_smem = pltpu.make_async_copy(idx_v, idx_s, loc_sem.at[0])
    to_smem.start()

    for load in loads[1:5]:
        load.wait()

    def relay(n, carry):
        lb, chunk = n // 8, n % 8
        rows, lanes = pl.ds(pl.multiple_of(lb * 8, 8), 8), pl.ds(pl.multiple_of(chunk * 128, 128), 128)
        dst = pl.ds(OWN + lb * 64 + chunk, 8, stride=8)
        cover = jnp.zeros((8, 128), F32)
        volume = jnp.zeros((8, 128), F32)
        for cat in range(5):
            part = r_conc[cat, rows, lanes] * r_mask[cat, rows, lanes].astype(F32)
            cover = cover + part
            volume = volume + r_thick[cat, rows, lanes] * part
        sc[0, dst, :] = cover
        sc[1, dst, :] = volume
        for ch in range(5):
            st[ch, dst, :] = r_state[ch, rows, lanes]
        return carry

    lax.fori_loop(0, 32, relay, 0)

    lane8, sub8 = iota((8, 128), 1), iota((8, 128), 0)

    def turned(v):
        for bit in (1, 2, 4):
            v = jnp.where((sub8 // bit) % 2 == 1, rot(v, bit, 0), rot(v, -bit, 0))
        for bit in (1, 2, 4):
            v = jnp.where((lane8 // bit) % 2 == 1, rot(v, bit, 1), rot(v, -bit, 1))
        return v

    def tops(dst, parts):
        full = []
        for n, (src, ch, sign) in enumerate([part for part in parts for _ in range(4)]):
            g, q = n % 4, n % 16
            v = rot(src[ch, pl.ds(OWN + (24 - 8 * g) * 8 + 7, 8, stride=8), :], 8 * q + 8, 1)
            v = v if sign > 0 else -v
            if q == 0:
                full.append(v)
            else:
                full[-1] = jnp.where(lane8 // 8 == q, v, full[-1])
        for n, v in enumerate(full):
            dst[8 * n : 8 * n + 8, :] = turned(v)

    def beyond(packed, count):
        for ch in range(count):
            for k in range(6):
                source, g = (1, 3) if k == 0 else (2, 0) if k == 5 else (0, k - 1)
                n = ch * 4 + g
                v = packed[source, 8 * (n // 16) : 8 * (n // 16) + 8, :]
                ext[ch, 8 * k : 8 * k + 8, :] = rot(v, 120 - 8 * (n % 16), 1)

    def strip_own(dst, src, count, fresh=None):
        for ch in range(count):
            for b in range(PER):
                v = rot(src[ch, pl.ds(b * 8 + 7, 8, stride=8 * PER), :], -H, 1)
                if fresh is not None:
                    lon = sub8 * PER + b
                    v = jnp.where((lon < H) | (lon >= H + NLON), v, dst[ch, b * 8 : b * 8 + 8, :])
                dst[ch, b * 8 : b * 8 + 8, :] = v

    def strip_far(dst, first, count):
        for ch in range(count):
            for b in range(PER):
                where = slice(b * 8, b * 8 + 8)
                far = ext[first + ch, pl.ds(b, 8, stride=PER), :]
                dst[ch, where, :] = jnp.where(lane8 < 128 - H, dst[ch, where, :], far)

    def merge():
        for ch in range(5):
            for b in range(PER):
                where = pl.ds(b * 8 + 7, 8, stride=8 * PER)
                new = rot(sp[ch, b * 8 : b * 8 + 8, :], H, 1)
                st[ch, where, :] = jnp.where(lane8 >= 128 - H, new, st[ch, where, :])

    state_parts = [(st, 0, -1), (st, 1, -1), (st, 2, 1), (st, 3, 1), (st, 4, 1)]
    tops(t7, state_parts + [(sc, 0, 1), (sc, 1, 1)])
    for ch in range(7):
        src, n = (st, ch) if ch < 5 else (sc, ch - 5)
        edge7[0, ch] = src[n, OWN : 2 * OWN, :]
        edge7[1, ch] = src[n, END - OWN : END, :]

    west, east = (me + NDEV - 1) % NDEV, (me + 1) % NDEV
    over, over_east, over_west = NDEV - 1 - me, (NDEV - me) % NDEV, (2 * NDEV - 2 - me) % NDEV

    def remote(src, dst, d, i):
        return pltpu.make_async_remote_copy(
            src_ref=src, dst_ref=dst, send_sem=x_send.at[i], recv_sem=x_recv.at[i],
            device_id=at(d), device_id_type=MESH,
        )

    def beside(to_west, to_east, at_west, at_east, i):
        return [
            (remote(to_west, at_east, west, i), None, None),
            (remote(to_east, at_west, east, i + 1), None, None),
        ]

    def halo(ref, count, width, i):
        def part(lon):
            return ref.at[pl.ds(0, count), pl.ds(lon * 8, width * 8)]

        return beside(part(H), part(H + NLON - width), part(H - width), part(H + NLON), i)

    def across(t, p, i):
        parts = []
        for n, d in enumerate([over, over_east, over_west]):
            here = pltpu.make_async_copy(t, p.at[n], x_recv.at[i + n]) if n else None
            parts.append((remote(t, p.at[n], d, i + n), here, d))
        return parts

    def start(copies):
        for copy, here, d in copies:
            if here is None:
                copy.start()
            else:
                pl.when(d != me)(copy.start)
                pl.when(d == me)(here.start)

    def landed(copies):
        for copy, _, _ in copies:
            copy.wait_recv()

    def left(copies):
        for copy, here, d in copies:
            if here is None:
                copy.wait_send()
            else:
                pl.when(d != me)(copy.wait_send)

    first = across(t7, p7, 4) + beside(edge7.at[0], edge7.at[1], h7.at[0], h7.at[1], 0)
    second = across(t4, p4, 9) + halo(fo, 4, H - 2, 7)
    third = across(t5, p5, 14) + beside(edge.at[0], edge.at[1], h5.at[0], h5.at[1], 12)

    to_smem.wait()
    loads[5].wait()

    def pack(c, carry):
        outb[c, 0:32, :] = fv[within(idx_s[0, c], NDEV)]
        outb[c, 32:33, :] = jnp.full((1, 128), idx_s[1, c].astype(F32))
        return carry

    lax.fori_loop(0, NDEV, pack, 0, unroll=4)

    pl.semaphore_wait(barrier, NDEV - 1)

    def send(a, b):
        pltpu.make_async_remote_copy(
            src_ref=outb.at[a * 4 + b], dst_ref=arr.at[me], send_sem=a_sem.at[0], recv_sem=a_sem.at[1],
            device_id=(a, b), device_id_type=MESH,
        ).start()

    for_peers(send)
    start(first)
    own_block = pltpu.make_async_copy(outb.at[me], arr.at[me], loc_sem.at[1])
    own_block.start()

    def get(ref, ch, r, n, shift=0):
        return ref[ch, pl.ds(pl.multiple_of(r, 8) + shift, 8 * n), :]

    def put(ref, ch, r, n, v):
        ref[ch, pl.ds(pl.multiple_of(r, 8), 8 * n), :] = v

    def diff_lon(ref, ch, r, n):
        return get(ref, ch, r + 8, n) - get(ref, ch, r - 8, n)

    def diff_lat(ref, ch, r, n):
        v = get(ref, ch, r, n)
        lane, sub = iota(v.shape, 1), iota(v.shape, 0) % 8
        up = jnp.where(lane == 0, get(ref, ch, r, n, 1), v)
        down = jnp.where(sub == 0, 0.0, get(ref, ch, r, n, -1))
        down = jnp.where(lane == 127, down, v)
        return rot(up, -1, 1) - rot(down, 1, 1)

    def strip_lon(v):
        upper = jnp.concatenate([v[1:], rot(v[:1], -1, 1)], axis=0)
        lower = jnp.concatenate([rot(v[-1:], 1, 1), v[:-1]], axis=0)
        return upper - lower

    def strip_lat(v):
        return rot(v, -1, 2) - rot(v, 1, 2)

    def whole(ref, ch):
        return ref[ch].reshape(PER, 8, 128)

    def keep(ref, ch, v):
        ref[ch] = v.reshape(PER * 8, 128)

    def sweep(lo, hi, body):
        def step(i, carry):
            body((lo + BODY * i) * 8, BODY)
            return carry

        count = (hi - lo) // BODY
        if count > 1:
            lax.fori_loop(0, count, step, 0)
        elif count:
            body(lo * 8, BODY)
        if (hi - lo) % BODY:
            body((lo + BODY * count) * 8, (hi - lo) % BODY)

    def stress_of(r, n):
        return (
            diff_lon(st, 0, r, n), diff_lat(st, 1, r, n), diff_lat(st, 0, r, n), diff_lon(st, 1, r, n),
            get(st, 2, r, n), get(st, 3, r, n), get(st, 4, r, n), get(sc, 2, r, n),
        )

    def stress_to(r, n, new):
        for ch in range(3):
            put(st, 2 + ch, r, n, new[ch])
        put(st, 5, r, n, new[0] - new[1])

    def stress_at(r, n):
        stress_to(r, n, stress(*stress_of(r, n)))

    def momentum_of(r, n):
        dxx = diff_lon(st, 2, r, n) + diff_lon(st, 3, r, n)
        return (
            get(st, 0, r, n), get(st, 1, r, n),
            dxx, diff_lat(st, 4, r, n), diff_lon(st, 4, r, n), diff_lat(st, 5, r, n),
            get(fo, 0, r, n), get(fo, 1, r, n), get(fo, 2, r, n), get(fo, 3, r, n), get(sc, 0, r, n), get(sc, 1, r, n),
        )

    def momentum_to(r, n, new):
        put(st, 0, r, n, new[0])
        put(st, 1, r, n, new[1])

    def momentum_at(r, n):
        momentum_to(r, n, momentum(*momentum_of(r, n)))

    def stress_of_strip():
        ue, un = whole(sp, 0), whole(sp, 1)
        return (
            strip_lon(ue), strip_lat(un), strip_lat(ue), strip_lon(un),
            whole(sp, 2), whole(sp, 3), whole(sp, 4), whole(spc, 2),
        )

    def momentum_of_strip():
        ss, sd, sh = whole(sp, 2), whole(sp, 3), whole(sp, 4)
        return (
            whole(sp, 0), whole(sp, 1), strip_lon(ss + sd), strip_lat(sh), strip_lon(sh), strip_lat(ss - sd),
            whole(spf, 0), whole(spf, 1), whole(spf, 2), whole(spf, 3), whole(spc, 0), whole(spc, 1),
        )

    def rims(lon, of, of_strip, step, to, channel):
        near, far = lon * 8, (W - lon - H) * 8
        parts = zip(of(near, H), of(far, H), of_strip(), strict=True)
        new = step(*[jnp.concatenate([a, b, c.reshape(PER * 8, 128)], axis=0) for a, b, c in parts])
        to(near, H, [v[0:OWN] for v in new])
        to(far, H, [v[OWN : 2 * OWN] for v in new])
        for n, v in enumerate(new):
            sp[channel + n] = v[2 * OWN :]

    def strength_of(volume, cover):
        return volume * jnp.exp(-2.0 * (1.0 - cover))

    def statics(r, n):
        cover, volume = get(sc, 0, r, n), get(sc, 1, r, n)
        put(sc, 1, r, n, volume + 0.5)
        put(sc, 2, r, n, strength_of(volume, cover))

    def inner(done):
        for m in range(HALF):
            if m or not done:
                sweep(H + 1 + 2 * m, W - H - 1 - 2 * m, stress_at)
            sweep(H + 2 + 2 * m, W - H - 2 - 2 * m, momentum_at)

    def outer(m, carry):
        rims(1 + 2 * m, stress_of, stress_of_strip, stress, stress_to, 2)
        rims(2 + 2 * m, momentum_of, momentum_of_strip, momentum, momentum_to, 0)
        return carry

    strip_own(sp, st, 5)
    strip_own(spc, sc, 2)
    sweep(H, H + NLON, statics)
    sweep(H + 1, W - H - 1, stress_at)

    own_block.wait()
    some = pltpu.make_async_remote_copy(
        src_ref=outb.at[pl.ds(0, NDEV - 1)], dst_ref=arr.at[pl.ds(0, NDEV - 1)],
        send_sem=a_sem.at[0], recv_sem=a_sem.at[1], device_id=(gx, gy), device_id_type=MESH,
    )
    some.wait_recv()

    def tag(s, carry):
        tagm[pl.ds(s, 1), :] = arr[s, 32:33, :]
        return carry

    lax.fori_loop(0, NDEV, tag, 0, unroll=8)
    tags = tagm[...]
    origin = jnp.sum(jnp.where(tags.astype(jnp.int32) == lane_sq, sub_sq.astype(F32), 0.0), axis=0, keepdims=True)
    back = jnp.sum(jnp.where(sub_sq == lane_sq, tags, 0.0), axis=0, keepdims=True)
    dst_v[0:1, :] = origin.astype(jnp.int32)
    dst_v[1:2, :] = jnp.maximum(back, 0.0).astype(jnp.int32)
    to_smem = pltpu.make_async_copy(dst_v, dst_s, loc_sem.at[2])
    to_smem.start()
    to_smem.wait()

    group8 = lane8 // 32

    def place_rows(chunk, carry):
        sources = [within(dst_s[0, chunk * 4 + j], NDEV) for j in range(4)]
        for ch in range(4):
            rows = quads(*[arr[s, pl.ds(ch, 8, stride=4), :] for s in sources], group8)
            for p in range(4):
                fo[ch, pl.ds(OWN + p * 8 + chunk, 8, stride=32), :] = rows[p]
        return carry

    place_rows(7, 0)
    tops(t4, [(fo, 0, -1), (fo, 1, -1), (fo, 2, -1), (fo, 3, -1)])
    start(second[:3])
    lax.fori_loop(0, 7, place_rows, 0, unroll=7)
    start(second[3:])

    inner(1)

    landed(first)
    for ch in range(7):
        dst, n = (st, ch) if ch < 5 else (sc, ch - 5)
        dst[n, 0:OWN, :] = h7[0, ch]
        dst[n, END:, :] = h7[1, ch]
    beyond(p7, 7)
    strip_own(sp, st, 5, True)
    strip_far(sp, 0, 5)
    strip_own(spc, sc, 2, True)
    strip_far(spc, 5, 2)
    statics(0, H)
    statics(END, H)
    cover, volume = whole(spc, 0), whole(spc, 1)
    keep(spc, 1, volume + 0.5)
    keep(spc, 2, strength_of(volume, cover))
    landed(second[:3])
    beyond(p4, 4)
    landed(second[3:])
    strip_own(spf, fo, 4)
    strip_far(spf, 0, 4)

    lax.fori_loop(0, HALF, outer, 0)
    merge()
    tops(t5, state_parts)
    start(third[:3])
    for ch in range(5):
        edge[0, ch] = st[ch, OWN : 2 * OWN, :]
        edge[1, ch] = st[ch, END - OWN : END, :]
    start(third[3:])
    strip_own(sp, st, 5)
    inner(0)

    landed(third[:3])
    beyond(p5, 5)
    landed(third[3:])
    for ch in range(5):
        st[ch, 0:OWN, :] = h5[0, ch]
        st[ch, END:, :] = h5[1, ch]
    strip_own(sp, st, 5, True)
    strip_far(sp, 0, 5)

    lax.fori_loop(0, HALF, outer, 0)
    merge()

    def drag(r, n):
        a = get(st, 0, r, n) - get(fo, 0, r, n)
        b = get(st, 1, r, n) - get(fo, 1, r, n)
        rate = get(sc, 0, r, n) * root(a * a + b * b)
        put(dr, 0, r - OWN, n, rate * a)
        put(dr, 1, r - OWN, n, rate * b)

    sweep(H, H + NLON, drag)

    def blocks(chunk, carry):
        for ch in range(2):
            rows = quads(*[dr[ch, pl.ds(p * 8 + chunk, 8, stride=32), :] for p in range(4)], group8)
            for j in range(4):
                sb[chunk * 4 + j, pl.ds(ch, 8, stride=2), :] = rows[j]
        return carry

    lax.fori_loop(0, 8, blocks, 0, unroll=8)

    def give(a, b):
        d = a * 4 + b
        out2[d] = sb[within(dst_s[1, d], 32)]
        pltpu.make_async_remote_copy(
            src_ref=out2.at[d], dst_ref=ret.at[me], send_sem=r_sem.at[0], recv_sem=r_sem.at[1],
            device_id=(a, b), device_id_type=MESH,
        ).start()

    for_peers(give)
    out2[me] = sb[within(dst_s[1, me], 32)]
    own_stress = pltpu.make_async_copy(out2.at[me], ret.at[me], loc_sem.at[1])
    own_stress.start()

    def lay_out(n, carry):
        lb, chunk = n // 8, n % 8
        rows, lanes = pl.ds(pl.multiple_of(lb * 8, 8), 8), pl.ds(pl.multiple_of(chunk * 128, 128), 128)
        for ch in range(5):
            ice_v[ch, rows, lanes] = st[ch, pl.ds(OWN + lb * 64 + chunk, 8, stride=8), :]
        return carry

    lax.fori_loop(0, 32, lay_out, 0)
    store = pltpu.make_async_copy(ice_v, ice_out, loc_sem.at[3])
    store.start()

    left(first)
    left(second)
    left(third)
    some.wait_send()
    some = pltpu.make_async_remote_copy(
        src_ref=out2.at[pl.ds(0, NDEV - 1)], dst_ref=ret.at[pl.ds(0, NDEV - 1)],
        send_sem=r_sem.at[0], recv_sem=r_sem.at[1], device_id=(gx, gy), device_id_type=MESH,
    )
    some.wait_recv()

    own_stress.wait()
    store.wait()
    some.wait_send()


def hand_out(tgt, ice, ret, ice_out, ocean_out, tgt_s, ret_v, ice_v, ocean_v, sem):
    loads = [
        pltpu.make_async_copy(src, dst, sem.at[i])
        for i, (src, dst) in enumerate([(tgt, tgt_s), (ret, ret_v), (ice, ice_v)])
    ]
    for load in loads:
        load.start()
    store = pltpu.make_async_copy(ice_v, ice_out, sem.at[3])
    loads[2].wait()
    store.start()
    loads[0].wait()
    loads[1].wait()

    def unpack(b, carry):
        t = tgt_s[0, b]
        v = ret_v[within(t // 32, NDEV)]
        ocean_v[b] = jnp.where(t >= 0, v, 0.0)
        return carry

    parts = []
    for n in range(4):
        lax.fori_loop(32 * n, 32 * n + 32, unpack, 0, unroll=8)
        part = pl.ds(32 * n, 32)
        parts.append(pltpu.make_async_copy(ocean_v.at[part], ocean_out.at[part], sem.at[4 + n]))
        parts[-1].start()
    store.wait()
    for part in parts:
        part.wait()


def local(ice_state, thickness, concentration, cat_mask, forcing, ice_target):
    blocks = forcing.reshape(NDEV, 4, 8, 128).transpose(0, 2, 1, 3).reshape(NDEV, 32, 128)
    hbm = pl.BlockSpec(memory_space=pl.ANY)
    vmem, dma = pltpu.VMEM, pltpu.SemaphoreType.DMA

    def v(*shape, dtype=F32):
        return vmem(shape, dtype)

    raw = (5, NLON, 1024)
    rows = W * 8
    listed = ice_target.reshape(1, NDEV)
    outs = (jax.ShapeDtypeStruct(raw, F32), jax.ShapeDtypeStruct((NDEV, 16, 128), F32))
    ice, back = pl.pallas_call(
        kernel,
        out_shape=outs,
        in_specs=[hbm] * 6,
        out_specs=(hbm, hbm),
        scratch_shapes=[
            v(1, 128, dtype=jnp.int32),
            v(8, 128, dtype=jnp.int32), pltpu.SMEM((8, 128), jnp.int32),
            v(8, 128, dtype=jnp.int32), pltpu.SMEM((8, 128), jnp.int32),
            v(*raw), v(*raw), v(*raw), v(*raw, dtype=jnp.int32),
            v(NDEV, 32, 128), v(NDEV, RB, 128), v(NDEV, RB, 128), v(NDEV, 128),
            v(6, rows, 128), v(3, rows, 128), v(4, rows, 128),
            v(5, W, 128), v(3, W, 128), v(4, W, 128),
            v(16, 128), v(3, 16, 128), v(8, 128), v(3, 8, 128), v(16, 128), v(3, 16, 128), v(7, W, 128),
            v(2, 5, OWN, 128), v(2, 5, OWN, 128), v(2, 7, OWN, 128), v(2, 7, OWN, 128),
            v(2, NLON * 8, 128), v(32, 16, 128), v(NDEV, 16, 128), v(*raw),
            dma((7,)), dma((4,)), dma((2,)), dma((2,)), dma((17,)), dma((17,)),
        ],
        compiler_params=pltpu.CompilerParams(
            collective_id=0, has_side_effects=True, vmem_limit_bytes=58 * 2**20
        ),
        name="ice",
    )(listed, ice_state[0], thickness[0], concentration[0], cat_mask[0], blocks)
    ice, ocean = pl.pallas_call(
        hand_out,
        out_shape=outs,
        in_specs=[hbm] * 3,
        out_specs=(hbm, hbm),
        scratch_shapes=[
            pltpu.SMEM((1, 128), jnp.int32), v(NDEV, 16, 128), v(*raw), v(NDEV, 16, 128), dma((8,)),
        ],
        compiler_params=pltpu.CompilerParams(vmem_limit_bytes=58 * 2**20),
        name="hand_out",
    )(listed, ice, back)
    ocean = ocean.reshape(NDEV, 8, 2, 128).transpose(0, 2, 1, 3).reshape(NDEV, 2, 1024)
    return ice[None], ocean


def solution(mesh):
    lead = ("gx", "gy")
    four, three = P(lead, None, None, None), P(lead, None, None)
    return jax.shard_map(
        local,
        mesh=mesh,
        in_specs=(four, four, four, four, three, P(lead)),
        out_specs=(four, three),
        check_vma=False,
    )
```
